32 devices in a mesh: gx: 4 (over y, core), yz: 8 (over z, x).
Axes of the slice: x: 2, y: 2, z: 4, core: 2. Of those that a mesh axis runs over, the one named last changes fastest.
Arguments:
- forcing: float32 [4, 8, 128, 512], P('gx', 'yz'), may hold values from -60 to 60
- viscosity: float32 [4, 8, 128, 512], P('gx', 'yz'), may hold values from 0.02 to 0.5
- mass_rate: float32 [4, 8, 128, 512], P('gx', 'yz'), may hold values from 10 to 80
- slot_element: int32 [4, 8, 128], P('gx', 'yz'), may hold values from 0 to 127, as said below
Outputs:
- solution: float32 [4, 8, 128, 512], P('gx', 'yz')
- residual: float32 [4, 8, 128, 512], P('gx', 'yz')
The draws below stay inside these ranges and needn't reach their ends.
Inputs may be any that keep to these rules, and one draw needn't show every extreme that they name: `slot_element`: in each device block the 128 entries are every number 0 to 127 once.
All inputs are finite; a program needn't handle non-finite values.
Results may differ from the reference program's by a relative error of at most 0.0045.
Values sent between devices are 32-bit elements; how exact they have to be, the bound alone decides.
No kernel may reach another device: no remote copies, remote signals or barrier semaphores. Data moves between devices by JAX's collectives and lax.ppermute only.
A program may use at most 64 MiB of HBM per device.

```python
import math
import jax
import jax.numpy as jnp
import numpy as np
from jax import lax

EX = 2
EY = 1
EZ = 64
POINTS = 512
ITERS = 3
EL_DEV = 128
SLABS = 4
COLUMNS = 8
NEX = 8
NEY = 8


def draw_slot_element(key, part):
    key = jax.random.fold_in(key, 5)
    subkeys = jax.random.split(key, SLABS * COLUMNS)
    orders = jax.vmap(lambda single: jax.random.permutation(single, EL_DEV))(subkeys)
    return orders.reshape(SLABS, COLUMNS, EL_DEV).astype(jnp.int32)


def draw_forcing(key, part):
    key = jax.random.fold_in(key, 11)
    dimensions = (SLABS, COLUMNS, EL_DEV, POINTS)
    values = jnp.clip(jax.random.normal(jax.random.fold_in(key, 1), dimensions, jnp.float32), -4.0, 4.0) * 0.3
    rising = 0.5
    scales = jnp.exp(jax.random.uniform(jax.random.fold_in(key, 2), (SLABS, COLUMNS, EL_DEV, 1), jnp.float32, 0.0, math.log(10.0)))
    slab_pos = jnp.arange(SLABS, dtype=jnp.float32) / max(SLABS - 1, 1)
    column_pos = jnp.arange(COLUMNS, dtype=jnp.float32) / max(COLUMNS - 1, 1)
    growth = jnp.exp(math.log(3.0) * rising * (slab_pos[:, None, None, None] + column_pos[None, :, None, None]))
    return (values * scales * growth).astype(jnp.float32)


def block_levels(stream_key, shape, pieces, low, high):
    factor_of = 1.0
    for axis_at, shards_of in pieces:
        draws = jax.random.uniform(jax.random.fold_in(jax.random.fold_in(stream_key, 6), axis_at), (shards_of,), jnp.float32, low / len(pieces), high / len(pieces))
        factor_of = factor_of * jnp.repeat(jnp.exp(draws), shape[axis_at] // shards_of).reshape((-1,) + (1,) * (len(shape) - 1 - axis_at))
    return factor_of


def setup_inputs(seed: int = 0) -> dict:
    key_list = jax.random.split(jax.random.key(seed), 5)
    return {
        "forcing": draw_forcing(jax.random.fold_in(key_list[4], 71), 0),
        "viscosity": jnp.clip(jnp.exp(math.log(0.5) - 3.218876 * jax.random.uniform(key_list[1], (SLABS, COLUMNS, EL_DEV, POINTS), jnp.float32) ** block_levels(key_list[1], (SLABS, COLUMNS, EL_DEV, POINTS), ((0, 4), (1, 8)), -0.2, 0.2)), 0.02, 0.5),
        "mass_rate": jnp.clip(jnp.exp(math.log(80.0) - 2.0794415 * jax.random.uniform(key_list[2], (SLABS, COLUMNS, EL_DEV, POINTS), jnp.float32) ** block_levels(key_list[2], (SLABS, COLUMNS, EL_DEV, POINTS), ((0, 4), (1, 8)), -0.2, 0.2)), 10.0, 80.0),
        "slot_element": draw_slot_element(jax.random.fold_in(key_list[4], 71), 0),
    }


axis_weights = (1.0, 1.0, 4.0)
highest = lax.Precision.HIGHEST


def legendre_rows(nodes, degree):
    rows = [nodes * 0.0 + 1.0, nodes]
    for order in range(2, degree + 1):
        rows.append(((2 * order - 1) * nodes * rows[-1] - (order - 1) * rows[-2]) / order)
    return np.stack(rows, 1)


def spectral_tables():
    degree = 7
    nodes = np.cos(np.pi * np.arange(degree + 1) / degree)
    for sweep in range(60):
        legendre = legendre_rows(nodes, degree)
        nodes = nodes - (nodes * legendre[:, degree] - legendre[:, degree - 1]) / ((degree + 1) * legendre[:, degree])
    nodes = nodes[::-1].copy()
    top_values = legendre_rows(nodes, degree)[:, degree]
    weights = 2.0 / (degree * (degree + 1) * top_values ** 2)
    identity = np.eye(degree + 1)
    spacing = nodes[:, None] - nodes[None, :] + identity
    derivative = top_values[:, None] / top_values[None, :] / spacing * (1.0 - identity)
    corner_fix = np.zeros(degree + 1)
    corner_fix[0] = -degree * (degree + 1) / 4.0
    corner_fix[degree] = degree * (degree + 1) / 4.0
    derivative = derivative + identity * corner_fix[None, :]
    kron_table = np.concatenate((np.kron(derivative, identity).T, np.kron(identity, derivative).T), 1)
    weights3 = (weights[:, None, None] * weights[None, :, None] * weights[None, None, :]).reshape(-1)
    return derivative, kron_table, weights3


def inverse_multiplicity(depth):
    point = np.arange(512)
    ends_a = ((point // 64) % 7 == 0) * 1.0
    ends_b = (((point // 8) % 8) % 7 == 0) * 1.0
    within = point % 8
    layer = np.arange(depth)[:, None]
    vertical = 1.0 + ((within == 0) & (layer > 0)) + ((within == 7) & (layer < depth - 1))
    return 1.0 / ((1.0 + ends_a) * (1.0 + ends_b) * vertical)


def contract(values, coef_x, coef_yz, coef_mass, derivative, kron_table):
    elements = values.shape[0]
    slab_view = values.reshape(elements, 8, 64)
    grad_x = jnp.einsum("ab,ebk->eak", derivative, slab_view, precision=highest)
    grad_yz = jnp.dot(values.reshape(elements * 8, 64), kron_table, precision=highest)
    back_x = jnp.einsum("ba,ebk->eak", derivative, grad_x * coef_x, precision=highest).reshape(elements, 512)
    back_yz = jnp.dot(grad_yz * coef_yz, kron_table.T, precision=highest).reshape(elements, 512)
    return back_x + back_yz + coef_mass * values


def coefficients(visc_rows, mass_rows, weights3):
    elements = visc_rows.shape[0]
    spread = visc_rows * weights3
    coef_x = (axis_weights[0] * spread).reshape(elements, 8, 64)
    coef_yz = jnp.concatenate(((axis_weights[1] * spread).reshape(elements * 8, 64), (axis_weights[2] * spread).reshape(elements * 8, 64)), 1)
    coef_mass = mass_rows * weights3
    return coef_x, coef_yz, coef_mass


def join_periodic(low_face, high_face, position):
    summed = high_face + jnp.roll(low_face, -1, position)
    return jnp.roll(summed, 1, position), summed


def join_walls(low_face, high_face, position):
    extent = low_face.shape[position]
    summed = lax.slice_in_dim(high_face, 0, extent - 1, axis=position) + lax.slice_in_dim(low_face, 1, extent, axis=position)
    new_high = jnp.concatenate((summed, lax.slice_in_dim(high_face, extent - 1, extent, axis=position)), position)
    new_low = jnp.concatenate((lax.slice_in_dim(low_face, 0, 1, axis=position), summed), position)
    return new_low, new_high


def assemble(values):
    outer_shape = values.shape
    new_low, new_high = join_periodic(values[..., :64], values[..., 448:], 0)
    values = jnp.concatenate((new_low, values[..., 64:448], new_high), -1)
    planes = values.reshape(outer_shape[:3] + (8, 64))
    new_low, new_high = join_periodic(planes[..., 0:8], planes[..., 56:64], 1)
    values = jnp.concatenate((new_low, planes[..., 8:56], new_high), -1).reshape(outer_shape)
    column_view = values.reshape(outer_shape[:3] + (64, 8))
    new_low, new_high = join_walls(column_view[..., 0], column_view[..., 7], 2)
    return jnp.concatenate((new_low[..., None], column_view[..., 1:7], new_high[..., None]), -1).reshape(outer_shape)


def invert(order_slots):
    return jnp.zeros(order_slots.shape, jnp.int32).at[order_slots].set(jnp.arange(order_slots.shape[0], dtype=jnp.int32))


def take_rows(rows, indices):
    return jnp.take(rows, indices, axis=0)


def to_grid(values, slot_element):
    inverse = jax.vmap(jax.vmap(invert))(slot_element)
    gathered = jax.vmap(jax.vmap(take_rows))(values, inverse)
    gathered = gathered.reshape(SLABS, COLUMNS, EX, EY, EZ, POINTS).transpose(0, 2, 1, 3, 4, 5)
    return gathered.reshape(NEX, NEY, EZ, POINTS)


def from_grid(values, slot_element):
    blocks = values.reshape(SLABS, EX, COLUMNS, EY, EZ, POINTS).transpose(0, 2, 1, 3, 4, 5)
    blocks = blocks.reshape(SLABS, COLUMNS, EL_DEV, POINTS)
    return jax.vmap(jax.vmap(take_rows))(blocks, slot_element)


def reference(forcing, viscosity, mass_rate, slot_element):
    derivative_np, kron_np, weights_np = spectral_tables()
    derivative = jnp.asarray(derivative_np, jnp.float32)
    kron_table = jnp.asarray(kron_np, jnp.float32)
    weights3 = jnp.asarray(weights_np, jnp.float32)
    inv_mult = jnp.asarray(inverse_multiplicity(EZ), jnp.float32)
    grid_forcing = to_grid(forcing, slot_element)
    visc_slabs = to_grid(viscosity, slot_element).reshape(NEX, NEY * EZ, POINTS)
    mass_slabs = to_grid(mass_rate, slot_element).reshape(NEX, NEY * EZ, POINTS)
    grid_shape = (NEX, NEY, EZ, POINTS)

    def slab_diagonal(items):
        coef_x, coef_yz, coef_mass = coefficients(items[0], items[1], weights3)
        elements = coef_mass.shape[0]
        part_x = jnp.einsum("ba,ebk->eak", derivative * derivative, coef_x, precision=highest).reshape(elements, 512)
        part_yz = jnp.dot(coef_yz, (kron_table * kron_table).T, precision=highest).reshape(elements, 512)
        return part_x + part_yz + coef_mass

    def slab_apply(items):
        coef_x, coef_yz, coef_mass = coefficients(items[1], items[2], weights3)
        return contract(items[0], coef_x, coef_yz, coef_mass, derivative, kron_table)

    def apply_operator(values):
        local_terms = lax.map(slab_apply, (values.reshape(NEX, NEY * EZ, POINTS), visc_slabs, mass_slabs))
        return assemble(local_terms.reshape(grid_shape))

    def inner(left, right):
        return jnp.sum(left * right * inv_mult)

    right_side = assemble(grid_forcing)
    diagonal = assemble(lax.map(slab_diagonal, (visc_slabs, mass_slabs)).reshape(grid_shape))
    jacobi = 1.0 / diagonal
    solution = jnp.zeros(grid_shape, jnp.float32)
    residual = right_side
    precond = jacobi * residual
    direction = precond
    norm_now = inner(residual, precond)
    for step in range(ITERS):
        mapped = apply_operator(direction)
        step_len = norm_now / inner(direction, mapped)
        solution = solution + step_len * direction
        residual = residual - step_len * mapped
        if step + 1 < ITERS:
            precond = jacobi * residual
            norm_next = inner(residual, precond)
            direction = precond + (norm_next / norm_now) * direction
            norm_now = norm_next
    return from_grid(solution, slot_element), from_grid(residual, slot_element)
```

```python
import functools

import jax
import jax.numpy as jnp
import numpy as np
from jax import lax
from jax.experimental import pallas as pl
from jax.experimental.pallas import tpu as pltpu
from jax.sharding import PartitionSpec as P

EZ = 64
LANES = 128
HALF = 64
POINTS = 512
SPLIT = 2
VERTICAL = 4.0
VMEM_BYTES = 24 * 1024 * 1024


def legendre_rows(nodes, degree):
    rows = [nodes * 0.0 + 1.0, nodes]
    for order in range(2, degree + 1):
        rows.append(((2 * order - 1) * nodes * rows[-1] - (order - 1) * rows[-2]) / order)
    return np.stack(rows, 1)


def spectral_tables():
    degree = 7
    nodes = np.cos(np.pi * np.arange(degree + 1) / degree)
    for sweep in range(60):
        legendre = legendre_rows(nodes, degree)
        nodes = nodes - (nodes * legendre[:, degree] - legendre[:, degree - 1]) / (
            (degree + 1) * legendre[:, degree]
        )
    nodes = nodes[::-1].copy()
    top_values = legendre_rows(nodes, degree)[:, degree]
    weights = 2.0 / (degree * (degree + 1) * top_values**2)
    identity = np.eye(degree + 1)
    spacing = nodes[:, None] - nodes[None, :] + identity
    derivative = top_values[:, None] / top_values[None, :] / spacing * (1.0 - identity)
    corner_fix = np.zeros(degree + 1)
    corner_fix[0] = -degree * (degree + 1) / 4.0
    corner_fix[degree] = degree * (degree + 1) / 4.0
    derivative = derivative + identity * corner_fix[None, :]
    weights3 = (weights[:, None, None] * weights[None, :, None] * weights[None, None, :]).reshape(
        -1
    )
    return (derivative, weights3)


DERIVATIVE, WEIGHTS3 = spectral_tables()


def row(a, b):
    return pl.ds(64 * a + 8 * b, 8)


def across(a, c):
    return pl.ds(64 * a + c, 8, stride=8)


def along(matrix, lines, sign):
    evens = [lines[j] + lines[7 - j] for j in range(4)]
    odds = [lines[j] - lines[7 - j] for j in range(4)]
    out = [None] * 8
    for i in range(4):
        even = odd = None
        for j in range(4):
            even_term = evens[j] * float((matrix[i, j] + matrix[i, 7 - j]) / 2)
            odd_term = odds[j] * float((matrix[i, j] - matrix[i, 7 - j]) / 2)
            even = even_term if even is None else even + even_term
            odd = odd_term if odd is None else odd + odd_term
        out[i] = even + odd
        out[7 - i] = even - odd if sign > 0 else odd - even
    return out


def lane_index():
    return lax.broadcasted_iota(jnp.int32, (8, LANES), 1)


def sublane_index():
    return lax.broadcasted_iota(jnp.int32, (8, LANES), 0)


def join_vertical(low, high):
    layer = lane_index() % EZ
    new_low = low + jnp.where(layer > 0, pltpu.roll(high, 1, 1), 0.0)
    new_high = high + jnp.where(layer < EZ - 1, pltpu.roll(low, LANES - 1, 1), 0.0)
    return new_low, new_high


def pack_faces(grid, face_x, face_y, field):
    first = lane_index() < HALF
    for b in range(8):
        face_x[pl.ds(64 * field + 8 * b, 8), :] = jnp.where(
            first, grid[row(0, b), :], grid[row(7, b), :]
        )
    for a in range(8):
        face_y[pl.ds(128 * field + 8 * a, 8), :] = grid[row(a, 0), :]
        face_y[pl.ds(128 * field + 64 + 8 * a, 8), :] = grid[row(a, 7), :]


def ghost_x(from_even, from_odd, field, b):
    rows = pl.ds(64 * field + 8 * b, 8)
    odd = lax.axis_index("gx") % 2
    first = (lane_index() < HALF).astype(jnp.int32)
    return jnp.where(first != odd, from_even[rows, :], from_odd[rows, :])


def joined_x(a, low, high, ghost):
    first = lane_index() < HALF
    if a == 0:
        return low + pltpu.roll(jnp.where(first, high, ghost), HALF, 1)
    return high + pltpu.roll(jnp.where(first, ghost, low), HALF, 1)


def assembled(a, b, grid, received, field):
    even_x, odd_x, even_y, odd_y = received
    value = grid[row(a, b), :]
    if a in (0, 7):
        value = joined_x(
            a, grid[row(0, b), :], grid[row(7, b), :], ghost_x(even_x, odd_x, field, b)
        )
    if b in (0, 7):
        rows = pl.ds(64 * field + 8 * a, 8)
        odd = lax.axis_index("yz") % 2 == 1
        pick = odd if b == 0 else jnp.logical_not(odd)
        value = value + jnp.where(pick, even_y[rows, :], odd_y[rows, :])
    return value


def edges_kernel(fields, face_y, even_x, odd_x, to_even, to_odd):
    odd = lax.axis_index("yz") % 2 == 1
    for field in range(fields):
        faces = []
        for side in range(2):
            part = [face_y[pl.ds(128 * field + 64 * side + 8 * a, 8), :] for a in range(8)]
            ghost = ghost_x(even_x, odd_x, field, 7 * side)
            low, high = part[0], part[7]
            part[0] = joined_x(0, low, high, ghost)
            part[7] = joined_x(7, low, high, ghost)
            faces.append(part)
        for a in range(8):
            rows = pl.ds(64 * field + 8 * a, 8)
            to_even[rows, :] = jnp.where(odd, faces[0][a], faces[1][a])
            to_odd[rows, :] = jnp.where(odd, faces[1][a], faces[0][a])


def selection(slots):
    elements = lax.broadcasted_iota(jnp.int32, (LANES, LANES), 0)
    return jnp.where(elements == slots[...], 1.0, 0.0)


def parts_of(values):
    parts = []
    for _ in range(SPLIT):
        parts.append(values.astype(jnp.bfloat16))
        values = values - parts[-1].astype(jnp.float32)
    return parts


def to_grid(chosen, values):
    parts = jnp.concatenate(parts_of(values[0, 0]), 0)
    picked = jnp.dot(
        jnp.concatenate([chosen.astype(jnp.bfloat16)] * SPLIT, 1),
        parts,
        preferred_element_type=jnp.float32,
    )
    return picked.T


def setup_kernel(
    forcing, viscosity, mass_rate, slots, weights, right, diagonal, spread, mass, face_x, face_y
):
    chosen = selection(slots)
    right[...] = to_grid(chosen, forcing)
    spread[...] = to_grid(chosen, viscosity) * weights[...]
    mass[...] = to_grid(chosen, mass_rate) * weights[...]
    squares = (DERIVATIVE * DERIVATIVE).T
    for b in range(8):
        lines = along(squares, [spread[row(a, b), :] for a in range(8)], 1)
        for a in range(8):
            diagonal[row(a, b), :] = lines[a] + mass[row(a, b), :]
    for a in range(8):
        lines = along(squares, [spread[row(a, b), :] for b in range(8)], 1)
        for b in range(8):
            diagonal[row(a, b), :] += lines[b]
    for a in range(8):
        lines = along(VERTICAL * squares, [spread[across(a, c), :] for c in range(8)], 1)
        lines = [lines[c] + diagonal[across(a, c), :] for c in range(8)]
        lines[0], lines[7] = join_vertical(lines[0], lines[7])
        for c in range(8):
            diagonal[across(a, c), :] = lines[c]
        low, high = join_vertical(right[across(a, 0), :], right[across(a, 7), :])
        right[across(a, 0), :] = low
        right[across(a, 7), :] = high
    pack_faces(right, face_x, face_y, 0)
    pack_faces(diagonal, face_x, face_y, 1)


def operate(values, spread, mass, image, face_x, face_y):
    forward, backward = DERIVATIVE, DERIVATIVE.T
    for b in range(8):
        lines = [values[row(a, b), :] for a in range(8)]
        slopes = along(forward, lines, -1)
        back = along(backward, [slopes[a] * spread[row(a, b), :] for a in range(8)], -1)
        for a in range(8):
            image[row(a, b), :] = back[a] + mass[row(a, b), :] * lines[a]
    for a in range(8):
        slopes = along(forward, [values[row(a, b), :] for b in range(8)], -1)
        back = along(backward, [slopes[b] * spread[row(a, b), :] for b in range(8)], -1)
        for b in range(8):
            image[row(a, b), :] += back[b]
    energy = jnp.zeros((8, LANES), jnp.float32)
    for a in range(8):
        lines = [values[across(a, c), :] for c in range(8)]
        slopes = along(forward, lines, -1)
        back = along(
            VERTICAL * backward, [slopes[c] * spread[across(a, c), :] for c in range(8)], -1
        )
        back = [back[c] + image[across(a, c), :] for c in range(8)]
        for c in range(8):
            energy = energy + back[c] * lines[c]
        back[0], back[7] = join_vertical(back[0], back[7])
        for c in range(8):
            image[across(a, c), :] = back[c]
    pack_faces(image, face_x, face_y, 0)
    return energy


def weighted(sums):
    layer, point = lane_index() % EZ, sublane_index()
    below = jnp.logical_and(point == 0, layer > 0)
    above = jnp.logical_and(point == 7, layer < EZ - 1)
    shared = jnp.where(jnp.logical_or(below, above), 0.5, 1.0)
    return (sums[0] + 0.5 * sums[1] + 0.25 * sums[2]) * shared


def ends(a, b):
    return int(a in (0, 7)) + int(b in (0, 7))


def first_kernel(
    right, diagonal, even_x, odd_x, even_y, odd_y, spread, mass,
    whole_diagonal, values, image, face_x, face_y, moments,
):
    received = (even_x, odd_x, even_y, odd_y)
    sums = [jnp.zeros((8, LANES), jnp.float32)] * 3
    for a in range(8):
        for b in range(8):
            source = assembled(a, b, right, received, 0)
            scale = assembled(a, b, diagonal, received, 1)
            value = source / scale
            whole_diagonal[row(a, b), :] = scale
            values[row(a, b), :] = value
            sums[ends(a, b)] = sums[ends(a, b)] + source * value
    moments[...] = weighted(sums)
    operate(values, spread, mass, image, face_x, face_y)


def next_values(before_image, received, diagonal, before, values):
    cross = [jnp.zeros((8, LANES), jnp.float32)] * 3
    square = [jnp.zeros((8, LANES), jnp.float32)] * 3
    for a in range(8):
        for b in range(8):
            scale = diagonal[row(a, b), :]
            old = before[row(a, b), :]
            value = assembled(a, b, before_image, received, 0) / scale - old
            values[row(a, b), :] = value
            scaled = scale * value
            kind = ends(a, b)
            cross[kind] = cross[kind] + scaled * old
            square[kind] = square[kind] + scaled * value
    return weighted(cross), weighted(square)


def second_kernel(
    before_image, even_x, odd_x, even_y, odd_y, diagonal, before, spread, mass,
    values, image, face_x, face_y, moments,
):
    received = (even_x, odd_x, even_y, odd_y)
    cross, square = next_values(before_image, received, diagonal, before, values)
    moments[pl.ds(0, 8), :] = cross
    moments[pl.ds(8, 8), :] = square
    operate(values, spread, mass, image, face_x, face_y)


def third_kernel(
    before_image, even_x, odd_x, even_y, odd_y, diagonal, before, spread, mass, moments0, moments1,
    values, image, face_x, face_y, sums,
):
    received = (even_x, odd_x, even_y, odd_y)
    cross, square = next_values(before_image, received, diagonal, before, values)
    energy = operate(values, spread, mass, image, face_x, face_y)
    parts = [
        moments0[...], moments1[pl.ds(0, 8), :], moments1[pl.ds(8, 8), :], cross, square, energy
    ]
    lane = lax.broadcasted_iota(jnp.int32, (1, LANES), 1)
    line = jnp.zeros((1, LANES), jnp.float32)
    for k, part in enumerate(parts):
        total = jnp.sum(jnp.sum(part, 0, keepdims=True), 1, keepdims=True)
        line = jnp.where(lane == k, total, line)
    sums[...] = jnp.broadcast_to(line[None], sums.shape)


def recurrence(moments):
    moments = moments[:5] + [moments[5] - moments[4]]
    zero = jnp.zeros_like(moments[0])
    one = zero + 1.0

    def form(left, right, shift):
        total = zero
        for i in range(3):
            for j in range(3):
                if left[i] is not None and right[j] is not None:
                    entry = moments[i + j]
                    if shift:
                        entry = entry + moments[i + j + 1]
                    total = total + left[i] * right[j] * entry
        return total

    def ratio(top, bottom):
        fine = jnp.logical_and(bottom > 0.0, top > 0.0)
        return jnp.where(fine, top / jnp.where(fine, bottom, 1.0), 0.0)

    def add(left, scale, right):
        out = []
        for x, y in zip(left, right):
            if y is None:
                out.append(x)
            else:
                out.append(scale * y if x is None else x + scale * y)
        return out

    direction = [one, None, None, None]
    precond = [one, None, None, None]
    result = [None, None, None, None]
    norm = moments[0]
    for step in range(3):
        curve = form(direction, direction, True)
        length = ratio(norm, curve)
        result = add(result, length, direction)
        moved = add(direction, 1.0, [None] + direction[:3])
        if step == 0:
            precond = [jnp.where(curve > 0.0, moments[1] / curve, 1.0), -length, None, None]
        else:
            precond = add(precond, -length, moved)
        if step < 2:
            norm_next = form(precond, precond, False)
            direction = add(precond, ratio(norm_next, norm), direction)
            norm = norm_next
    return result[:3], precond


def last_kernel(
    before_image, even_x, odd_x, even_y, odd_y, diagonal, values0, values1, values2, sums, slots,
    solution, residual, solution_grid, residual_grid,
):
    received = (even_x, odd_x, even_y, odd_y)
    line = jnp.sum(sums[...], 0)
    lane = lax.broadcasted_iota(jnp.int32, (1, LANES), 1)
    moments = [
        jnp.sum(jnp.where(lane == k, line, 0.0), 1, keepdims=True) for k in range(6)
    ]
    result, precond = recurrence(moments)
    spread_out = lambda scalar: jnp.broadcast_to(scalar, (8, LANES))
    result = [spread_out(entry) for entry in result]
    precond = [spread_out(entry) for entry in precond]
    for a in range(8):
        for b in range(8):
            rows = row(a, b)
            basis = [values0[rows, :], values1[rows, :], values2[rows, :]]
            scale = diagonal[rows, :]
            image = assembled(a, b, before_image, received, 0) - scale * basis[2]
            near = result[0] * basis[0] + result[1] * basis[1] + result[2] * basis[2]
            far = precond[0] * basis[0] + precond[1] * basis[1] + precond[2] * basis[2]
            solution_grid[rows, :] = near
            residual_grid[rows, :] = scale * far + precond[3] * image
    chosen = selection(slots).T.astype(jnp.bfloat16)
    for grid, out in ((solution_grid, solution), (residual_grid, residual)):
        total = None
        for part in parts_of(grid[...]):
            term = lax.dot_general(
                chosen, part, (((1,), (1,)), ((), ())), preferred_element_type=jnp.float32
            )
            total = term if total is None else total + term
        out[0, 0] = total


def call(kernel, name, shapes, scratch, *operands):
    return pl.pallas_call(
        kernel,
        out_shape=[jax.ShapeDtypeStruct(shape, jnp.float32) for shape in shapes],
        in_specs=[pl.BlockSpec(memory_space=pltpu.VMEM)] * len(operands),
        out_specs=[pl.BlockSpec(memory_space=pltpu.VMEM)] * len(shapes),
        scratch_shapes=[pltpu.VMEM(shape, jnp.float32) for shape in scratch],
        compiler_params=pltpu.CompilerParams(vmem_limit_bytes=VMEM_BYTES),
        name=name,
    )(*operands)


def swapped(block, axis):
    extent = lax.axis_size(axis)
    even = [(i, i ^ 1) for i in range(extent)]
    odd = [(i, (((i + 1) ^ 1) - 1) % extent) for i in range(extent)]
    return lax.ppermute(block[0], axis, even), lax.ppermute(block[1], axis, odd)


def exchange(fields, face_x, face_y):
    received_x = swapped((face_x, face_x), "gx")
    shape = (64 * fields, LANES)
    sent_y = call(
        functools.partial(edges_kernel, fields), "edges", [shape, shape], [], face_y, *received_x
    )
    return (*received_x, *swapped(sent_y, "yz"))


def body(forcing, viscosity, mass_rate, slot_element):
    devices = lax.axis_size("gx") * lax.axis_size("yz")
    slots = slot_element[0]
    weights = jnp.broadcast_to(jnp.asarray(WEIGHTS3, jnp.float32)[:, None], (POINTS, LANES))
    grid = (POINTS, LANES)
    face_x, face_y, moment = (64, LANES), (128, LANES), (8, LANES)
    right, diagonal, spread, mass, out_x, out_y = call(
        setup_kernel, "setup", [grid] * 4 + [(128, LANES), (256, LANES)], [],
        forcing, viscosity, mass_rate, slots, weights,
    )
    received = exchange(2, out_x, out_y)
    diagonal, values0, image, out_x, out_y, moments0 = call(
        first_kernel, "first", [grid] * 3 + [face_x, face_y, moment], [],
        right, diagonal, *received, spread, mass,
    )
    received = exchange(1, out_x, out_y)
    values1, image, out_x, out_y, moments1 = call(
        second_kernel, "second", [grid] * 2 + [face_x, face_y, (16, LANES)], [],
        image, *received, diagonal, values0, spread, mass,
    )
    received = exchange(1, out_x, out_y)
    values2, image, out_x, out_y, sums = call(
        third_kernel, "third", [grid] * 2 + [face_x, face_y, (devices, 1, LANES)], [],
        image, *received, diagonal, values1, spread, mass, moments0, moments1,
    )
    sums = lax.all_to_all(sums, ("gx", "yz"), 0, 0)
    received = exchange(1, out_x, out_y)
    return call(
        last_kernel, "last", [forcing.shape] * 2, [grid] * 2,
        image, *received, diagonal, values0, values1, values2, sums, slots,
    )


def solution(mesh):
    placed = (
        P("gx", "yz", None, None),
        P("gx", "yz", None, None),
        P("gx", "yz", None, None),
        P("gx", "yz", None),
    )
    return jax.shard_map(
        body,
        mesh=mesh,
        in_specs=placed,
        out_specs=(P("gx", "yz", None, None), P("gx", "yz", None, None)),
        check_vma=False,
    )
```

```python
import functools

import jax
import jax.numpy as jnp
import numpy as np
from jax import lax
from jax.experimental import pallas as pl
from jax.experimental.pallas import tpu as pltpu
from jax.sharding import PartitionSpec as P

EZ = 64
LANES = 128
HALF = 64
POINTS = 512
SPLIT = 2
VERTICAL = 4.0
VMEM_BYTES = 24 * 1024 * 1024


def legendre_rows(nodes, degree):
    rows = [nodes * 0.0 + 1.0, nodes]
    for order in range(2, degree + 1):
        rows.append(((2 * order - 1) * nodes * rows[-1] - (order - 1) * rows[-2]) / order)
    return np.stack(rows, 1)


def spectral_tables():
    degree = 7
    nodes = np.cos(np.pi * np.arange(degree + 1) / degree)
    for sweep in range(60):
        legendre = legendre_rows(nodes, degree)
        nodes = nodes - (nodes * legendre[:, degree] - legendre[:, degree - 1]) / (
            (degree + 1) * legendre[:, degree]
        )
    nodes = nodes[::-1].copy()
    top_values = legendre_rows(nodes, degree)[:, degree]
    weights = 2.0 / (degree * (degree + 1) * top_values**2)
    identity = np.eye(degree + 1)
    spacing = nodes[:, None] - nodes[None, :] + identity
    derivative = top_values[:, None] / top_values[None, :] / spacing * (1.0 - identity)
    corner_fix = np.zeros(degree + 1)
    corner_fix[0] = -degree * (degree + 1) / 4.0
    corner_fix[degree] = degree * (degree + 1) / 4.0
    derivative = derivative + identity * corner_fix[None, :]
    return (derivative, weights)


DERIVATIVE, WEIGHTS = spectral_tables()


def row(a, b):
    return pl.ds(64 * a + 8 * b, 8)


def across(a, c):
    return pl.ds(64 * a + c, 8, stride=8)


def along(matrix, lines, sign):
    evens = [lines[j] + lines[7 - j] for j in range(4)]
    odds = [lines[j] - lines[7 - j] for j in range(4)]
    out = [None] * 8
    for i in range(4):
        even = odd = None
        for j in range(4):
            even_term = evens[j] * float((matrix[i, j] + matrix[i, 7 - j]) / 2)
            odd_term = odds[j] * float((matrix[i, j] - matrix[i, 7 - j]) / 2)
            even = even_term if even is None else even + even_term
            odd = odd_term if odd is None else odd + odd_term
        out[i] = even + odd
        out[7 - i] = even - odd if sign > 0 else odd - even
    return out


def lane_index():
    return lax.broadcasted_iota(jnp.int32, (8, LANES), 1)


def sublane_index():
    return lax.broadcasted_iota(jnp.int32, (8, LANES), 0)


def join_vertical(low, high):
    layer = lane_index() % EZ
    new_low = low + jnp.where(layer > 0, pltpu.roll(high, 1, 1), 0.0)
    new_high = high + jnp.where(layer < EZ - 1, pltpu.roll(low, LANES - 1, 1), 0.0)
    return new_low, new_high


def pack_faces(grid, face_x, face_y, field):
    first = lane_index() < HALF
    for b in range(8):
        face_x[pl.ds(64 * field + 8 * b, 8), :] = jnp.where(
            first, grid[row(0, b), :], grid[row(7, b), :]
        )
    for a in range(8):
        face_y[pl.ds(128 * field + 8 * a, 8), :] = grid[row(a, 0), :]
        face_y[pl.ds(128 * field + 64 + 8 * a, 8), :] = grid[row(a, 7), :]


def ghost_x(from_even, from_odd, field, b):
    rows = pl.ds(64 * field + 8 * b, 8)
    odd = lax.axis_index("gx") % 2
    first = (lane_index() < HALF).astype(jnp.int32)
    return jnp.where(first != odd, from_even[rows, :], from_odd[rows, :])


def joined_x(a, low, high, ghost):
    first = lane_index() < HALF
    if a == 0:
        return low + pltpu.roll(jnp.where(first, high, ghost), HALF, 1)
    return high + pltpu.roll(jnp.where(first, ghost, low), HALF, 1)


def assembled(a, b, grid, received, field):
    even_x, odd_x, even_y, odd_y = received
    value = grid[row(a, b), :]
    if a in (0, 7):
        value = joined_x(
            a, grid[row(0, b), :], grid[row(7, b), :], ghost_x(even_x, odd_x, field, b)
        )
    if b in (0, 7):
        rows = pl.ds(64 * field + 8 * a, 8)
        odd = lax.axis_index("yz") % 2 == 1
        pick = odd if b == 0 else jnp.logical_not(odd)
        value = value + jnp.where(pick, even_y[rows, :], odd_y[rows, :])
    return value


def edges_kernel(fields, face_y, even_x, odd_x, to_even, to_odd):
    odd = lax.axis_index("yz") % 2 == 1
    for field in range(fields):
        faces = []
        for side in range(2):
            part = [face_y[pl.ds(128 * field + 64 * side + 8 * a, 8), :] for a in range(8)]
            ghost = ghost_x(even_x, odd_x, field, 7 * side)
            low, high = part[0], part[7]
            part[0] = joined_x(0, low, high, ghost)
            part[7] = joined_x(7, low, high, ghost)
            faces.append(part)
        for a in range(8):
            rows = pl.ds(64 * field + 8 * a, 8)
            to_even[rows, :] = jnp.where(odd, faces[0][a], faces[1][a])
            to_odd[rows, :] = jnp.where(odd, faces[1][a], faces[0][a])


def selection(slots):
    elements = lax.broadcasted_iota(jnp.int32, (LANES, LANES), 0)
    return jnp.where(elements == slots[...], 1.0, 0.0)


def parts_of(values):
    parts = []
    for _ in range(SPLIT):
        parts.append(values.astype(jnp.bfloat16))
        values = values - parts[-1].astype(jnp.float32)
    return parts


def to_grid(chosen, values):
    parts = jnp.concatenate(parts_of(values), 0)
    picked = jnp.dot(
        jnp.concatenate([chosen.astype(jnp.bfloat16)] * SPLIT, 1),
        parts,
        preferred_element_type=jnp.float32,
    )
    return picked.T


def setup_kernel(
    forcing, viscosity, mass_rate, slots, right, diagonal, spread, mass, face_x, face_y,
    held, arrived,
):
    copies = [
        pltpu.make_async_copy(source.at[0, 0], held.at[k], arrived.at[k])
        for k, source in enumerate((viscosity, mass_rate, forcing))
    ]
    for copy in copies:
        copy.start()
    chosen = selection(slots)
    point = sublane_index()
    last_weight = jnp.zeros((8, LANES), jnp.float32)
    for c in range(8):
        last_weight = jnp.where(point == c, float(WEIGHTS[c]), last_weight)
    copies[0].wait()
    spread[...] = to_grid(chosen, held[0])
    copies[1].wait()
    mass[...] = to_grid(chosen, held[1])
    for a in range(8):
        for b in range(8):
            weight = last_weight * float(WEIGHTS[a] * WEIGHTS[b])
            spread[row(a, b), :] *= weight
            mass[row(a, b), :] *= weight
    copies[2].wait()
    right[...] = to_grid(chosen, held[2])
    squares = (DERIVATIVE * DERIVATIVE).T
    for b in range(8):
        lines = along(squares, [spread[row(a, b), :] for a in range(8)], 1)
        for a in range(8):
            diagonal[row(a, b), :] = lines[a] + mass[row(a, b), :]
    for a in range(8):
        lines = along(squares, [spread[row(a, b), :] for b in range(8)], 1)
        for b in range(8):
            diagonal[row(a, b), :] += lines[b]
    for a in range(8):
        lines = along(VERTICAL * squares, [spread[across(a, c), :] for c in range(8)], 1)
        lines = [lines[c] + diagonal[across(a, c), :] for c in range(8)]
        lines[0], lines[7] = join_vertical(lines[0], lines[7])
        for c in range(8):
            diagonal[across(a, c), :] = lines[c]
        low, high = join_vertical(right[across(a, 0), :], right[across(a, 7), :])
        right[across(a, 0), :] = low
        right[across(a, 7), :] = high
    pack_faces(right, face_x, face_y, 0)
    pack_faces(diagonal, face_x, face_y, 1)


def operate(values, spread, mass, image, face_x, face_y):
    forward, backward = DERIVATIVE, DERIVATIVE.T
    for b in range(8):
        lines = [values[row(a, b), :] for a in range(8)]
        slopes = along(forward, lines, -1)
        back = along(backward, [slopes[a] * spread[row(a, b), :] for a in range(8)], -1)
        for a in range(8):
            image[row(a, b), :] = back[a] + mass[row(a, b), :] * lines[a]
    for a in range(8):
        slopes = along(forward, [values[row(a, b), :] for b in range(8)], -1)
        back = along(backward, [slopes[b] * spread[row(a, b), :] for b in range(8)], -1)
        for b in range(8):
            image[row(a, b), :] += back[b]
    energy = jnp.zeros((8, LANES), jnp.float32)
    for a in range(8):
        lines = [values[across(a, c), :] for c in range(8)]
        slopes = along(forward, lines, -1)
        back = along(
            VERTICAL * backward, [slopes[c] * spread[across(a, c), :] for c in range(8)], -1
        )
        back = [back[c] + image[across(a, c), :] for c in range(8)]
        for c in range(8):
            energy = energy + back[c] * lines[c]
        back[0], back[7] = join_vertical(back[0], back[7])
        for c in range(8):
            image[across(a, c), :] = back[c]
    pack_faces(image, face_x, face_y, 0)
    return energy


def weighted(sums):
    layer, point = lane_index() % EZ, sublane_index()
    below = jnp.logical_and(point == 0, layer > 0)
    above = jnp.logical_and(point == 7, layer < EZ - 1)
    shared = jnp.where(jnp.logical_or(below, above), 0.5, 1.0)
    return (sums[0] + 0.5 * sums[1] + 0.25 * sums[2]) * shared


def ends(a, b):
    return int(a in (0, 7)) + int(b in (0, 7))


def first_kernel(
    right, diagonal, even_x, odd_x, even_y, odd_y, spread, mass,
    whole_diagonal, values, image, face_x, face_y, moments,
):
    received = (even_x, odd_x, even_y, odd_y)
    sums = [jnp.zeros((8, LANES), jnp.float32)] * 3
    for a in range(8):
        for b in range(8):
            source = assembled(a, b, right, received, 0)
            scale = assembled(a, b, diagonal, received, 1)
            value = source / scale
            whole_diagonal[row(a, b), :] = scale
            values[row(a, b), :] = value
            sums[ends(a, b)] = sums[ends(a, b)] + source * value
    moments[...] = weighted(sums)
    operate(values, spread, mass, image, face_x, face_y)


def next_values(before_image, received, diagonal, before, values):
    cross = [jnp.zeros((8, LANES), jnp.float32)] * 3
    square = [jnp.zeros((8, LANES), jnp.float32)] * 3
    for a in range(8):
        for b in range(8):
            scale = diagonal[row(a, b), :]
            old = before[row(a, b), :]
            value = assembled(a, b, before_image, received, 0) / scale - old
            values[row(a, b), :] = value
            scaled = scale * value
            kind = ends(a, b)
            cross[kind] = cross[kind] + scaled * old
            square[kind] = square[kind] + scaled * value
    return weighted(cross), weighted(square)


def second_kernel(
    before_image, even_x, odd_x, even_y, odd_y, diagonal, before, spread, mass,
    values, image, face_x, face_y, moments,
):
    received = (even_x, odd_x, even_y, odd_y)
    cross, square = next_values(before_image, received, diagonal, before, values)
    moments[pl.ds(0, 8), :] = cross
    moments[pl.ds(8, 8), :] = square
    operate(values, spread, mass, image, face_x, face_y)


def third_kernel(
    before_image, even_x, odd_x, even_y, odd_y, diagonal, before, spread, mass, moments0, moments1,
    values, image, face_x, face_y, sums,
):
    received = (even_x, odd_x, even_y, odd_y)
    cross, square = next_values(before_image, received, diagonal, before, values)
    energy = operate(values, spread, mass, image, face_x, face_y)
    parts = [
        moments0[...], moments1[pl.ds(0, 8), :], moments1[pl.ds(8, 8), :], cross, square, energy
    ]
    lane = lax.broadcasted_iota(jnp.int32, (1, LANES), 1)
    line = jnp.zeros((1, LANES), jnp.float32)
    for k, part in enumerate(parts):
        total = jnp.sum(jnp.sum(part, 0, keepdims=True), 1, keepdims=True)
        line = jnp.where(lane == k, total, line)
    sums[...] = jnp.broadcast_to(line[None], sums.shape)


def recurrence(moments):
    moments = moments[:5] + [moments[5] - moments[4]]
    zero = jnp.zeros_like(moments[0])
    one = zero + 1.0

    def form(left, right, shift):
        total = zero
        for i in range(3):
            for j in range(3):
                if left[i] is not None and right[j] is not None:
                    entry = moments[i + j]
                    if shift:
                        entry = entry + moments[i + j + 1]
                    total = total + left[i] * right[j] * entry
        return total

    def ratio(top, bottom):
        fine = jnp.logical_and(bottom > 0.0, top > 0.0)
        return jnp.where(fine, top / jnp.where(fine, bottom, 1.0), 0.0)

    def add(left, scale, right):
        out = []
        for x, y in zip(left, right):
            if y is None:
                out.append(x)
            else:
                out.append(scale * y if x is None else x + scale * y)
        return out

    direction = [one, None, None, None]
    precond = [one, None, None, None]
    result = [None, None, None, None]
    norm = moments[0]
    for step in range(3):
        curve = form(direction, direction, True)
        length = ratio(norm, curve)
        result = add(result, length, direction)
        moved = add(direction, 1.0, [None] + direction[:3])
        if step == 0:
            precond = [jnp.where(curve > 0.0, moments[1] / curve, 1.0), -length, None, None]
        else:
            precond = add(precond, -length, moved)
        if step < 2:
            norm_next = form(precond, precond, False)
            direction = add(precond, ratio(norm_next, norm), direction)
            norm = norm_next
    return result[:3], precond


def last_kernel(
    before_image, even_x, odd_x, even_y, odd_y, diagonal, values0, values1, values2, sums, slots,
    solution, residual, solution_grid, residual_grid,
):
    received = (even_x, odd_x, even_y, odd_y)
    line = jnp.sum(sums[...], 0)
    lane = lax.broadcasted_iota(jnp.int32, (1, LANES), 1)
    moments = [
        jnp.sum(jnp.where(lane == k, line, 0.0), 1, keepdims=True) for k in range(6)
    ]
    result, precond = recurrence(moments)
    spread_out = lambda scalar: jnp.broadcast_to(scalar, (8, LANES))
    result = [spread_out(entry) for entry in result]
    precond = [spread_out(entry) for entry in precond]
    for a in range(8):
        for b in range(8):
            rows = row(a, b)
            basis = [values0[rows, :], values1[rows, :], values2[rows, :]]
            scale = diagonal[rows, :]
            image = assembled(a, b, before_image, received, 0) - scale * basis[2]
            near = result[0] * basis[0] + result[1] * basis[1] + result[2] * basis[2]
            far = precond[0] * basis[0] + precond[1] * basis[1] + precond[2] * basis[2]
            solution_grid[rows, :] = near
            residual_grid[rows, :] = scale * far + precond[3] * image
    chosen = selection(slots).T.astype(jnp.bfloat16)
    for grid, out in ((solution_grid, solution), (residual_grid, residual)):
        total = None
        for part in parts_of(grid[...]):
            term = lax.dot_general(
                chosen, part, (((1,), (1,)), ((), ())), preferred_element_type=jnp.float32
            )
            total = term if total is None else total + term
        out[0, 0] = total


def call(kernel, name, shapes, scratch, *operands, outside=0):
    places = [pltpu.HBM] * outside + [pltpu.VMEM] * (len(operands) - outside)
    return pl.pallas_call(
        kernel,
        out_shape=[jax.ShapeDtypeStruct(shape, jnp.float32) for shape in shapes],
        in_specs=[pl.BlockSpec(memory_space=place) for place in places],
        out_specs=[pl.BlockSpec(memory_space=pltpu.VMEM)] * len(shapes),
        scratch_shapes=scratch,
        compiler_params=pltpu.CompilerParams(vmem_limit_bytes=VMEM_BYTES),
        name=name,
    )(*operands)


def swapped(block, axis):
    extent = lax.axis_size(axis)
    even = [(i, i ^ 1) for i in range(extent)]
    odd = [(i, (((i + 1) ^ 1) - 1) % extent) for i in range(extent)]
    return lax.ppermute(block[0], axis, even), lax.ppermute(block[1], axis, odd)


def exchange(fields, face_x, face_y):
    received_x = swapped((face_x, face_x), "gx")
    shape = (64 * fields, LANES)
    sent_y = call(
        functools.partial(edges_kernel, fields), "edges", [shape, shape], [], face_y, *received_x
    )
    return (*received_x, *swapped(sent_y, "yz"))


def body(forcing, viscosity, mass_rate, slot_element):
    devices = lax.axis_size("gx") * lax.axis_size("yz")
    slots = slot_element[0]
    grid = (POINTS, LANES)
    face_x, face_y, moment = (64, LANES), (128, LANES), (8, LANES)
    right, diagonal, spread, mass, out_x, out_y = call(
        setup_kernel, "setup", [grid] * 4 + [(128, LANES), (256, LANES)],
        [pltpu.VMEM((3, LANES, POINTS), jnp.float32), pltpu.SemaphoreType.DMA((3,))],
        forcing, viscosity, mass_rate, slots, outside=3,
    )
    received = exchange(2, out_x, out_y)
    diagonal, values0, image, out_x, out_y, moments0 = call(
        first_kernel, "first", [grid] * 3 + [face_x, face_y, moment], [],
        right, diagonal, *received, spread, mass,
    )
    received = exchange(1, out_x, out_y)
    values1, image, out_x, out_y, moments1 = call(
        second_kernel, "second", [grid] * 2 + [face_x, face_y, (16, LANES)], [],
        image, *received, diagonal, values0, spread, mass,
    )
    received = exchange(1, out_x, out_y)
    values2, image, out_x, out_y, sums = call(
        third_kernel, "third", [grid] * 2 + [face_x, face_y, (devices, 1, LANES)], [],
        image, *received, diagonal, values1, spread, mass, moments0, moments1,
    )
    sums = lax.all_to_all(sums, ("gx", "yz"), 0, 0)
    received = exchange(1, out_x, out_y)
    return call(
        last_kernel, "last", [forcing.shape] * 2, [pltpu.VMEM(grid, jnp.float32)] * 2,
        image, *received, diagonal, values0, values1, values2, sums, slots,
    )


def solution(mesh):
    placed = (
        P("gx", "yz", None, None),
        P("gx", "yz", None, None),
        P("gx", "yz", None, None),
        P("gx", "yz", None),
    )
    return jax.shard_map(
        body,
        mesh=mesh,
        in_specs=placed,
        out_specs=(P("gx", "yz", None, None), P("gx", "yz", None, None)),
        check_vma=False,
    )
```

```python
import functools

import jax
import jax.numpy as jnp
import numpy as np
from jax import lax
from jax.experimental import pallas as pl
from jax.experimental.pallas import tpu as pltpu
from jax.sharding import PartitionSpec as P

EZ = 64
LANES = 128
HALF = 64
POINTS = 512
SPLIT = 2
VERTICAL = 4.0
VMEM_BYTES = 24 * 1024 * 1024


def legendre_rows(nodes, degree):
    rows = [nodes * 0.0 + 1.0, nodes]
    for order in range(2, degree + 1):
        rows.append(((2 * order - 1) * nodes * rows[-1] - (order - 1) * rows[-2]) / order)
    return np.stack(rows, 1)


def spectral_tables():
    degree = 7
    nodes = np.cos(np.pi * np.arange(degree + 1) / degree)
    for sweep in range(60):
        legendre = legendre_rows(nodes, degree)
        nodes = nodes - (nodes * legendre[:, degree] - legendre[:, degree - 1]) / (
            (degree + 1) * legendre[:, degree]
        )
    nodes = nodes[::-1].copy()
    top_values = legendre_rows(nodes, degree)[:, degree]
    weights = 2.0 / (degree * (degree + 1) * top_values**2)
    identity = np.eye(degree + 1)
    spacing = nodes[:, None] - nodes[None, :] + identity
    derivative = top_values[:, None] / top_values[None, :] / spacing * (1.0 - identity)
    corner_fix = np.zeros(degree + 1)
    corner_fix[0] = -degree * (degree + 1) / 4.0
    corner_fix[degree] = degree * (degree + 1) / 4.0
    derivative = derivative + identity * corner_fix[None, :]
    return (derivative, weights)


DERIVATIVE, WEIGHTS = spectral_tables()


def row(a, b):
    return pl.ds(64 * a + 8 * b, 8)


def across(a, c):
    return pl.ds(64 * a + c, 8, stride=8)


def along(matrix, lines, sign):
    evens = [lines[j] + lines[7 - j] for j in range(4)]
    odds = [lines[j] - lines[7 - j] for j in range(4)]
    out = [None] * 8
    for i in range(4):
        even = odd = None
        for j in range(4):
            even_term = evens[j] * float((matrix[i, j] + matrix[i, 7 - j]) / 2)
            odd_term = odds[j] * float((matrix[i, j] - matrix[i, 7 - j]) / 2)
            even = even_term if even is None else even + even_term
            odd = odd_term if odd is None else odd + odd_term
        out[i] = even + odd
        out[7 - i] = even - odd if sign > 0 else odd - even
    return out


def lane_index():
    return lax.broadcasted_iota(jnp.int32, (8, LANES), 1)


def sublane_index():
    return lax.broadcasted_iota(jnp.int32, (8, LANES), 0)


def join_vertical(low, high):
    layer = lane_index() % EZ
    new_low = low + jnp.where(layer > 0, pltpu.roll(high, 1, 1), 0.0)
    new_high = high + jnp.where(layer < EZ - 1, pltpu.roll(low, LANES - 1, 1), 0.0)
    return new_low, new_high


def pack_faces(grid, face_x, face_y, field):
    first = lane_index() < HALF
    for b in range(8):
        face_x[pl.ds(64 * field + 8 * b, 8), :] = jnp.where(
            first, grid[row(0, b), :], grid[row(7, b), :]
        )
    for a in range(8):
        face_y[pl.ds(128 * field + 8 * a, 8), :] = grid[row(a, 0), :]
        face_y[pl.ds(128 * field + 64 + 8 * a, 8), :] = grid[row(a, 7), :]


def ghost_x(from_even, from_odd, field, b):
    rows = pl.ds(64 * field + 8 * b, 8)
    odd = lax.axis_index("gx") % 2
    first = (lane_index() < HALF).astype(jnp.int32)
    return jnp.where(first != odd, from_even[rows, :], from_odd[rows, :])


def joined_x(a, low, high, ghost):
    first = lane_index() < HALF
    if a == 0:
        return low + pltpu.roll(jnp.where(first, high, ghost), HALF, 1)
    return high + pltpu.roll(jnp.where(first, ghost, low), HALF, 1)


def assembled(a, b, grid, received, field):
    even_x, odd_x, even_y, odd_y = received
    value = grid[row(a, b), :]
    if a in (0, 7):
        value = joined_x(
            a, grid[row(0, b), :], grid[row(7, b), :], ghost_x(even_x, odd_x, field, b)
        )
    if b in (0, 7):
        rows = pl.ds(64 * field + 8 * a, 8)
        odd = lax.axis_index("yz") % 2 == 1
        pick = odd if b == 0 else jnp.logical_not(odd)
        value = value + jnp.where(pick, even_y[rows, :], odd_y[rows, :])
    return value


def edges_kernel(fields, face_y, even_x, odd_x, to_even, to_odd):
    odd = lax.axis_index("yz") % 2 == 1
    for field in range(fields):
        faces = []
        for side in range(2):
            part = [face_y[pl.ds(128 * field + 64 * side + 8 * a, 8), :] for a in range(8)]
            ghost = ghost_x(even_x, odd_x, field, 7 * side)
            low, high = part[0], part[7]
            part[0] = joined_x(0, low, high, ghost)
            part[7] = joined_x(7, low, high, ghost)
            faces.append(part)
        for a in range(8):
            rows = pl.ds(64 * field + 8 * a, 8)
            to_even[rows, :] = jnp.where(odd, faces[0][a], faces[1][a])
            to_odd[rows, :] = jnp.where(odd, faces[1][a], faces[0][a])


def selection(slots):
    elements = lax.broadcasted_iota(jnp.int32, (LANES, LANES), 0)
    return jnp.where(elements == slots[...], 1.0, 0.0)


def parts_of(values):
    parts = []
    for _ in range(SPLIT):
        parts.append(values.astype(jnp.bfloat16))
        values = values - parts[-1].astype(jnp.float32)
    return parts


def to_grid(chosen, values):
    parts = jnp.concatenate(parts_of(values), 0)
    picked = jnp.dot(
        jnp.concatenate([chosen.astype(jnp.bfloat16)] * SPLIT, 1),
        parts,
        preferred_element_type=jnp.float32,
    )
    return picked.T


def setup_kernel(
    slots, forcing, viscosity, mass_rate, right, diagonal, spread, mass, face_x, face_y,
    order, held, arrived,
):
    ordered = pltpu.make_async_copy(slots, order, arrived.at[3])
    copies = [
        pltpu.make_async_copy(source.at[0, 0], held.at[k], arrived.at[k])
        for k, source in enumerate((viscosity, mass_rate, forcing))
    ]
    for copy in [ordered] + copies:
        copy.start()
    point = sublane_index()
    last_weight = jnp.zeros((8, LANES), jnp.float32)
    for c in range(8):
        last_weight = jnp.where(point == c, float(WEIGHTS[c]), last_weight)
    ordered.wait()
    chosen = selection(order)
    copies[0].wait()
    spread[...] = to_grid(chosen, held[0])
    copies[1].wait()
    mass[...] = to_grid(chosen, held[1])
    for a in range(8):
        for b in range(8):
            weight = last_weight * float(WEIGHTS[a] * WEIGHTS[b])
            spread[row(a, b), :] *= weight
            mass[row(a, b), :] *= weight
    copies[2].wait()
    right[...] = to_grid(chosen, held[2])
    squares = (DERIVATIVE * DERIVATIVE).T
    for b in range(8):
        lines = along(squares, [spread[row(a, b), :] for a in range(8)], 1)
        for a in range(8):
            diagonal[row(a, b), :] = lines[a] + mass[row(a, b), :]
    for a in range(8):
        lines = along(squares, [spread[row(a, b), :] for b in range(8)], 1)
        for b in range(8):
            diagonal[row(a, b), :] += lines[b]
    for a in range(8):
        lines = along(VERTICAL * squares, [spread[across(a, c), :] for c in range(8)], 1)
        lines = [lines[c] + diagonal[across(a, c), :] for c in range(8)]
        lines[0], lines[7] = join_vertical(lines[0], lines[7])
        for c in range(8):
            diagonal[across(a, c), :] = lines[c]
        low, high = join_vertical(right[across(a, 0), :], right[across(a, 7), :])
        right[across(a, 0), :] = low
        right[across(a, 7), :] = high
    pack_faces(right, face_x, face_y, 0)
    pack_faces(diagonal, face_x, face_y, 1)


def operate(values, spread, mass, image, face_x, face_y):
    forward, backward = DERIVATIVE, DERIVATIVE.T
    for b in range(8):
        lines = [values[row(a, b), :] for a in range(8)]
        slopes = along(forward, lines, -1)
        back = along(backward, [slopes[a] * spread[row(a, b), :] for a in range(8)], -1)
        for a in range(8):
            image[row(a, b), :] = back[a] + mass[row(a, b), :] * lines[a]
    for a in range(8):
        slopes = along(forward, [values[row(a, b), :] for b in range(8)], -1)
        back = along(backward, [slopes[b] * spread[row(a, b), :] for b in range(8)], -1)
        for b in range(8):
            image[row(a, b), :] += back[b]
    energy = jnp.zeros((8, LANES), jnp.float32)
    for a in range(8):
        lines = [values[across(a, c), :] for c in range(8)]
        slopes = along(forward, lines, -1)
        back = along(
            VERTICAL * backward, [slopes[c] * spread[across(a, c), :] for c in range(8)], -1
        )
        back = [back[c] + image[across(a, c), :] for c in range(8)]
        for c in range(8):
            energy = energy + back[c] * lines[c]
        back[0], back[7] = join_vertical(back[0], back[7])
        for c in range(8):
            image[across(a, c), :] = back[c]
    pack_faces(image, face_x, face_y, 0)
    return energy


def weighted(sums):
    layer, point = lane_index() % EZ, sublane_index()
    below = jnp.logical_and(point == 0, layer > 0)
    above = jnp.logical_and(point == 7, layer < EZ - 1)
    shared = jnp.where(jnp.logical_or(below, above), 0.5, 1.0)
    return (sums[0] + 0.5 * sums[1] + 0.25 * sums[2]) * shared


def ends(a, b):
    return int(a in (0, 7)) + int(b in (0, 7))


def first_kernel(
    right, diagonal, even_x, odd_x, even_y, odd_y, spread, mass,
    whole_diagonal, values, image, face_x, face_y, moments,
):
    received = (even_x, odd_x, even_y, odd_y)
    sums = [jnp.zeros((8, LANES), jnp.float32)] * 3
    for a in range(8):
        for b in range(8):
            source = assembled(a, b, right, received, 0)
            scale = assembled(a, b, diagonal, received, 1)
            value = source / scale
            whole_diagonal[row(a, b), :] = scale
            values[row(a, b), :] = value
            sums[ends(a, b)] = sums[ends(a, b)] + source * value
    moments[...] = weighted(sums)
    operate(values, spread, mass, image, face_x, face_y)


def next_values(before_image, received, diagonal, before, values):
    cross = [jnp.zeros((8, LANES), jnp.float32)] * 3
    square = [jnp.zeros((8, LANES), jnp.float32)] * 3
    for a in range(8):
        for b in range(8):
            scale = diagonal[row(a, b), :]
            old = before[row(a, b), :]
            value = assembled(a, b, before_image, received, 0) / scale - old
            values[row(a, b), :] = value
            scaled = scale * value
            kind = ends(a, b)
            cross[kind] = cross[kind] + scaled * old
            square[kind] = square[kind] + scaled * value
    return weighted(cross), weighted(square)


def second_kernel(
    before_image, even_x, odd_x, even_y, odd_y, diagonal, before, spread, mass,
    values, image, face_x, face_y, moments,
):
    received = (even_x, odd_x, even_y, odd_y)
    cross, square = next_values(before_image, received, diagonal, before, values)
    moments[pl.ds(0, 8), :] = cross
    moments[pl.ds(8, 8), :] = square
    operate(values, spread, mass, image, face_x, face_y)


def third_kernel(
    before_image, even_x, odd_x, even_y, odd_y, diagonal, before, spread, mass, moments0, moments1,
    values, image, face_x, face_y, sums,
):
    received = (even_x, odd_x, even_y, odd_y)
    cross, square = next_values(before_image, received, diagonal, before, values)
    energy = operate(values, spread, mass, image, face_x, face_y)
    parts = [
        moments0[...], moments1[pl.ds(0, 8), :], moments1[pl.ds(8, 8), :], cross, square, energy
    ]
    lane = lax.broadcasted_iota(jnp.int32, (1, LANES), 1)
    line = jnp.zeros((1, LANES), jnp.float32)
    for k, part in enumerate(parts):
        total = jnp.sum(jnp.sum(part, 0, keepdims=True), 1, keepdims=True)
        line = jnp.where(lane == k, total, line)
    sums[...] = jnp.broadcast_to(line[None], sums.shape)


def recurrence(moments):
    moments = moments[:5] + [moments[5] - moments[4]]
    zero = jnp.zeros_like(moments[0])
    one = zero + 1.0

    def form(left, right, shift):
        total = zero
        for i in range(3):
            for j in range(3):
                if left[i] is not None and right[j] is not None:
                    entry = moments[i + j]
                    if shift:
                        entry = entry + moments[i + j + 1]
                    total = total + left[i] * right[j] * entry
        return total

    def ratio(top, bottom):
        fine = jnp.logical_and(bottom > 0.0, top > 0.0)
        return jnp.where(fine, top / jnp.where(fine, bottom, 1.0), 0.0)

    def add(left, scale, right):
        out = []
        for x, y in zip(left, right):
            if y is None:
                out.append(x)
            else:
                out.append(scale * y if x is None else x + scale * y)
        return out

    direction = [one, None, None, None]
    precond = [one, None, None, None]
    result = [None, None, None, None]
    norm = moments[0]
    for step in range(3):
        curve = form(direction, direction, True)
        length = ratio(norm, curve)
        result = add(result, length, direction)
        moved = add(direction, 1.0, [None] + direction[:3])
        if step == 0:
            precond = [jnp.where(curve > 0.0, moments[1] / curve, 1.0), -length, None, None]
        else:
            precond = add(precond, -length, moved)
        if step < 2:
            norm_next = form(precond, precond, False)
            direction = add(precond, ratio(norm_next, norm), direction)
            norm = norm_next
    return result[:3], precond


def last_kernel(
    before_image, even_x, odd_x, even_y, odd_y, diagonal, values0, values1, values2, sums, slots,
    solution, residual, solution_grid, residual_grid,
):
    received = (even_x, odd_x, even_y, odd_y)
    line = jnp.sum(sums[...], 0)
    lane = lax.broadcasted_iota(jnp.int32, (1, LANES), 1)
    moments = [
        jnp.sum(jnp.where(lane == k, line, 0.0), 1, keepdims=True) for k in range(6)
    ]
    result, precond = recurrence(moments)
    spread_out = lambda scalar: jnp.broadcast_to(scalar, (8, LANES))
    result = [spread_out(entry) for entry in result]
    precond = [spread_out(entry) for entry in precond]
    for a in range(8):
        for b in range(8):
            rows = row(a, b)
            basis = [values0[rows, :], values1[rows, :], values2[rows, :]]
            scale = diagonal[rows, :]
            image = assembled(a, b, before_image, received, 0) - scale * basis[2]
            near = result[0] * basis[0] + result[1] * basis[1] + result[2] * basis[2]
            far = precond[0] * basis[0] + precond[1] * basis[1] + precond[2] * basis[2]
            solution_grid[rows, :] = near
            residual_grid[rows, :] = scale * far + precond[3] * image
    chosen = selection(slots).T.astype(jnp.bfloat16)
    for grid, out in ((solution_grid, solution), (residual_grid, residual)):
        total = None
        for part in parts_of(grid[...]):
            term = lax.dot_general(
                chosen, part, (((1,), (1,)), ((), ())), preferred_element_type=jnp.float32
            )
            total = term if total is None else total + term
        out[0, 0] = total


def call(kernel, name, shapes, scratch, *operands, outside=0):
    places = [pltpu.HBM] * outside + [pltpu.VMEM] * (len(operands) - outside)
    operands = [
        pltpu.with_memory_space_constraint(operand, place) if place == pltpu.HBM else operand
        for operand, place in zip(operands, places)
    ]
    return pl.pallas_call(
        kernel,
        out_shape=[jax.ShapeDtypeStruct(shape, jnp.float32) for shape in shapes],
        in_specs=[pl.BlockSpec(memory_space=place) for place in places],
        out_specs=[pl.BlockSpec(memory_space=pltpu.VMEM)] * len(shapes),
        scratch_shapes=scratch,
        compiler_params=pltpu.CompilerParams(vmem_limit_bytes=VMEM_BYTES),
        name=name,
    )(*operands)


def swapped(block, axis):
    extent = lax.axis_size(axis)
    even = [(i, i ^ 1) for i in range(extent)]
    odd = [(i, (((i + 1) ^ 1) - 1) % extent) for i in range(extent)]
    return lax.ppermute(block[0], axis, even), lax.ppermute(block[1], axis, odd)


def exchange(fields, face_x, face_y):
    received_x = swapped((face_x, face_x), "gx")
    shape = (64 * fields, LANES)
    sent_y = call(
        functools.partial(edges_kernel, fields), "edges", [shape, shape], [], face_y, *received_x
    )
    return (*received_x, *swapped(sent_y, "yz"))


def body(forcing, viscosity, mass_rate, slot_element):
    devices = lax.axis_size("gx") * lax.axis_size("yz")
    slots = slot_element[0]
    grid = (POINTS, LANES)
    face_x, face_y, moment = (64, LANES), (128, LANES), (8, LANES)
    right, diagonal, spread, mass, out_x, out_y = call(
        setup_kernel, "setup", [grid] * 4 + [(128, LANES), (256, LANES)],
        [
            pltpu.VMEM((1, LANES), jnp.int32),
            pltpu.VMEM((3, LANES, POINTS), jnp.float32),
            pltpu.SemaphoreType.DMA((4,)),
        ],
        slots, forcing, viscosity, mass_rate, outside=4,
    )
    received = exchange(2, out_x, out_y)
    diagonal, values0, image, out_x, out_y, moments0 = call(
        first_kernel, "first", [grid] * 3 + [face_x, face_y, moment], [],
        right, diagonal, *received, spread, mass,
    )
    received = exchange(1, out_x, out_y)
    values1, image, out_x, out_y, moments1 = call(
        second_kernel, "second", [grid] * 2 + [face_x, face_y, (16, LANES)], [],
        image, *received, diagonal, values0, spread, mass,
    )
    received = exchange(1, out_x, out_y)
    values2, image, out_x, out_y, sums = call(
        third_kernel, "third", [grid] * 2 + [face_x, face_y, (devices, 1, LANES)], [],
        image, *received, diagonal, values1, spread, mass, moments0, moments1,
    )
    sums = lax.all_to_all(sums, ("gx", "yz"), 0, 0)
    received = exchange(1, out_x, out_y)
    return call(
        last_kernel, "last", [forcing.shape] * 2, [pltpu.VMEM(grid, jnp.float32)] * 2,
        image, *received, diagonal, values0, values1, values2, sums, slots,
    )


def solution(mesh):
    placed = (
        P("gx", "yz", None, None),
        P("gx", "yz", None, None),
        P("gx", "yz", None, None),
        P("gx", "yz", None),
    )
    return jax.shard_map(
        body,
        mesh=mesh,
        in_specs=placed,
        out_specs=(P("gx", "yz", None, None), P("gx", "yz", None, None)),
        check_vma=False,
    )
```

```python
import jax
import jax.numpy as jnp
import numpy as np
from jax import lax
from jax.experimental import pallas as pl
from jax.experimental.pallas import tpu as pltpu
from jax.sharding import PartitionSpec as P

EZ = 64
LANES = 128
HALF = 64
POINTS = 512
SPLIT = 2
VERTICAL = 4.0
VMEM_BYTES = 24 * 1024 * 1024


def legendre_rows(nodes, degree):
    rows = [nodes * 0.0 + 1.0, nodes]
    for order in range(2, degree + 1):
        rows.append(((2 * order - 1) * nodes * rows[-1] - (order - 1) * rows[-2]) / order)
    return np.stack(rows, 1)


def spectral_tables():
    degree = 7
    nodes = np.cos(np.pi * np.arange(degree + 1) / degree)
    for sweep in range(60):
        legendre = legendre_rows(nodes, degree)
        nodes = nodes - (nodes * legendre[:, degree] - legendre[:, degree - 1]) / (
            (degree + 1) * legendre[:, degree]
        )
    nodes = nodes[::-1].copy()
    top_values = legendre_rows(nodes, degree)[:, degree]
    weights = 2.0 / (degree * (degree + 1) * top_values**2)
    identity = np.eye(degree + 1)
    spacing = nodes[:, None] - nodes[None, :] + identity
    derivative = top_values[:, None] / top_values[None, :] / spacing * (1.0 - identity)
    corner_fix = np.zeros(degree + 1)
    corner_fix[0] = -degree * (degree + 1) / 4.0
    corner_fix[degree] = degree * (degree + 1) / 4.0
    derivative = derivative + identity * corner_fix[None, :]
    return (derivative, weights)


DERIVATIVE, WEIGHTS = spectral_tables()


def row(a, b):
    return pl.ds(64 * a + 8 * b, 8)


def across(a, c):
    return pl.ds(64 * a + c, 8, stride=8)


def along(matrix, lines, sign):
    evens = [lines[j] + lines[7 - j] for j in range(4)]
    odds = [lines[j] - lines[7 - j] for j in range(4)]
    out = [None] * 8
    for i in range(4):
        even = odd = None
        for j in range(4):
            even_term = evens[j] * float((matrix[i, j] + matrix[i, 7 - j]) / 2)
            odd_term = odds[j] * float((matrix[i, j] - matrix[i, 7 - j]) / 2)
            even = even_term if even is None else even + even_term
            odd = odd_term if odd is None else odd + odd_term
        out[i] = even + odd
        out[7 - i] = even - odd if sign > 0 else odd - even
    return out


def lane_index():
    return lax.broadcasted_iota(jnp.int32, (8, LANES), 1)


def sublane_index():
    return lax.broadcasted_iota(jnp.int32, (8, LANES), 0)


def join_vertical(low, high):
    layer = lane_index() % EZ
    new_low = low + jnp.where(layer > 0, pltpu.roll(high, 1, 1), 0.0)
    new_high = high + jnp.where(layer < EZ - 1, pltpu.roll(low, LANES - 1, 1), 0.0)
    return new_low, new_high


def packed_x(grid, b):
    return jnp.where(lane_index() < HALF, grid[row(0, b), :], grid[row(7, b), :])


def pack_faces(grid, face_x, face_y, field):
    for b in range(8):
        face_x[pl.ds(64 * field + 8 * b, 8), :] = packed_x(grid, b)
    for a in range(8):
        face_y[pl.ds(128 * field + 8 * a, 8), :] = grid[row(a, 0), :]
        face_y[pl.ds(128 * field + 64 + 8 * a, 8), :] = grid[row(a, 7), :]


def lowest_to_highest(low_side, to_even, to_odd, rows, low, high):
    to_even[rows, :] = jnp.where(low_side, low, high)
    to_odd[rows, :] = jnp.where(low_side, high, low)


def is_odd(axis):
    return lax.axis_index(axis) % 2 == 1


def ghost_x(from_even, from_odd, field, b):
    rows = pl.ds(64 * field + 8 * b, 8)
    odd = lax.axis_index("gx") % 2
    first = (lane_index() < HALF).astype(jnp.int32)
    return jnp.where(first != odd, from_even[rows, :], from_odd[rows, :])


def joined_x(a, low, high, ghost):
    first = lane_index() < HALF
    if a == 0:
        return low + pltpu.roll(jnp.where(first, high, ghost), HALF, 1)
    return high + pltpu.roll(jnp.where(first, ghost, low), HALF, 1)


def from_y(even_y, odd_y, b, rows):
    odd = is_odd("yz")
    pick = odd if b == 0 else jnp.logical_not(odd)
    return jnp.where(pick, even_y[rows, :], odd_y[rows, :])


def assembled(a, b, grid, received, field):
    even_x, odd_x, even_y, odd_y = received
    value = grid[row(a, b), :]
    if a in (0, 7):
        value = joined_x(
            a, grid[row(0, b), :], grid[row(7, b), :], ghost_x(even_x, odd_x, field, b)
        )
    if b in (0, 7):
        rows = pl.ds(64 * field + 8 * a, 8)
        value = value + from_y(even_y, odd_y, b, rows)
    return value


def edges_kernel(face_y, fixed_y, even_x, odd_x, to_even, to_odd):
    odd = is_odd("yz")
    for field in range(2):
        faces = []
        for side in range(2):
            part = [face_y[pl.ds(128 * field + 64 * side + 8 * a, 8), :] for a in range(8)]
            ghost = ghost_x(even_x, odd_x, field, 7 * side)
            low, high = part[0], part[7]
            part[0] = joined_x(0, low, high, ghost)
            part[7] = joined_x(7, low, high, ghost)
            faces.append(part)
        for a in range(8):
            rows = pl.ds(64 * field + 8 * a, 8)
            lowest_to_highest(odd, to_even, to_odd, rows, faces[0][a], faces[1][a])
    for k in range(9):
        rows = pl.ds(128 + 8 * k, 8)
        low, high = fixed_y[pl.ds(8 * k, 8), :], fixed_y[pl.ds(72 + 8 * k, 8), :]
        lowest_to_highest(odd, to_even, to_odd, rows, low, high)


def selection(slots):
    elements = lax.broadcasted_iota(jnp.int32, (LANES, LANES), 0)
    return jnp.where(elements == slots[...], 1.0, 0.0)


def parts_of(values):
    parts = []
    for _ in range(SPLIT):
        parts.append(values.astype(jnp.bfloat16))
        values = values - parts[-1].astype(jnp.float32)
    return parts


def to_grid(chosen, values):
    parts = jnp.concatenate(parts_of(values), 0)
    picked = jnp.dot(
        jnp.concatenate([chosen.astype(jnp.bfloat16)] * SPLIT, 1),
        parts,
        preferred_element_type=jnp.float32,
    )
    return picked.T


def setup_kernel(
    slots, forcing, viscosity, mass_rate,
    right, diagonal, spread, mass, face_x, face_y, fixed_y, shifts, order, held, arrived,
):
    ordered = pltpu.make_async_copy(slots, order, arrived.at[3])
    copies = [
        pltpu.make_async_copy(source.at[0, 0], held.at[k], arrived.at[k])
        for k, source in enumerate((viscosity, mass_rate, forcing))
    ]
    for copy in [ordered] + copies:
        copy.start()
    point = sublane_index()
    last_weight = jnp.zeros((8, LANES), jnp.float32)
    for c in range(8):
        last_weight = jnp.where(point == c, float(WEIGHTS[c]), last_weight)
    ordered.wait()
    chosen = selection(order)
    copies[0].wait()
    spread[...] = to_grid(chosen, held[0])
    copies[1].wait()
    mass[...] = to_grid(chosen, held[1])
    for a in range(8):
        for b in range(8):
            weight = last_weight * float(WEIGHTS[a] * WEIGHTS[b])
            spread[row(a, b), :] *= weight
            mass[row(a, b), :] *= weight
    copies[2].wait()
    right[...] = to_grid(chosen, held[2])
    squares = (DERIVATIVE * DERIVATIVE).T
    for b in range(8):
        lines = along(squares, [spread[row(a, b), :] for a in range(8)], 1)
        for a in range(8):
            diagonal[row(a, b), :] = lines[a] + mass[row(a, b), :]
    for a in range(8):
        lines = along(squares, [spread[row(a, b), :] for b in range(8)], 1)
        for b in range(8):
            diagonal[row(a, b), :] += lines[b]
    for a in range(8):
        lines = along(VERTICAL * squares, [spread[across(a, c), :] for c in range(8)], 1)
        lines = [lines[c] + diagonal[across(a, c), :] for c in range(8)]
        lines[0], lines[7] = join_vertical(lines[0], lines[7])
        for c in range(8):
            diagonal[across(a, c), :] = lines[c]
        low, high = join_vertical(right[across(a, 0), :], right[across(a, 7), :])
        right[across(a, 0), :] = low
        right[across(a, 7), :] = high
    pack_faces(right, face_x, face_y, 0)
    pack_faces(diagonal, face_x, face_y, 1)
    for b in range(8):
        face_x[pl.ds(128 + 8 * b, 8), :] = packed_x(spread, b)
    for side in range(2):
        for a in range(8):
            fixed_y[pl.ds(72 * side + 8 * a, 8), :] = spread[row(a, 7 * side), :]
        fixed_y[pl.ds(72 * side + 64, 8), :] = packed_x(mass, 7 * side)
    for k in range(8):
        along_shift = back_shift = jnp.zeros((8, LANES), jnp.float32)
        for c in range(8):
            other = (c + k) % 8
            along_shift = jnp.where(point == c, float(DERIVATIVE[c, other]), along_shift)
            back_shift = jnp.where(
                point == c, float(VERTICAL * DERIVATIVE[other, c]), back_shift
            )
        shifts[pl.ds(8 * k, 8), :] = along_shift
        shifts[pl.ds(64 + 8 * k, 8), :] = back_shift


def join_vertical_packed(value):
    layer, point = lane_index() % EZ, sublane_index()
    from_below = pltpu.roll(pltpu.roll(value, 1, 0), 1, 1)
    from_above = pltpu.roll(pltpu.roll(value, 7, 0), LANES - 1, 1)
    below = jnp.logical_and(point == 0, layer > 0)
    above = jnp.logical_and(point == 7, layer < EZ - 1)
    return value + jnp.where(below, from_below, jnp.where(above, from_above, 0.0))


def shifted_sum(shifts, start, value):
    total = shifts[pl.ds(start, 8), :] * value
    for k in range(1, 8):
        total = total + shifts[pl.ds(start + 8 * k, 8), :] * pltpu.roll(value, 8 - k, 0)
    return total


def end_row(lines, end):
    total = None
    for q in range(8):
        term = lines[q] * float(DERIVATIVE[q, end])
        total = term if total is None else total + term
    return total


def corner_shares(values, outer, shifts):
    first = lane_index() < HALF
    lines = [packed_x(values, b) for b in range(8)]
    slopes = along(DERIVATIVE, lines, -1)
    slopes = [slopes[q] * outer[pl.ds(8 * q, 8), :] for q in range(8)]
    for_y = [end_row(slopes, 0), end_row(slopes, 7)]
    for_x = []
    for side in range(2):
        base = 64 + 72 * side
        spread = [outer[pl.ds(base + 8 * a, 8), :] for a in range(8)]
        slopes = along(DERIVATIVE, [values[row(a, 7 * side), :] for a in range(8)], -1)
        slopes = [slopes[q] * spread[q] for q in range(8)]
        share = jnp.where(first, end_row(slopes, 0), end_row(slopes, 7))
        corner = lines[7 * side]
        slope = shifted_sum(shifts, 0, corner) * jnp.where(first, spread[0], spread[7])
        share = share + shifted_sum(shifts, 64, slope) + outer[pl.ds(base + 64, 8), :] * corner
        for_x.append(share)
    return [join_vertical_packed(share) for share in for_x], [
        join_vertical_packed(share) for share in for_y
    ]


def send_faces(image, values, outer, shifts, face_x, to_even, to_odd):
    for_x, for_y = corner_shares(values, outer, shifts)
    first = lane_index() < HALF
    odd = is_odd("yz")
    for b in range(8):
        face = packed_x(image, b)
        if b in (0, 7):
            face = face + for_x[b // 7]
        face_x[pl.ds(8 * b, 8), :] = face
    faces = []
    for side in range(2):
        part = [image[row(a, 7 * side), :] for a in range(8)]
        low, high = part[0], part[7]
        part[0] = low + jnp.where(first, for_y[side], pltpu.roll(high, HALF, 1))
        part[7] = high + jnp.where(first, pltpu.roll(low, HALF, 1), for_y[side])
        faces.append(part)
    for a in range(8):
        lowest_to_highest(odd, to_even, to_odd, pl.ds(8 * a, 8), faces[0][a], faces[1][a])


def operate(values, spread, mass, image):
    forward, backward = DERIVATIVE, DERIVATIVE.T
    for b in range(8):
        lines = [values[row(a, b), :] for a in range(8)]
        slopes = along(forward, lines, -1)
        back = along(backward, [slopes[a] * spread[row(a, b), :] for a in range(8)], -1)
        for a in range(8):
            image[row(a, b), :] = back[a] + mass[row(a, b), :] * lines[a]
    for a in range(8):
        slopes = along(forward, [values[row(a, b), :] for b in range(8)], -1)
        back = along(backward, [slopes[b] * spread[row(a, b), :] for b in range(8)], -1)
        for b in range(8):
            image[row(a, b), :] += back[b]
    energy = jnp.zeros((8, LANES), jnp.float32)
    for a in range(8):
        lines = [values[across(a, c), :] for c in range(8)]
        slopes = along(forward, lines, -1)
        back = along(
            VERTICAL * backward, [slopes[c] * spread[across(a, c), :] for c in range(8)], -1
        )
        back = [back[c] + image[across(a, c), :] for c in range(8)]
        for c in range(8):
            energy = energy + back[c] * lines[c]
        back[0], back[7] = join_vertical(back[0], back[7])
        for c in range(8):
            image[across(a, c), :] = back[c]
    return energy


def weighted(sums):
    layer, point = lane_index() % EZ, sublane_index()
    below = jnp.logical_and(point == 0, layer > 0)
    above = jnp.logical_and(point == 7, layer < EZ - 1)
    shared = jnp.where(jnp.logical_or(below, above), 0.5, 1.0)
    return (sums[0] + 0.5 * sums[1] + 0.25 * sums[2]) * shared


def ends(a, b):
    return int(a in (0, 7)) + int(b in (0, 7))


def first_kernel(
    right, diagonal, even_x, odd_x, even_y, odd_y, spread, mass, shifts,
    whole_diagonal, values, image, outer, face_x, to_even, to_odd, moments,
):
    received = (even_x, odd_x, even_y, odd_y)
    sums = [jnp.zeros((8, LANES), jnp.float32)] * 3
    for a in range(8):
        for b in range(8):
            source = assembled(a, b, right, received, 0)
            scale = assembled(a, b, diagonal, received, 1)
            value = source / scale
            whole_diagonal[row(a, b), :] = scale
            values[row(a, b), :] = value
            sums[ends(a, b)] = sums[ends(a, b)] + source * value
    moments[...] = weighted(sums)
    for b in range(8):
        outer[pl.ds(8 * b, 8), :] = pltpu.roll(ghost_x(even_x, odd_x, 2, b), HALF, 1)
    for side in range(2):
        for k in range(9):
            outer[pl.ds(64 + 72 * side + 8 * k, 8), :] = from_y(
                even_y, odd_y, 7 * side, pl.ds(128 + 8 * k, 8)
            )
    operate(values, spread, mass, image)
    send_faces(image, values, outer, shifts, face_x, to_even, to_odd)


def next_values(before_image, received, diagonal, before, values):
    cross = [jnp.zeros((8, LANES), jnp.float32)] * 3
    square = [jnp.zeros((8, LANES), jnp.float32)] * 3
    for a in range(8):
        for b in range(8):
            scale = diagonal[row(a, b), :]
            old = before[row(a, b), :]
            value = assembled(a, b, before_image, received, 0) / scale - old
            values[row(a, b), :] = value
            scaled = scale * value
            kind = ends(a, b)
            cross[kind] = cross[kind] + scaled * old
            square[kind] = square[kind] + scaled * value
    return weighted(cross), weighted(square)


def second_kernel(
    before_image, even_x, odd_x, even_y, odd_y, diagonal, before, spread, mass, shifts, outer,
    values, image, face_x, to_even, to_odd, moments,
):
    received = (even_x, odd_x, even_y, odd_y)
    cross, square = next_values(before_image, received, diagonal, before, values)
    moments[pl.ds(0, 8), :] = cross
    moments[pl.ds(8, 8), :] = square
    operate(values, spread, mass, image)
    send_faces(image, values, outer, shifts, face_x, to_even, to_odd)


def third_kernel(
    before_image, even_x, odd_x, even_y, odd_y, diagonal, before, spread, mass, shifts, outer,
    moments0, moments1, values, image, face_x, to_even, to_odd, sums,
):
    received = (even_x, odd_x, even_y, odd_y)
    cross, square = next_values(before_image, received, diagonal, before, values)
    energy = operate(values, spread, mass, image)
    send_faces(image, values, outer, shifts, face_x, to_even, to_odd)
    parts = [
        moments0[...], moments1[pl.ds(0, 8), :], moments1[pl.ds(8, 8), :], cross, square, energy
    ]
    lane = lax.broadcasted_iota(jnp.int32, (1, LANES), 1)
    line = jnp.zeros((1, LANES), jnp.float32)
    for k, part in enumerate(parts):
        total = jnp.sum(jnp.sum(part, 0, keepdims=True), 1, keepdims=True)
        line = jnp.where(lane == k, total, line)
    sums[...] = jnp.broadcast_to(line[None], sums.shape)


def recurrence(moments):
    moments = moments[:5] + [moments[5] - moments[4]]
    zero = jnp.zeros_like(moments[0])
    one = zero + 1.0

    def form(left, right, shift):
        total = zero
        for i in range(3):
            for j in range(3):
                if left[i] is not None and right[j] is not None:
                    entry = moments[i + j]
                    if shift:
                        entry = entry + moments[i + j + 1]
                    total = total + left[i] * right[j] * entry
        return total

    def ratio(top, bottom):
        fine = jnp.logical_and(bottom > 0.0, top > 0.0)
        return jnp.where(fine, top / jnp.where(fine, bottom, 1.0), 0.0)

    def add(left, scale, right):
        out = []
        for x, y in zip(left, right):
            if y is None:
                out.append(x)
            else:
                out.append(scale * y if x is None else x + scale * y)
        return out

    direction = [one, None, None, None]
    precond = [one, None, None, None]
    result = [None, None, None, None]
    norm = moments[0]
    for step in range(3):
        curve = form(direction, direction, True)
        length = ratio(norm, curve)
        result = add(result, length, direction)
        moved = add(direction, 1.0, [None] + direction[:3])
        if step == 0:
            precond = [jnp.where(curve > 0.0, moments[1] / curve, 1.0), -length, None, None]
        else:
            precond = add(precond, -length, moved)
        if step < 2:
            norm_next = form(precond, precond, False)
            direction = add(precond, ratio(norm_next, norm), direction)
            norm = norm_next
    return result[:3], precond


def last_kernel(
    before_image, even_x, odd_x, even_y, odd_y, diagonal, values0, values1, values2, sums, slots,
    solution, residual, solution_grid, residual_grid,
):
    received = (even_x, odd_x, even_y, odd_y)
    line = jnp.sum(sums[...], 0)
    lane = lax.broadcasted_iota(jnp.int32, (1, LANES), 1)
    moments = [
        jnp.sum(jnp.where(lane == k, line, 0.0), 1, keepdims=True) for k in range(6)
    ]
    result, precond = recurrence(moments)
    spread_out = lambda scalar: jnp.broadcast_to(scalar, (8, LANES))
    result = [spread_out(entry) for entry in result]
    precond = [spread_out(entry) for entry in precond]
    for a in range(8):
        for b in range(8):
            rows = row(a, b)
            basis = [values0[rows, :], values1[rows, :], values2[rows, :]]
            scale = diagonal[rows, :]
            image = assembled(a, b, before_image, received, 0) - scale * basis[2]
            near = result[0] * basis[0] + result[1] * basis[1] + result[2] * basis[2]
            far = precond[0] * basis[0] + precond[1] * basis[1] + precond[2] * basis[2]
            solution_grid[rows, :] = near
            residual_grid[rows, :] = scale * far + precond[3] * image
    chosen = selection(slots).T.astype(jnp.bfloat16)
    for grid, out in ((solution_grid, solution), (residual_grid, residual)):
        total = None
        for part in parts_of(grid[...]):
            term = lax.dot_general(
                chosen, part, (((1,), (1,)), ((), ())), preferred_element_type=jnp.float32
            )
            total = term if total is None else total + term
        out[0, 0] = total


def call(kernel, name, shapes, scratch, *operands, outside=0):
    places = [pltpu.HBM] * outside + [pltpu.VMEM] * (len(operands) - outside)
    operands = [
        pltpu.with_memory_space_constraint(operand, place) if place == pltpu.HBM else operand
        for operand, place in zip(operands, places)
    ]
    return pl.pallas_call(
        kernel,
        out_shape=[jax.ShapeDtypeStruct(shape, jnp.float32) for shape in shapes],
        in_specs=[pl.BlockSpec(memory_space=place) for place in places],
        out_specs=[pl.BlockSpec(memory_space=pltpu.VMEM)] * len(shapes),
        scratch_shapes=scratch,
        compiler_params=pltpu.CompilerParams(vmem_limit_bytes=VMEM_BYTES),
        name=name,
    )(*operands)


def swapped(block, axis):
    extent = lax.axis_size(axis)
    even = [(i, i ^ 1) for i in range(extent)]
    odd = [(i, (((i + 1) ^ 1) - 1) % extent) for i in range(extent)]
    return lax.ppermute(block[0], axis, even), lax.ppermute(block[1], axis, odd)


def body(forcing, viscosity, mass_rate, slot_element):
    devices = lax.axis_size("gx") * lax.axis_size("yz")
    slots = slot_element[0]
    grid, face, tile = (POINTS, LANES), (64, LANES), (8, LANES)
    right, diagonal, spread, mass, out_x, out_y, fixed_y, shifts = call(
        setup_kernel, "setup",
        [grid] * 4 + [(192, LANES), (256, LANES), (144, LANES), (128, LANES)],
        [
            pltpu.VMEM((1, LANES), jnp.int32),
            pltpu.VMEM((3, LANES, POINTS), jnp.float32),
            pltpu.SemaphoreType.DMA((4,)),
        ],
        slots, forcing, viscosity, mass_rate, outside=4,
    )
    received_x = swapped((out_x, out_x), "gx")
    sent_y = call(
        edges_kernel, "edges", [(200, LANES)] * 2, [], out_y, fixed_y, *received_x
    )
    received_y = swapped(sent_y, "yz")
    diagonal, values0, image, outer, out_x, *sent_y, moments0 = call(
        first_kernel, "first", [grid] * 3 + [(208, LANES)] + [face] * 3 + [tile], [],
        right, diagonal, *received_x, *received_y, spread, mass, shifts,
    )
    received = (*swapped((out_x, out_x), "gx"), *swapped(sent_y, "yz"))
    values1, image, out_x, *sent_y, moments1 = call(
        second_kernel, "second", [grid] * 2 + [face] * 3 + [(16, LANES)], [],
        image, *received, diagonal, values0, spread, mass, shifts, outer,
    )
    received = (*swapped((out_x, out_x), "gx"), *swapped(sent_y, "yz"))
    values2, image, out_x, *sent_y, sums = call(
        third_kernel, "third", [grid] * 2 + [face] * 3 + [(devices, 1, LANES)], [],
        image, *received, diagonal, values1, spread, mass, shifts, outer, moments0, moments1,
    )
    sums = lax.all_to_all(sums, ("gx", "yz"), 0, 0)
    received = (*swapped((out_x, out_x), "gx"), *swapped(sent_y, "yz"))
    return call(
        last_kernel, "last", [forcing.shape] * 2, [pltpu.VMEM(grid, jnp.float32)] * 2,
        image, *received, diagonal, values0, values1, values2, sums, slots,
    )


def solution(mesh):
    placed = (
        P("gx", "yz", None, None),
        P("gx", "yz", None, None),
        P("gx", "yz", None, None),
        P("gx", "yz", None),
    )
    return jax.shard_map(
        body,
        mesh=mesh,
        in_specs=placed,
        out_specs=(P("gx", "yz", None, None), P("gx", "yz", None, None)),
        check_vma=False,
    )
```

```python
import jax
import jax.numpy as jnp
import numpy as np
from jax import lax
from jax.experimental import pallas as pl
from jax.experimental.pallas import tpu as pltpu
from jax.sharding import PartitionSpec as P

EZ = 64
LANES = 128
HALF = 64
POINTS = 512
SPLIT = 2
VERTICAL = 4.0
VMEM_BYTES = 24 * 1024 * 1024


def legendre_rows(nodes, degree):
    rows = [nodes * 0.0 + 1.0, nodes]
    for order in range(2, degree + 1):
        rows.append(((2 * order - 1) * nodes * rows[-1] - (order - 1) * rows[-2]) / order)
    return np.stack(rows, 1)


def spectral_tables():
    degree = 7
    nodes = np.cos(np.pi * np.arange(degree + 1) / degree)
    for sweep in range(60):
        legendre = legendre_rows(nodes, degree)
        nodes = nodes - (nodes * legendre[:, degree] - legendre[:, degree - 1]) / (
            (degree + 1) * legendre[:, degree]
        )
    nodes = nodes[::-1].copy()
    top_values = legendre_rows(nodes, degree)[:, degree]
    weights = 2.0 / (degree * (degree + 1) * top_values**2)
    identity = np.eye(degree + 1)
    spacing = nodes[:, None] - nodes[None, :] + identity
    derivative = top_values[:, None] / top_values[None, :] / spacing * (1.0 - identity)
    corner_fix = np.zeros(degree + 1)
    corner_fix[0] = -degree * (degree + 1) / 4.0
    corner_fix[degree] = degree * (degree + 1) / 4.0
    derivative = derivative + identity * corner_fix[None, :]
    return (derivative, weights)


DERIVATIVE, WEIGHTS = spectral_tables()


def row(a, b):
    return pl.ds(64 * a + 8 * b, 8)


def across(a, c):
    return pl.ds(64 * a + c, 8, stride=8)


def along(matrix, lines, sign):
    evens = [lines[j] + lines[7 - j] for j in range(4)]
    odds = [lines[j] - lines[7 - j] for j in range(4)]
    out = [None] * 8
    for i in range(4):
        even = odd = None
        for j in range(4):
            even_term = evens[j] * float((matrix[i, j] + matrix[i, 7 - j]) / 2)
            odd_term = odds[j] * float((matrix[i, j] - matrix[i, 7 - j]) / 2)
            even = even_term if even is None else even + even_term
            odd = odd_term if odd is None else odd + odd_term
        out[i] = even + odd
        out[7 - i] = even - odd if sign > 0 else odd - even
    return out


def lane_index():
    return lax.broadcasted_iota(jnp.int32, (8, LANES), 1)


def sublane_index():
    return lax.broadcasted_iota(jnp.int32, (8, LANES), 0)


def join_vertical(low, high):
    layer = lane_index() % EZ
    new_low = low + jnp.where(layer > 0, pltpu.roll(high, 1, 1), 0.0)
    new_high = high + jnp.where(layer < EZ - 1, pltpu.roll(low, LANES - 1, 1), 0.0)
    return new_low, new_high


def packed_x(grid, b):
    return jnp.where(lane_index() < HALF, grid[row(0, b), :], grid[row(7, b), :])


def lowest_to_highest(low_side, to_even, to_odd, rows, low, high):
    to_even[rows, :] = jnp.where(low_side, low, high)
    to_odd[rows, :] = jnp.where(low_side, high, low)


def is_odd(axis):
    return lax.axis_index(axis) % 2 == 1


def ghost_x(from_even, from_odd, rows):
    odd = lax.axis_index("gx") % 2
    first = (lane_index() < HALF).astype(jnp.int32)
    return jnp.where(first != odd, from_even[rows, :], from_odd[rows, :])


def joined_x(a, low, high, ghost):
    first = lane_index() < HALF
    if a == 0:
        return low + pltpu.roll(jnp.where(first, high, ghost), HALF, 1)
    return high + pltpu.roll(jnp.where(first, ghost, low), HALF, 1)


def from_y(even_y, odd_y, b, rows):
    odd = is_odd("yz")
    pick = odd if b == 0 else jnp.logical_not(odd)
    return jnp.where(pick, even_y[rows, :], odd_y[rows, :])


def assembled(a, b, grid, received, field):
    even_x, odd_x, even_y, odd_y, *shared = received
    value = grid[row(a, b), :]
    if a in (0, 7):
        if shared and b in (0, 7):
            ghost = ghost_x(*shared, pl.ds(16 * field + 8 * (b // 7), 8))
        else:
            ghost = ghost_x(even_x, odd_x, pl.ds(64 * field + 8 * b, 8))
        value = joined_x(a, grid[row(0, b), :], grid[row(7, b), :], ghost)
    if b in (0, 7):
        rows = pl.ds(64 * field + 8 * a, 8)
        value = value + from_y(even_y, odd_y, b, rows)
    return value


def corners_kernel(corners, even_y, odd_y, shared):
    first = lane_index() < HALF
    for field in range(2):
        for side in range(2):
            rows = pl.ds(16 * field + 8 * side, 8)
            low = from_y(even_y, odd_y, 7 * side, pl.ds(64 * field, 8))
            high = from_y(even_y, odd_y, 7 * side, pl.ds(64 * field + 56, 8))
            shared[rows, :] = corners[rows, :] + jnp.where(first, low, high)


def selection(slots):
    elements = lax.broadcasted_iota(jnp.int32, (LANES, LANES), 0)
    return jnp.where(elements.astype(jnp.float32) == slots[pl.ds(0, 1), :], 1.0, 0.0)


def parts_of(values):
    parts = []
    for _ in range(SPLIT):
        parts.append(values.astype(jnp.bfloat16))
        values = values - parts[-1].astype(jnp.float32)
    return parts


def to_grid(chosen, values):
    parts = jnp.concatenate(parts_of(values), 0)
    picked = jnp.dot(
        jnp.concatenate([chosen.astype(jnp.bfloat16)] * SPLIT, 1),
        parts,
        preferred_element_type=jnp.float32,
    )
    return picked.T


def setup_kernel(
    slots, forcing, viscosity, mass_rate,
    right, diagonal, spread, mass, face_x, to_even, to_odd, corners, shifts, slot_rows,
    order, held, arrived,
):
    ordered = pltpu.make_async_copy(slots, order, arrived.at[3])
    copies = [
        pltpu.make_async_copy(source.at[0, 0], held.at[k], arrived.at[k])
        for k, source in enumerate((viscosity, mass_rate, forcing))
    ]
    for copy in [ordered] + copies:
        copy.start()
    point = sublane_index()
    last_weight = jnp.zeros((8, LANES), jnp.float32)
    for c in range(8):
        last_weight = jnp.where(point == c, float(WEIGHTS[c]), last_weight)
    ordered.wait()
    slot_rows[...] = jnp.broadcast_to(order[...].astype(jnp.float32), slot_rows.shape)
    chosen = selection(slot_rows)
    copies[0].wait()
    spread[...] = to_grid(chosen, held[0])
    copies[1].wait()
    mass[...] = to_grid(chosen, held[1])
    for a in range(8):
        for b in range(8):
            weight = last_weight * float(WEIGHTS[a] * WEIGHTS[b])
            spread[row(a, b), :] *= weight
            mass[row(a, b), :] *= weight
    copies[2].wait()
    right[...] = to_grid(chosen, held[2])
    squares = (DERIVATIVE * DERIVATIVE).T
    for b in range(8):
        lines = along(squares, [spread[row(a, b), :] for a in range(8)], 1)
        for a in range(8):
            diagonal[row(a, b), :] = lines[a] + mass[row(a, b), :]
    for a in range(8):
        lines = along(squares, [spread[row(a, b), :] for b in range(8)], 1)
        for b in range(8):
            diagonal[row(a, b), :] += lines[b]
    for a in range(8):
        lines = along(VERTICAL * squares, [spread[across(a, c), :] for c in range(8)], 1)
        lines = [lines[c] + diagonal[across(a, c), :] for c in range(8)]
        lines[0], lines[7] = join_vertical(lines[0], lines[7])
        for c in range(8):
            diagonal[across(a, c), :] = lines[c]
        low, high = join_vertical(right[across(a, 0), :], right[across(a, 7), :])
        right[across(a, 0), :] = low
        right[across(a, 7), :] = high
    odd = is_odd("yz")
    for field, source in enumerate((right, diagonal, spread)):
        for b in range(8):
            face_x[pl.ds(64 * field + 8 * b, 8), :] = packed_x(source, b)
        faces = []
        for side in range(2):
            part = [source[row(a, 7 * side), :] for a in range(8)]
            if field < 2:
                corners[pl.ds(16 * field + 8 * side, 8), :] = packed_x(source, 7 * side)
                part = joined_inside(part, 0.0)
            faces.append(part)
        for a in range(8):
            rows = pl.ds(64 * field + 8 * a, 8)
            lowest_to_highest(odd, to_even, to_odd, rows, faces[0][a], faces[1][a])
    rows = pl.ds(192, 8)
    lowest_to_highest(odd, to_even, to_odd, rows, packed_x(mass, 0), packed_x(mass, 7))
    for k in range(8):
        along_shift = back_shift = jnp.zeros((8, LANES), jnp.float32)
        for c in range(8):
            other = (c + k) % 8
            along_shift = jnp.where(point == c, float(DERIVATIVE[c, other]), along_shift)
            back_shift = jnp.where(
                point == c, float(VERTICAL * DERIVATIVE[other, c]), back_shift
            )
        shifts[pl.ds(8 * k, 8), :] = along_shift
        shifts[pl.ds(64 + 8 * k, 8), :] = back_shift


def join_vertical_packed(value):
    layer, point = lane_index() % EZ, sublane_index()
    from_below = pltpu.roll(pltpu.roll(value, 1, 0), 1, 1)
    from_above = pltpu.roll(pltpu.roll(value, 7, 0), LANES - 1, 1)
    below = jnp.logical_and(point == 0, layer > 0)
    above = jnp.logical_and(point == 7, layer < EZ - 1)
    return value + jnp.where(below, from_below, jnp.where(above, from_above, 0.0))


def shifted_sum(shifts, start, value):
    total = shifts[pl.ds(start, 8), :] * value
    for k in range(1, 8):
        total = total + shifts[pl.ds(start + 8 * k, 8), :] * pltpu.roll(value, 8 - k, 0)
    return total


def end_row(lines, end):
    total = None
    for q in range(8):
        term = lines[q] * float(DERIVATIVE[q, end])
        total = term if total is None else total + term
    return total


def corner_shares(values, outer, shifts):
    first = lane_index() < HALF
    lines = [packed_x(values, b) for b in range(8)]
    slopes = along(DERIVATIVE, lines, -1)
    slopes = [slopes[q] * outer[pl.ds(8 * q, 8), :] for q in range(8)]
    for_y = [end_row(slopes, 0), end_row(slopes, 7)]
    for_x = []
    for side in range(2):
        base = 64 + 72 * side
        spread = [outer[pl.ds(base + 8 * a, 8), :] for a in range(8)]
        slopes = along(DERIVATIVE, [values[row(a, 7 * side), :] for a in range(8)], -1)
        slopes = [slopes[q] * spread[q] for q in range(8)]
        share = jnp.where(first, end_row(slopes, 0), end_row(slopes, 7))
        corner = lines[7 * side]
        slope = shifted_sum(shifts, 0, corner) * jnp.where(first, spread[0], spread[7])
        share = share + shifted_sum(shifts, 64, slope) + outer[pl.ds(base + 64, 8), :] * corner
        for_x.append(share)
    return [join_vertical_packed(share) for share in for_x], [
        join_vertical_packed(share) for share in for_y
    ]


def joined_inside(lines, share):
    first = lane_index() < HALF
    low, high = lines[0], lines[7]
    new_low = low + jnp.where(first, share, pltpu.roll(high, HALF, 1))
    new_high = high + jnp.where(first, pltpu.roll(low, HALF, 1), share)
    return [new_low] + lines[1:7] + [new_high]


def send_faces(image, values, outer, shifts, face_x, to_even, to_odd):
    for_x, for_y = corner_shares(values, outer, shifts)
    odd = is_odd("yz")
    for b in range(8):
        face = packed_x(image, b)
        if b in (0, 7):
            face = face + for_x[b // 7]
        face_x[pl.ds(8 * b, 8), :] = face
    faces = []
    for side in range(2):
        part = [image[row(a, 7 * side), :] for a in range(8)]
        part = joined_inside(part, for_y[side])
        faces.append(part)
    for a in range(8):
        lowest_to_highest(odd, to_even, to_odd, pl.ds(8 * a, 8), faces[0][a], faces[1][a])


def operate(values, spread, mass, image):
    forward, backward = DERIVATIVE, DERIVATIVE.T
    for b in range(8):
        lines = [values[row(a, b), :] for a in range(8)]
        slopes = along(forward, lines, -1)
        back = along(backward, [slopes[a] * spread[row(a, b), :] for a in range(8)], -1)
        for a in range(8):
            image[row(a, b), :] = back[a] + mass[row(a, b), :] * lines[a]
    for a in range(8):
        slopes = along(forward, [values[row(a, b), :] for b in range(8)], -1)
        back = along(backward, [slopes[b] * spread[row(a, b), :] for b in range(8)], -1)
        for b in range(8):
            image[row(a, b), :] += back[b]
    energy = jnp.zeros((8, LANES), jnp.float32)
    for a in range(8):
        lines = [values[across(a, c), :] for c in range(8)]
        slopes = along(forward, lines, -1)
        back = along(
            VERTICAL * backward, [slopes[c] * spread[across(a, c), :] for c in range(8)], -1
        )
        back = [back[c] + image[across(a, c), :] for c in range(8)]
        for c in range(8):
            energy = energy + back[c] * lines[c]
        back[0], back[7] = join_vertical(back[0], back[7])
        for c in range(8):
            image[across(a, c), :] = back[c]
    return energy


def weighted(sums):
    layer, point = lane_index() % EZ, sublane_index()
    below = jnp.logical_and(point == 0, layer > 0)
    above = jnp.logical_and(point == 7, layer < EZ - 1)
    shared = jnp.where(jnp.logical_or(below, above), 0.5, 1.0)
    return (sums[0] + 0.5 * sums[1] + 0.25 * sums[2]) * shared


def ends(a, b):
    return int(a in (0, 7)) + int(b in (0, 7))


def first_kernel(
    right, diagonal, even_x, odd_x, even_y, odd_y, even_shared, odd_shared, spread, mass, shifts,
    whole_diagonal, values, image, outer, face_x, to_even, to_odd, moments,
):
    received = (even_x, odd_x, even_y, odd_y, even_shared, odd_shared)
    sums = [jnp.zeros((8, LANES), jnp.float32)] * 3
    for a in range(8):
        for b in range(8):
            source = assembled(a, b, right, received, 0)
            scale = assembled(a, b, diagonal, received, 1)
            value = source / scale
            whole_diagonal[row(a, b), :] = scale
            values[row(a, b), :] = value
            sums[ends(a, b)] = sums[ends(a, b)] + source * value
    moments[...] = weighted(sums)
    for b in range(8):
        outer[pl.ds(8 * b, 8), :] = pltpu.roll(
            ghost_x(even_x, odd_x, pl.ds(128 + 8 * b, 8)), HALF, 1
        )
    for side in range(2):
        for k in range(9):
            outer[pl.ds(64 + 72 * side + 8 * k, 8), :] = from_y(
                even_y, odd_y, 7 * side, pl.ds(128 + 8 * k, 8)
            )
    operate(values, spread, mass, image)
    send_faces(image, values, outer, shifts, face_x, to_even, to_odd)


def next_values(before_image, received, diagonal, before, values):
    cross = [jnp.zeros((8, LANES), jnp.float32)] * 3
    square = [jnp.zeros((8, LANES), jnp.float32)] * 3
    for a in range(8):
        for b in range(8):
            scale = diagonal[row(a, b), :]
            old = before[row(a, b), :]
            value = assembled(a, b, before_image, received, 0) / scale - old
            values[row(a, b), :] = value
            scaled = scale * value
            kind = ends(a, b)
            cross[kind] = cross[kind] + scaled * old
            square[kind] = square[kind] + scaled * value
    return weighted(cross), weighted(square)


def second_kernel(
    before_image, even_x, odd_x, odd_y, even_y, diagonal, before, spread, mass, shifts, outer,
    values, image, face_x, to_even, to_odd, moments,
):
    received = (even_x, odd_x, even_y, odd_y)
    cross, square = next_values(before_image, received, diagonal, before, values)
    moments[pl.ds(0, 8), :] = cross
    moments[pl.ds(8, 8), :] = square
    operate(values, spread, mass, image)
    send_faces(image, values, outer, shifts, face_x, to_even, to_odd)


def third_kernel(
    before_image, even_x, odd_x, odd_y, even_y, diagonal, before, spread, mass, shifts, outer,
    moments0, moments1, values, image, face_x, to_even, to_odd, sums,
):
    received = (even_x, odd_x, even_y, odd_y)
    cross, square = next_values(before_image, received, diagonal, before, values)
    energy = operate(values, spread, mass, image)
    send_faces(image, values, outer, shifts, face_x, to_even, to_odd)
    parts = [
        moments0[...], moments1[pl.ds(0, 8), :], moments1[pl.ds(8, 8), :], cross, square, energy
    ]
    lane = lax.broadcasted_iota(jnp.int32, (1, LANES), 1)
    line = jnp.zeros((1, LANES), jnp.float32)
    for k, part in enumerate(parts):
        total = jnp.sum(jnp.sum(part, 0, keepdims=True), 1, keepdims=True)
        line = jnp.where(lane == k, total, line)
    sums[...] = jnp.broadcast_to(line[None], sums.shape)


def recurrence(moments):
    moments = moments[:5] + [moments[5] - moments[4]]
    zero = jnp.zeros_like(moments[0])
    one = zero + 1.0

    def form(left, right, shift):
        total = zero
        for i in range(3):
            for j in range(3):
                if left[i] is not None and right[j] is not None:
                    entry = moments[i + j]
                    if shift:
                        entry = entry + moments[i + j + 1]
                    total = total + left[i] * right[j] * entry
        return total

    def ratio(top, bottom):
        fine = jnp.logical_and(bottom > 0.0, top > 0.0)
        return jnp.where(fine, top / jnp.where(fine, bottom, 1.0), 0.0)

    def add(left, scale, right):
        out = []
        for x, y in zip(left, right):
            if y is None:
                out.append(x)
            else:
                out.append(scale * y if x is None else x + scale * y)
        return out

    direction = [one, None, None, None]
    precond = [one, None, None, None]
    result = [None, None, None, None]
    norm = moments[0]
    for step in range(3):
        curve = form(direction, direction, True)
        length = ratio(norm, curve)
        result = add(result, length, direction)
        moved = add(direction, 1.0, [None] + direction[:3])
        if step == 0:
            precond = [jnp.where(curve > 0.0, moments[1] / curve, 1.0), -length, None, None]
        else:
            precond = add(precond, -length, moved)
        if step < 2:
            norm_next = form(precond, precond, False)
            direction = add(precond, ratio(norm_next, norm), direction)
            norm = norm_next
    return result[:3], precond


def last_kernel(
    before_image, even_x, odd_x, odd_y, even_y, diagonal, values0, values1, values2, sums,
    slot_rows, solution, residual, solution_grid, residual_grid,
):
    received = (even_x, odd_x, even_y, odd_y)
    line = jnp.sum(sums[...], 0)[0:1]
    lane = lax.broadcasted_iota(jnp.int32, (1, LANES), 1)
    moments = [
        jnp.sum(jnp.where(lane == k, line, 0.0), 1, keepdims=True) for k in range(6)
    ]
    result, precond = recurrence(moments)
    spread_out = lambda scalar: jnp.broadcast_to(scalar, (8, LANES))
    result = [spread_out(entry) for entry in result]
    precond = [spread_out(entry) for entry in precond]
    for a in range(8):
        for b in range(8):
            rows = row(a, b)
            basis = [values0[rows, :], values1[rows, :], values2[rows, :]]
            scale = diagonal[rows, :]
            image = assembled(a, b, before_image, received, 0) - scale * basis[2]
            near = result[0] * basis[0] + result[1] * basis[1] + result[2] * basis[2]
            far = precond[0] * basis[0] + precond[1] * basis[1] + precond[2] * basis[2]
            solution_grid[rows, :] = near
            residual_grid[rows, :] = scale * far + precond[3] * image
    chosen = selection(slot_rows).T.astype(jnp.bfloat16)
    for grid, out in ((solution_grid, solution), (residual_grid, residual)):
        total = None
        for part in parts_of(grid[...]):
            term = lax.dot_general(
                chosen, part, (((1,), (1,)), ((), ())), preferred_element_type=jnp.float32
            )
            total = term if total is None else total + term
        out[0, 0] = total


def call(kernel, name, shapes, scratch, *operands, outside=0):
    places = [pltpu.HBM] * outside + [pltpu.VMEM] * (len(operands) - outside)
    operands = [
        pltpu.with_memory_space_constraint(operand, place) if place == pltpu.HBM else operand
        for operand, place in zip(operands, places)
    ]
    return pl.pallas_call(
        kernel,
        out_shape=[jax.ShapeDtypeStruct(shape, jnp.float32) for shape in shapes],
        in_specs=[pl.BlockSpec(memory_space=place) for place in places],
        out_specs=[pl.BlockSpec(memory_space=pltpu.VMEM)] * len(shapes),
        scratch_shapes=scratch,
        compiler_params=pltpu.CompilerParams(vmem_limit_bytes=VMEM_BYTES),
        name=name,
    )(*operands)


def swapped(block, axis):
    extent = lax.axis_size(axis)
    even = [(i, i ^ 1) for i in range(extent)]
    odd = [(i, (((i + 1) ^ 1) - 1) % extent) for i in range(extent)]
    return lax.ppermute(block[0], axis, even), lax.ppermute(block[1], axis, odd)


def body(forcing, viscosity, mass_rate, slot_element):
    devices = lax.axis_size("gx") * lax.axis_size("yz")
    slots = slot_element[0]
    grid, face, tile = (POINTS, LANES), (64, LANES), (8, LANES)
    right, diagonal, spread, mass, out_x, *sent_y, corners, shifts, slot_rows = call(
        setup_kernel, "setup",
        [grid] * 4 + [(192, LANES), (200, LANES), (200, LANES), (32, LANES), (128, LANES)]
        + [tile],
        [
            pltpu.VMEM((1, LANES), jnp.int32),
            pltpu.VMEM((3, LANES, POINTS), jnp.float32),
            pltpu.SemaphoreType.DMA((4,)),
        ],
        slots, forcing, viscosity, mass_rate, outside=4,
    )
    received_x, received_y = swapped((out_x, out_x), "gx"), swapped(sent_y, "yz")
    [shared] = call(corners_kernel, "corners", [(32, LANES)], [], corners, *received_y)
    received = (*received_x, *received_y, *swapped((shared, shared), "gx"))
    diagonal, values0, image, outer, out_x, *sent_y, moments0 = call(
        first_kernel, "first", [grid] * 3 + [(208, LANES)] + [face] * 3 + [tile], [],
        right, diagonal, *received, spread, mass, shifts,
    )
    received = (*swapped((out_x, out_x), "gx"), *swapped(sent_y, "yz")[::-1])
    values1, image, out_x, *sent_y, moments1 = call(
        second_kernel, "second", [grid] * 2 + [face] * 3 + [(16, LANES)], [],
        image, *received, diagonal, values0, spread, mass, shifts, outer,
    )
    received = (*swapped((out_x, out_x), "gx"), *swapped(sent_y, "yz")[::-1])
    values2, image, out_x, *sent_y, sums = call(
        third_kernel, "third", [grid] * 2 + [face] * 3 + [(devices, 2, LANES)], [],
        image, *received, diagonal, values1, spread, mass, shifts, outer, moments0, moments1,
    )
    sums = lax.all_to_all(sums, ("gx", "yz"), 0, 0)
    received = (*swapped((out_x, out_x), "gx"), *swapped(sent_y, "yz")[::-1])
    return call(
        last_kernel, "last", [forcing.shape] * 2, [pltpu.VMEM(grid, jnp.float32)] * 2,
        image, *received, diagonal, values0, values1, values2, sums, slot_rows,
    )


def solution(mesh):
    placed = (
        P("gx", "yz", None, None),
        P("gx", "yz", None, None),
        P("gx", "yz", None, None),
        P("gx", "yz", None),
    )
    return jax.shard_map(
        body,
        mesh=mesh,
        in_specs=placed,
        out_specs=(P("gx", "yz", None, None), P("gx", "yz", None, None)),
        check_vma=False,
    )
```

```python
import jax
import jax.numpy as jnp
import numpy as np
from jax import lax
from jax.experimental import pallas as pl
from jax.experimental.pallas import tpu as pltpu
from jax.sharding import PartitionSpec as P

EZ = 64
LANES = 128
HALF = 64
POINTS = 512
SPLIT = 2
VERTICAL = 4.0
VMEM_BYTES = 24 * 1024 * 1024


def legendre_rows(nodes, degree):
    rows = [nodes * 0.0 + 1.0, nodes]
    for order in range(2, degree + 1):
        rows.append(((2 * order - 1) * nodes * rows[-1] - (order - 1) * rows[-2]) / order)
    return np.stack(rows, 1)


def spectral_tables():
    degree = 7
    nodes = np.cos(np.pi * np.arange(degree + 1) / degree)
    for sweep in range(60):
        legendre = legendre_rows(nodes, degree)
        nodes = nodes - (nodes * legendre[:, degree] - legendre[:, degree - 1]) / (
            (degree + 1) * legendre[:, degree]
        )
    nodes = nodes[::-1].copy()
    top_values = legendre_rows(nodes, degree)[:, degree]
    weights = 2.0 / (degree * (degree + 1) * top_values**2)
    identity = np.eye(degree + 1)
    spacing = nodes[:, None] - nodes[None, :] + identity
    derivative = top_values[:, None] / top_values[None, :] / spacing * (1.0 - identity)
    corner_fix = np.zeros(degree + 1)
    corner_fix[0] = -degree * (degree + 1) / 4.0
    corner_fix[degree] = degree * (degree + 1) / 4.0
    derivative = derivative + identity * corner_fix[None, :]
    return (derivative, weights)


DERIVATIVE, WEIGHTS = spectral_tables()


def row(a, b):
    return pl.ds(64 * a + 8 * b, 8)


def across(a, c):
    return pl.ds(64 * a + c, 8, stride=8)


def along(matrix, lines, sign):
    evens = [lines[j] + lines[7 - j] for j in range(4)]
    odds = [lines[j] - lines[7 - j] for j in range(4)]
    out = [None] * 8
    for i in range(4):
        even = odd = None
        for j in range(4):
            even_term = evens[j] * float((matrix[i, j] + matrix[i, 7 - j]) / 2)
            odd_term = odds[j] * float((matrix[i, j] - matrix[i, 7 - j]) / 2)
            even = even_term if even is None else even + even_term
            odd = odd_term if odd is None else odd + odd_term
        out[i] = even + odd
        out[7 - i] = even - odd if sign > 0 else odd - even
    return out


def lane_index():
    return lax.broadcasted_iota(jnp.int32, (8, LANES), 1)


def sublane_index():
    return lax.broadcasted_iota(jnp.int32, (8, LANES), 0)


def join_vertical(low, high):
    layer = lane_index() % EZ
    new_low = low + jnp.where(layer > 0, pltpu.roll(high, 1, 1), 0.0)
    new_high = high + jnp.where(layer < EZ - 1, pltpu.roll(low, LANES - 1, 1), 0.0)
    return new_low, new_high


def packed_x(grid, b):
    return jnp.where(lane_index() < HALF, grid[row(0, b), :], grid[row(7, b), :])


def lowest_to_highest(low_side, to_even, to_odd, rows, low, high):
    to_even[rows, :] = jnp.where(low_side, low, high)
    to_odd[rows, :] = jnp.where(low_side, high, low)


def is_odd(axis):
    return lax.axis_index(axis) % 2 == 1


def ghost_x(from_even, from_odd, rows):
    odd = lax.axis_index("gx") % 2
    first = (lane_index() < HALF).astype(jnp.int32)
    return jnp.where(first != odd, from_even[rows, :], from_odd[rows, :])


def joined_x(a, low, high, ghost):
    first = lane_index() < HALF
    if a == 0:
        return low + pltpu.roll(jnp.where(first, high, ghost), HALF, 1)
    return high + pltpu.roll(jnp.where(first, ghost, low), HALF, 1)


def from_y(even_y, odd_y, b, rows):
    odd = is_odd("yz")
    pick = odd if b == 0 else jnp.logical_not(odd)
    return jnp.where(pick, even_y[rows, :], odd_y[rows, :])


def assembled(a, b, grid, received, field):
    even_x, odd_x, even_y, odd_y, *shared = received
    value = grid[row(a, b), :]
    if a in (0, 7):
        if shared and b in (0, 7):
            ghost = ghost_x(*shared, pl.ds(16 * field + 8 * (b // 7), 8))
        else:
            ghost = ghost_x(even_x, odd_x, pl.ds(64 * field + 8 * b, 8))
        value = joined_x(a, grid[row(0, b), :], grid[row(7, b), :], ghost)
    if b in (0, 7):
        rows = pl.ds(64 * field + 8 * a, 8)
        value = value + from_y(even_y, odd_y, b, rows)
    return value


def corners_kernel(corners, odd_y, even_y, shared):
    first = lane_index() < HALF
    for field in range(2):
        for side in range(2):
            rows = pl.ds(16 * field + 8 * side, 8)
            low = from_y(even_y, odd_y, 7 * side, pl.ds(64 * field, 8))
            high = from_y(even_y, odd_y, 7 * side, pl.ds(64 * field + 56, 8))
            shared[rows, :] = corners[rows, :] + jnp.where(first, low, high)


def selection(slots):
    elements = lax.broadcasted_iota(jnp.int32, (LANES, LANES), 0)
    return jnp.where(elements.astype(jnp.float32) == slots[pl.ds(0, 1), :], 1.0, 0.0)


def parts_of(values):
    parts = []
    for _ in range(SPLIT):
        parts.append(values.astype(jnp.bfloat16))
        values = values - parts[-1].astype(jnp.float32)
    return parts


def to_grid(chosen, values):
    parts = jnp.concatenate(parts_of(values), 0)
    picked = jnp.dot(
        jnp.concatenate([chosen.astype(jnp.bfloat16)] * SPLIT, 1),
        parts,
        preferred_element_type=jnp.float32,
    )
    return picked.T


def setup_kernel(
    slots, forcing, viscosity, mass_rate,
    right, diagonal, spread, mass, face_x, to_even, to_odd, corners, shifts, slot_rows,
    order, held, arrived,
):
    ordered = pltpu.make_async_copy(slots, order, arrived.at[3])
    copies = [
        pltpu.make_async_copy(source.at[0, 0], held.at[k], arrived.at[k])
        for k, source in enumerate((viscosity, mass_rate, forcing))
    ]
    for copy in [ordered] + copies:
        copy.start()
    point = sublane_index()
    last_weight = jnp.zeros((8, LANES), jnp.float32)
    for c in range(8):
        last_weight = jnp.where(point == c, float(WEIGHTS[c]), last_weight)
    ordered.wait()
    slot_rows[...] = jnp.broadcast_to(order[...].astype(jnp.float32), slot_rows.shape)
    chosen = selection(slot_rows)
    copies[0].wait()
    spread[...] = to_grid(chosen, held[0])
    copies[1].wait()
    mass[...] = to_grid(chosen, held[1])
    for a in range(8):
        for b in range(8):
            weight = last_weight * float(WEIGHTS[a] * WEIGHTS[b])
            spread[row(a, b), :] *= weight
            mass[row(a, b), :] *= weight
    copies[2].wait()
    right[...] = to_grid(chosen, held[2])
    squares = (DERIVATIVE * DERIVATIVE).T
    for b in range(8):
        lines = along(squares, [spread[row(a, b), :] for a in range(8)], 1)
        for a in range(8):
            diagonal[row(a, b), :] = lines[a] + mass[row(a, b), :]
    for a in range(8):
        lines = along(squares, [spread[row(a, b), :] for b in range(8)], 1)
        for b in range(8):
            diagonal[row(a, b), :] += lines[b]
    for a in range(8):
        lines = along(VERTICAL * squares, [spread[across(a, c), :] for c in range(8)], 1)
        lines = [lines[c] + diagonal[across(a, c), :] for c in range(8)]
        lines[0], lines[7] = join_vertical(lines[0], lines[7])
        for c in range(8):
            diagonal[across(a, c), :] = lines[c]
        low, high = join_vertical(right[across(a, 0), :], right[across(a, 7), :])
        right[across(a, 0), :] = low
        right[across(a, 7), :] = high
    odd = is_odd("yz")
    for field, source in enumerate((right, diagonal, spread)):
        for b in range(8):
            face_x[pl.ds(64 * field + 8 * b, 8), :] = packed_x(source, b)
        faces = []
        for side in range(2):
            part = [source[row(a, 7 * side), :] for a in range(8)]
            if field < 2:
                corners[pl.ds(16 * field + 8 * side, 8), :] = packed_x(source, 7 * side)
                part = joined_inside(part, 0.0)
            faces.append(part)
        for a in range(8):
            rows = pl.ds(64 * field + 8 * a, 8)
            lowest_to_highest(odd, to_even, to_odd, rows, faces[0][a], faces[1][a])
    rows = pl.ds(192, 8)
    lowest_to_highest(odd, to_even, to_odd, rows, packed_x(mass, 0), packed_x(mass, 7))
    for k in range(8):
        along_shift = back_shift = jnp.zeros((8, LANES), jnp.float32)
        for c in range(8):
            other = (c + k) % 8
            along_shift = jnp.where(point == c, float(DERIVATIVE[c, other]), along_shift)
            back_shift = jnp.where(
                point == c, float(VERTICAL * DERIVATIVE[other, c]), back_shift
            )
        shifts[pl.ds(8 * k, 8), :] = along_shift
        shifts[pl.ds(64 + 8 * k, 8), :] = back_shift


def join_vertical_packed(value):
    layer, point = lane_index() % EZ, sublane_index()
    from_below = pltpu.roll(pltpu.roll(value, 1, 0), 1, 1)
    from_above = pltpu.roll(pltpu.roll(value, 7, 0), LANES - 1, 1)
    below = jnp.logical_and(point == 0, layer > 0)
    above = jnp.logical_and(point == 7, layer < EZ - 1)
    return value + jnp.where(below, from_below, jnp.where(above, from_above, 0.0))


def shifted_sum(shifts, start, value):
    total = shifts[pl.ds(start, 8), :] * value
    for k in range(1, 8):
        total = total + shifts[pl.ds(start + 8 * k, 8), :] * pltpu.roll(value, 8 - k, 0)
    return total


def end_row(lines, end):
    total = None
    for q in range(8):
        term = lines[q] * float(DERIVATIVE[q, end])
        total = term if total is None else total + term
    return total


def corner_shares(values, outer, shifts):
    first = lane_index() < HALF
    lines = [packed_x(values, b) for b in range(8)]
    slopes = along(DERIVATIVE, lines, -1)
    slopes = [slopes[q] * outer[pl.ds(8 * q, 8), :] for q in range(8)]
    for_y = [end_row(slopes, 0), end_row(slopes, 7)]
    for_x = []
    for side in range(2):
        base = 64 + 72 * side
        spread = [outer[pl.ds(base + 8 * a, 8), :] for a in range(8)]
        slopes = along(DERIVATIVE, [values[row(a, 7 * side), :] for a in range(8)], -1)
        slopes = [slopes[q] * spread[q] for q in range(8)]
        share = jnp.where(first, end_row(slopes, 0), end_row(slopes, 7))
        corner = lines[7 * side]
        slope = shifted_sum(shifts, 0, corner) * jnp.where(first, spread[0], spread[7])
        share = share + shifted_sum(shifts, 64, slope) + outer[pl.ds(base + 64, 8), :] * corner
        for_x.append(share)
    return [join_vertical_packed(share) for share in for_x], [
        join_vertical_packed(share) for share in for_y
    ]


def joined_inside(lines, share):
    first = lane_index() < HALF
    low, high = lines[0], lines[7]
    new_low = low + jnp.where(first, share, pltpu.roll(high, HALF, 1))
    new_high = high + jnp.where(first, pltpu.roll(low, HALF, 1), share)
    return [new_low] + lines[1:7] + [new_high]


def send_faces(image, values, outer, shifts, face_x, to_even, to_odd):
    for_x, for_y = corner_shares(values, outer, shifts)
    odd = is_odd("yz")
    for b in range(8):
        face = packed_x(image, b)
        if b in (0, 7):
            face = face + for_x[b // 7]
        face_x[pl.ds(8 * b, 8), :] = face
    faces = []
    for side in range(2):
        part = [image[row(a, 7 * side), :] for a in range(8)]
        part = joined_inside(part, for_y[side])
        faces.append(part)
    for a in range(8):
        lowest_to_highest(odd, to_even, to_odd, pl.ds(8 * a, 8), faces[0][a], faces[1][a])


def operate(values, spread, mass, image):
    forward, backward = DERIVATIVE, DERIVATIVE.T
    for b in range(8):
        lines = [values[row(a, b), :] for a in range(8)]
        slopes = along(forward, lines, -1)
        back = along(backward, [slopes[a] * spread[row(a, b), :] for a in range(8)], -1)
        for a in range(8):
            image[row(a, b), :] = back[a] + mass[row(a, b), :] * lines[a]
    for a in range(8):
        slopes = along(forward, [values[row(a, b), :] for b in range(8)], -1)
        back = along(backward, [slopes[b] * spread[row(a, b), :] for b in range(8)], -1)
        for b in range(8):
            image[row(a, b), :] += back[b]
    energy = jnp.zeros((8, LANES), jnp.float32)
    for a in range(8):
        lines = [values[across(a, c), :] for c in range(8)]
        slopes = along(forward, lines, -1)
        back = along(
            VERTICAL * backward, [slopes[c] * spread[across(a, c), :] for c in range(8)], -1
        )
        back = [back[c] + image[across(a, c), :] for c in range(8)]
        for c in range(8):
            energy = energy + back[c] * lines[c]
        back[0], back[7] = join_vertical(back[0], back[7])
        for c in range(8):
            image[across(a, c), :] = back[c]
    return energy


def weighted(sums):
    layer, point = lane_index() % EZ, sublane_index()
    below = jnp.logical_and(point == 0, layer > 0)
    above = jnp.logical_and(point == 7, layer < EZ - 1)
    shared = jnp.where(jnp.logical_or(below, above), 0.5, 1.0)
    return (sums[0] + 0.5 * sums[1] + 0.25 * sums[2]) * shared


def ends(a, b):
    return int(a in (0, 7)) + int(b in (0, 7))


def first_kernel(
    right, diagonal, even_x, odd_x, odd_y, even_y, even_shared, odd_shared, spread, mass, shifts,
    whole_diagonal, values, image, outer, face_x, to_even, to_odd, moments,
):
    received = (even_x, odd_x, even_y, odd_y, even_shared, odd_shared)
    sums = [jnp.zeros((8, LANES), jnp.float32)] * 3
    for a in range(8):
        for b in range(8):
            source = assembled(a, b, right, received, 0)
            scale = assembled(a, b, diagonal, received, 1)
            value = source / scale
            whole_diagonal[row(a, b), :] = scale
            values[row(a, b), :] = value
            sums[ends(a, b)] = sums[ends(a, b)] + source * value
    moments[...] = weighted(sums)
    for b in range(8):
        outer[pl.ds(8 * b, 8), :] = pltpu.roll(
            ghost_x(even_x, odd_x, pl.ds(128 + 8 * b, 8)), HALF, 1
        )
    for side in range(2):
        for k in range(9):
            outer[pl.ds(64 + 72 * side + 8 * k, 8), :] = from_y(
                even_y, odd_y, 7 * side, pl.ds(128 + 8 * k, 8)
            )
    operate(values, spread, mass, image)
    send_faces(image, values, outer, shifts, face_x, to_even, to_odd)


def next_values(before_image, received, diagonal, before, values):
    cross = [jnp.zeros((8, LANES), jnp.float32)] * 3
    square = [jnp.zeros((8, LANES), jnp.float32)] * 3
    for a in range(8):
        for b in range(8):
            scale = diagonal[row(a, b), :]
            old = before[row(a, b), :]
            value = assembled(a, b, before_image, received, 0) / scale - old
            values[row(a, b), :] = value
            scaled = scale * value
            kind = ends(a, b)
            cross[kind] = cross[kind] + scaled * old
            square[kind] = square[kind] + scaled * value
    return weighted(cross), weighted(square)


def second_kernel(
    before_image, even_x, odd_x, odd_y, even_y, diagonal, before, spread, mass, shifts, outer,
    values, image, face_x, to_even, to_odd, moments,
):
    received = (even_x, odd_x, even_y, odd_y)
    cross, square = next_values(before_image, received, diagonal, before, values)
    moments[pl.ds(0, 8), :] = cross
    moments[pl.ds(8, 8), :] = square
    operate(values, spread, mass, image)
    send_faces(image, values, outer, shifts, face_x, to_even, to_odd)


def third_kernel(
    before_image, even_x, odd_x, odd_y, even_y, diagonal, before, spread, mass, shifts, outer,
    values, image, face_x, to_even, to_odd, moments,
):
    received = (even_x, odd_x, even_y, odd_y)
    cross, square = next_values(before_image, received, diagonal, before, values)
    energy = operate(values, spread, mass, image)
    send_faces(image, values, outer, shifts, face_x, to_even, to_odd)
    for k, part in enumerate((cross, square, energy)):
        moments[pl.ds(8 * k, 8), :] = part


def sums_kernel(moments0, moments1, moments2, sums):
    parts = [
        moments0[...], moments1[pl.ds(0, 8), :], moments1[pl.ds(8, 8), :], *(moments2[pl.ds(8 * k, 8), :] for k in range(3))
    ]
    lane = lax.broadcasted_iota(jnp.int32, (1, LANES), 1)
    line = jnp.zeros((1, LANES), jnp.float32)
    for k, part in enumerate(parts):
        total = jnp.sum(jnp.sum(part, 0, keepdims=True), 1, keepdims=True)
        line = jnp.where(lane == k, total, line)
    sums[...] = jnp.broadcast_to(line[None], sums.shape)


def recurrence(moments):
    moments = moments[:5] + [moments[5] - moments[4]]
    zero = jnp.zeros_like(moments[0])
    one = zero + 1.0

    def form(left, right, shift):
        total = zero
        for i in range(3):
            for j in range(3):
                if left[i] is not None and right[j] is not None:
                    entry = moments[i + j]
                    if shift:
                        entry = entry + moments[i + j + 1]
                    total = total + left[i] * right[j] * entry
        return total

    def ratio(top, bottom):
        fine = jnp.logical_and(bottom > 0.0, top > 0.0)
        return jnp.where(fine, top / jnp.where(fine, bottom, 1.0), 0.0)

    def add(left, scale, right):
        out = []
        for x, y in zip(left, right):
            if y is None:
                out.append(x)
            else:
                out.append(scale * y if x is None else x + scale * y)
        return out

    direction = [one, None, None, None]
    precond = [one, None, None, None]
    result = [None, None, None, None]
    norm = moments[0]
    for step in range(3):
        curve = form(direction, direction, True)
        length = ratio(norm, curve)
        result = add(result, length, direction)
        moved = add(direction, 1.0, [None] + direction[:3])
        if step == 0:
            precond = [jnp.where(curve > 0.0, moments[1] / curve, 1.0), -length, None, None]
        else:
            precond = add(precond, -length, moved)
        if step < 2:
            norm_next = form(precond, precond, False)
            direction = add(precond, ratio(norm_next, norm), direction)
            norm = norm_next
    return result[:3], precond


def last_kernel(
    before_image, even_x, odd_x, odd_y, even_y, diagonal, values0, values1, values2, sums,
    slot_rows, solution, residual, solution_grid, residual_grid,
):
    received = (even_x, odd_x, even_y, odd_y)
    line = jnp.sum(sums[...], 0)[0:1]
    lane = lax.broadcasted_iota(jnp.int32, (1, LANES), 1)
    moments = [
        jnp.sum(jnp.where(lane == k, line, 0.0), 1, keepdims=True) for k in range(6)
    ]
    result, precond = recurrence(moments)
    spread_out = lambda scalar: jnp.broadcast_to(scalar, (8, LANES))
    result = [spread_out(entry) for entry in result]
    precond = [spread_out(entry) for entry in precond]
    for a in range(8):
        for b in range(8):
            rows = row(a, b)
            basis = [values0[rows, :], values1[rows, :], values2[rows, :]]
            scale = diagonal[rows, :]
            image = assembled(a, b, before_image, received, 0) - scale * basis[2]
            near = result[0] * basis[0] + result[1] * basis[1] + result[2] * basis[2]
            far = precond[0] * basis[0] + precond[1] * basis[1] + precond[2] * basis[2]
            solution_grid[rows, :] = near
            residual_grid[rows, :] = scale * far + precond[3] * image
    chosen = selection(slot_rows).T.astype(jnp.bfloat16)
    for grid, out in ((solution_grid, solution), (residual_grid, residual)):
        total = None
        for part in parts_of(grid[...]):
            term = lax.dot_general(
                chosen, part, (((1,), (1,)), ((), ())), preferred_element_type=jnp.float32
            )
            total = term if total is None else total + term
        out[0, 0] = total


def call(kernel, name, shapes, scratch, *operands, outside=0):
    places = [pltpu.HBM] * outside + [pltpu.VMEM] * (len(operands) - outside)
    operands = [
        pltpu.with_memory_space_constraint(operand, place) if place == pltpu.HBM else operand
        for operand, place in zip(operands, places)
    ]
    return pl.pallas_call(
        kernel,
        out_shape=[jax.ShapeDtypeStruct(shape, jnp.float32) for shape in shapes],
        in_specs=[pl.BlockSpec(memory_space=place) for place in places],
        out_specs=[pl.BlockSpec(memory_space=pltpu.VMEM)] * len(shapes),
        scratch_shapes=scratch,
        compiler_params=pltpu.CompilerParams(vmem_limit_bytes=VMEM_BYTES),
        name=name,
    )(*operands)


def swapped(block, axis):
    extent = lax.axis_size(axis)
    even = [(i, i ^ 1) for i in range(extent)]
    odd = [(i, (((i + 1) ^ 1) - 1) % extent) for i in range(extent)]
    return lax.ppermute(block[0], axis, even), lax.ppermute(block[1], axis, odd)


def body(forcing, viscosity, mass_rate, slot_element):
    devices = lax.axis_size("gx") * lax.axis_size("yz")
    slots = slot_element[0]
    grid, face, tile = (POINTS, LANES), (64, LANES), (8, LANES)
    right, diagonal, spread, mass, out_x, *sent_y, corners, shifts, slot_rows = call(
        setup_kernel, "setup",
        [grid] * 4 + [(192, LANES), (200, LANES), (200, LANES), (32, LANES), (128, LANES)]
        + [tile],
        [
            pltpu.VMEM((1, LANES), jnp.int32),
            pltpu.VMEM((3, LANES, POINTS), jnp.float32),
            pltpu.SemaphoreType.DMA((4,)),
        ],
        slots, forcing, viscosity, mass_rate, outside=4,
    )
    received_x, received_y = swapped((out_x, out_x), "gx"), swapped(sent_y, "yz")[::-1]
    [shared] = call(corners_kernel, "corners", [(32, LANES)], [], corners, *received_y)
    received = (*received_x, *received_y, *swapped((shared, shared), "gx"))
    diagonal, values0, image, outer, out_x, *sent_y, moments0 = call(
        first_kernel, "first", [grid] * 3 + [(208, LANES)] + [face] * 3 + [tile], [],
        right, diagonal, *received, spread, mass, shifts,
    )
    received = (*swapped((out_x, out_x), "gx"), *swapped(sent_y, "yz")[::-1])
    values1, image, out_x, *sent_y, moments1 = call(
        second_kernel, "second", [grid] * 2 + [face] * 3 + [(16, LANES)], [],
        image, *received, diagonal, values0, spread, mass, shifts, outer,
    )
    received = (*swapped((out_x, out_x), "gx"), *swapped(sent_y, "yz")[::-1])
    values2, image, out_x, *sent_y, moments2 = call(
        third_kernel, "third", [grid] * 2 + [face] * 3 + [(24, LANES)], [],
        image, *received, diagonal, values1, spread, mass, shifts, outer,
    )
    [sums] = call(sums_kernel, "sums", [(devices, 2, LANES)], [], moments0, moments1, moments2)
    sums = lax.all_to_all(sums, ("gx", "yz"), 0, 0)
    received = (*swapped((out_x, out_x), "gx"), *swapped(sent_y, "yz")[::-1])
    return call(
        last_kernel, "last", [forcing.shape] * 2, [pltpu.VMEM(grid, jnp.float32)] * 2,
        image, *received, diagonal, values0, values1, values2, sums, slot_rows,
    )


def solution(mesh):
    placed = (
        P("gx", "yz", None, None),
        P("gx", "yz", None, None),
        P("gx", "yz", None, None),
        P("gx", "yz", None),
    )
    return jax.shard_map(
        body,
        mesh=mesh,
        in_specs=placed,
        out_specs=(P("gx", "yz", None, None), P("gx", "yz", None, None)),
        check_vma=False,
    )
```

```python
import jax
import jax.numpy as jnp
import numpy as np
from jax import lax
from jax.experimental import pallas as pl
from jax.experimental.pallas import tpu as pltpu
from jax.sharding import PartitionSpec as P

EZ = 64
LANES = 128
HALF = 64
POINTS = 512
SPLIT = 2
VERTICAL = 4.0
VMEM_BYTES = 24 * 1024 * 1024


def legendre_rows(nodes, degree):
    rows = [nodes * 0.0 + 1.0, nodes]
    for order in range(2, degree + 1):
        rows.append(((2 * order - 1) * nodes * rows[-1] - (order - 1) * rows[-2]) / order)
    return np.stack(rows, 1)


def spectral_tables():
    degree = 7
    nodes = np.cos(np.pi * np.arange(degree + 1) / degree)
    for sweep in range(60):
        legendre = legendre_rows(nodes, degree)
        nodes = nodes - (nodes * legendre[:, degree] - legendre[:, degree - 1]) / (
            (degree + 1) * legendre[:, degree]
        )
    nodes = nodes[::-1].copy()
    top_values = legendre_rows(nodes, degree)[:, degree]
    weights = 2.0 / (degree * (degree + 1) * top_values**2)
    identity = np.eye(degree + 1)
    spacing = nodes[:, None] - nodes[None, :] + identity
    derivative = top_values[:, None] / top_values[None, :] / spacing * (1.0 - identity)
    corner_fix = np.zeros(degree + 1)
    corner_fix[0] = -degree * (degree + 1) / 4.0
    corner_fix[degree] = degree * (degree + 1) / 4.0
    derivative = derivative + identity * corner_fix[None, :]
    return (derivative, weights)


DERIVATIVE, WEIGHTS = spectral_tables()


def row(a, b):
    return pl.ds(64 * a + 8 * b, 8)


def across(a, c):
    return pl.ds(64 * a + c, 8, stride=8)


def along(matrix, lines, sign):
    evens = [lines[j] + lines[7 - j] for j in range(4)]
    odds = [lines[j] - lines[7 - j] for j in range(4)]
    out = [None] * 8
    for i in range(4):
        even = odd = None
        for j in range(4):
            even_term = evens[j] * float((matrix[i, j] + matrix[i, 7 - j]) / 2)
            odd_term = odds[j] * float((matrix[i, j] - matrix[i, 7 - j]) / 2)
            even = even_term if even is None else even + even_term
            odd = odd_term if odd is None else odd + odd_term
        out[i] = even + odd
        out[7 - i] = even - odd if sign > 0 else odd - even
    return out


def lane_index():
    return lax.broadcasted_iota(jnp.int32, (8, LANES), 1)


def sublane_index():
    return lax.broadcasted_iota(jnp.int32, (8, LANES), 0)


def join_vertical(low, high):
    layer = lane_index() % EZ
    new_low = low + jnp.where(layer > 0, pltpu.roll(high, 1, 1), 0.0)
    new_high = high + jnp.where(layer < EZ - 1, pltpu.roll(low, LANES - 1, 1), 0.0)
    return new_low, new_high


def packed_x(grid, b):
    return jnp.where(lane_index() < HALF, grid[row(0, b), :], grid[row(7, b), :])


def lowest_to_highest(low_side, to_even, to_odd, rows, low, high):
    to_even[rows, :] = jnp.where(low_side, low, high)
    to_odd[rows, :] = jnp.where(low_side, high, low)


def is_odd(axis):
    return lax.axis_index(axis) % 2 == 1


def ghost_x(from_even, from_odd, rows):
    odd = lax.axis_index("gx") % 2
    first = (lane_index() < HALF).astype(jnp.int32)
    return jnp.where(first != odd, from_even[rows, :], from_odd[rows, :])


def joined_x(a, low, high, ghost):
    first = lane_index() < HALF
    if a == 0:
        return low + pltpu.roll(jnp.where(first, high, ghost), HALF, 1)
    return high + pltpu.roll(jnp.where(first, ghost, low), HALF, 1)


def from_y(even_y, odd_y, b, rows):
    odd = is_odd("yz")
    pick = odd if b == 0 else jnp.logical_not(odd)
    return jnp.where(pick, even_y[rows, :], odd_y[rows, :])


def assembled(a, b, grid, received, field):
    even_x, odd_x, even_y, odd_y, *shared = received
    value = grid[row(a, b), :]
    if a in (0, 7):
        if shared and b in (0, 7):
            ghost = ghost_x(*shared, pl.ds(16 * field + 8 * (b // 7), 8))
        else:
            ghost = ghost_x(even_x, odd_x, pl.ds(64 * field + 8 * b, 8))
        value = joined_x(a, grid[row(0, b), :], grid[row(7, b), :], ghost)
    if b in (0, 7):
        rows = pl.ds(64 * field + 8 * a, 8)
        value = value + from_y(even_y, odd_y, b, rows)
    return value


def corners_kernel(corners, odd_y, even_y, shared):
    first = lane_index() < HALF
    for field in range(2):
        for side in range(2):
            rows = pl.ds(16 * field + 8 * side, 8)
            low = from_y(even_y, odd_y, 7 * side, pl.ds(64 * field, 8))
            high = from_y(even_y, odd_y, 7 * side, pl.ds(64 * field + 56, 8))
            shared[rows, :] = corners[rows, :] + jnp.where(first, low, high)


def selection(slots):
    elements = lax.broadcasted_iota(jnp.int32, (LANES, LANES), 0)
    return jnp.where(elements.astype(jnp.float32) == slots[pl.ds(0, 1), :], 1.0, 0.0)


def parts_of(values):
    parts = []
    for _ in range(SPLIT):
        parts.append(values.astype(jnp.bfloat16))
        values = values - parts[-1].astype(jnp.float32)
    return parts


def to_grid(chosen, values):
    parts = jnp.concatenate(parts_of(values), 0)
    picked = jnp.dot(
        jnp.concatenate([chosen.astype(jnp.bfloat16)] * SPLIT, 1),
        parts,
        preferred_element_type=jnp.float32,
    )
    return picked.T


def setup_kernel(
    slots, forcing, viscosity, mass_rate,
    right, diagonal, spread, mass, face_x, to_even, to_odd, corners, shifts, slot_rows,
    order, held, arrived,
):
    ordered = pltpu.make_async_copy(slots, order, arrived.at[3])
    copies = [
        pltpu.make_async_copy(source.at[0, 0], held.at[k], arrived.at[k])
        for k, source in enumerate((viscosity, mass_rate, forcing))
    ]
    for copy in [ordered] + copies:
        copy.start()
    point = sublane_index()
    last_weight = jnp.zeros((8, LANES), jnp.float32)
    for c in range(8):
        last_weight = jnp.where(point == c, float(WEIGHTS[c]), last_weight)
    ordered.wait()
    slot_rows[...] = jnp.broadcast_to(order[...].astype(jnp.float32), slot_rows.shape)
    chosen = selection(slot_rows)
    for copy in copies:
        copy.wait()
    spread[...] = to_grid(chosen, held[0])
    mass[...] = to_grid(chosen, held[1])
    for a in range(8):
        for b in range(8):
            weight = last_weight * float(WEIGHTS[a] * WEIGHTS[b])
            spread[row(a, b), :] *= weight
            mass[row(a, b), :] *= weight
    right[...] = to_grid(chosen, held[2])
    squares = (DERIVATIVE * DERIVATIVE).T
    for b in range(8):
        lines = along(squares, [spread[row(a, b), :] for a in range(8)], 1)
        for a in range(8):
            diagonal[row(a, b), :] = lines[a] + mass[row(a, b), :]
    for a in range(8):
        lines = along(squares, [spread[row(a, b), :] for b in range(8)], 1)
        for b in range(8):
            diagonal[row(a, b), :] += lines[b]
    for a in range(8):
        lines = along(VERTICAL * squares, [spread[across(a, c), :] for c in range(8)], 1)
        lines = [lines[c] + diagonal[across(a, c), :] for c in range(8)]
        lines[0], lines[7] = join_vertical(lines[0], lines[7])
        for c in range(8):
            diagonal[across(a, c), :] = lines[c]
        low, high = join_vertical(right[across(a, 0), :], right[across(a, 7), :])
        right[across(a, 0), :] = low
        right[across(a, 7), :] = high
    odd = is_odd("yz")
    for field, source in enumerate((right, diagonal, spread)):
        for b in range(8):
            face_x[pl.ds(64 * field + 8 * b, 8), :] = packed_x(source, b)
        faces = []
        for side in range(2):
            part = [source[row(a, 7 * side), :] for a in range(8)]
            if field < 2:
                corners[pl.ds(16 * field + 8 * side, 8), :] = packed_x(source, 7 * side)
                part = joined_inside(part, 0.0)
            faces.append(part)
        for a in range(8):
            rows = pl.ds(64 * field + 8 * a, 8)
            lowest_to_highest(odd, to_even, to_odd, rows, faces[0][a], faces[1][a])
    rows = pl.ds(192, 8)
    lowest_to_highest(odd, to_even, to_odd, rows, packed_x(mass, 0), packed_x(mass, 7))
    for k in range(8):
        along_shift = back_shift = jnp.zeros((8, LANES), jnp.float32)
        for c in range(8):
            other = (c + k) % 8
            along_shift = jnp.where(point == c, float(DERIVATIVE[c, other]), along_shift)
            back_shift = jnp.where(
                point == c, float(VERTICAL * DERIVATIVE[other, c]), back_shift
            )
        shifts[pl.ds(8 * k, 8), :] = along_shift
        shifts[pl.ds(64 + 8 * k, 8), :] = back_shift


def join_vertical_packed(value):
    layer, point = lane_index() % EZ, sublane_index()
    from_below = pltpu.roll(pltpu.roll(value, 1, 0), 1, 1)
    from_above = pltpu.roll(pltpu.roll(value, 7, 0), LANES - 1, 1)
    below = jnp.logical_and(point == 0, layer > 0)
    above = jnp.logical_and(point == 7, layer < EZ - 1)
    return value + jnp.where(below, from_below, jnp.where(above, from_above, 0.0))


def shifted_sum(shifts, start, value):
    total = shifts[pl.ds(start, 8), :] * value
    for k in range(1, 8):
        total = total + shifts[pl.ds(start + 8 * k, 8), :] * pltpu.roll(value, 8 - k, 0)
    return total


def end_row(lines, end):
    total = None
    for q in range(8):
        term = lines[q] * float(DERIVATIVE[q, end])
        total = term if total is None else total + term
    return total


def corner_shares(values, outer, shifts):
    first = lane_index() < HALF
    lines = [packed_x(values, b) for b in range(8)]
    slopes = along(DERIVATIVE, lines, -1)
    slopes = [slopes[q] * outer[pl.ds(8 * q, 8), :] for q in range(8)]
    for_y = [end_row(slopes, 0), end_row(slopes, 7)]
    for_x = []
    for side in range(2):
        base = 64 + 72 * side
        spread = [outer[pl.ds(base + 8 * a, 8), :] for a in range(8)]
        slopes = along(DERIVATIVE, [values[row(a, 7 * side), :] for a in range(8)], -1)
        slopes = [slopes[q] * spread[q] for q in range(8)]
        share = jnp.where(first, end_row(slopes, 0), end_row(slopes, 7))
        corner = lines[7 * side]
        slope = shifted_sum(shifts, 0, corner) * jnp.where(first, spread[0], spread[7])
        share = share + shifted_sum(shifts, 64, slope) + outer[pl.ds(base + 64, 8), :] * corner
        for_x.append(share)
    return [join_vertical_packed(share) for share in for_x], [
        join_vertical_packed(share) for share in for_y
    ]


def joined_inside(lines, share):
    first = lane_index() < HALF
    low, high = lines[0], lines[7]
    new_low = low + jnp.where(first, share, pltpu.roll(high, HALF, 1))
    new_high = high + jnp.where(first, pltpu.roll(low, HALF, 1), share)
    return [new_low] + lines[1:7] + [new_high]


def send_faces(image, values, outer, shifts, face_x, to_even, to_odd):
    for_x, for_y = corner_shares(values, outer, shifts)
    odd = is_odd("yz")
    for b in range(8):
        face = packed_x(image, b)
        if b in (0, 7):
            face = face + for_x[b // 7]
        face_x[pl.ds(8 * b, 8), :] = face
    faces = []
    for side in range(2):
        part = [image[row(a, 7 * side), :] for a in range(8)]
        part = joined_inside(part, for_y[side])
        faces.append(part)
    for a in range(8):
        lowest_to_highest(odd, to_even, to_odd, pl.ds(8 * a, 8), faces[0][a], faces[1][a])


def streamwise(lines, b, spread, mass, image):
    slopes = along(DERIVATIVE, lines, -1)
    back = along(DERIVATIVE.T, [slopes[a] * spread[row(a, b), :] for a in range(8)], -1)
    for a in range(8):
        image[row(a, b), :] = back[a] + mass[row(a, b), :] * lines[a]


def operate(values, spread, image):
    forward, backward = DERIVATIVE, DERIVATIVE.T
    for a in range(8):
        slopes = along(forward, [values[row(a, b), :] for b in range(8)], -1)
        back = along(backward, [slopes[b] * spread[row(a, b), :] for b in range(8)], -1)
        for b in range(8):
            image[row(a, b), :] += back[b]
    energy = jnp.zeros((8, LANES), jnp.float32)
    for a in range(8):
        lines = [values[across(a, c), :] for c in range(8)]
        slopes = along(forward, lines, -1)
        back = along(
            VERTICAL * backward, [slopes[c] * spread[across(a, c), :] for c in range(8)], -1
        )
        back = [back[c] + image[across(a, c), :] for c in range(8)]
        for c in range(8):
            energy = energy + back[c] * lines[c]
        back[0], back[7] = join_vertical(back[0], back[7])
        for c in range(8):
            image[across(a, c), :] = back[c]
    return energy


def weighted(sums):
    layer, point = lane_index() % EZ, sublane_index()
    below = jnp.logical_and(point == 0, layer > 0)
    above = jnp.logical_and(point == 7, layer < EZ - 1)
    shared = jnp.where(jnp.logical_or(below, above), 0.5, 1.0)
    return (sums[0] + 0.5 * sums[1] + 0.25 * sums[2]) * shared


def ends(a, b):
    return int(a in (0, 7)) + int(b in (0, 7))


def early_kernel(
    right, diagonal, even_x, odd_x, odd_y, even_y, spread, mass,
    whole_diagonal, jacobi, values, image, outer, moments,
):
    received = (even_x, odd_x, even_y, odd_y)
    first = lane_index() < HALF
    sums = [jnp.zeros((8, LANES), jnp.float32)] * 3
    for b in range(8):
        lines = []
        for a in range(8):
            source = assembled(a, b, right, received, 0)
            scale = assembled(a, b, diagonal, received, 1)
            inverse = 1.0 / scale
            value = source * inverse
            if ends(a, b) == 2:
                value = jnp.where(first, 0.0, value) if a == 0 else jnp.where(first, value, 0.0)
            whole_diagonal[row(a, b), :] = scale
            jacobi[row(a, b), :] = inverse
            values[row(a, b), :] = value
            sums[ends(a, b)] = sums[ends(a, b)] + source * value
            lines.append(value)
        streamwise(lines, b, spread, mass, image)
    moments[...] = weighted(sums)
    for b in range(8):
        outer[pl.ds(8 * b, 8), :] = pltpu.roll(
            ghost_x(even_x, odd_x, pl.ds(128 + 8 * b, 8)), HALF, 1
        )
    for side in range(2):
        for k in range(9):
            outer[pl.ds(64 + 72 * side + 8 * k, 8), :] = from_y(
                even_y, odd_y, 7 * side, pl.ds(128 + 8 * k, 8)
            )
    operate(values, spread, image)


def add_packed(grid, b, value):
    first = lane_index() < HALF
    grid[row(0, b), :] += jnp.where(first, value, 0.0)
    grid[row(7, b), :] += jnp.where(first, 0.0, value)


def first_kernel(
    right, diagonal, even_x, odd_x, odd_y, even_y, even_shared, odd_shared, spread, mass, shifts,
    outer, early_diagonal, early_jacobi, early_values, early_image, early_moments,
    whole_diagonal, jacobi, values, image, face_x, to_even, to_odd, moments,
):
    received = (even_x, odd_x, even_y, odd_y, even_shared, odd_shared)
    first = lane_index() < HALF
    corners = []
    total = jnp.zeros((8, LANES), jnp.float32)
    for b in (0, 7):
        packed = []
        for a in (0, 7):
            source = assembled(a, b, right, received, 0)
            scale = assembled(a, b, diagonal, received, 1)
            inverse = 1.0 / scale
            value = source * inverse
            whole_diagonal[row(a, b), :] = scale
            jacobi[row(a, b), :] = inverse
            values[row(a, b), :] = value
            packed.append((value, source * value))
        corners.append(jnp.where(first, packed[0][0], packed[1][0]))
        total = total + jnp.where(first, packed[0][1], packed[1][1])
    zero = jnp.zeros((8, LANES), jnp.float32)
    moments[...] = early_moments[...] + weighted([zero, zero, total])
    for side, corner in enumerate(corners):
        b = 7 * side
        slopes = []
        for q in range(8):
            slope = jnp.where(first, float(DERIVATIVE[q, 0]), float(DERIVATIVE[q, 7]))
            slopes.append(spread[row(q, b), :] * (slope * corner))
        back = along(DERIVATIVE.T, slopes, -1)
        for a in range(8):
            image[row(a, b), :] += join_vertical_packed(back[a])
    slopes = []
    for q in range(8):
        slope = corners[0] * float(DERIVATIVE[q, 0]) + corners[1] * float(DERIVATIVE[q, 7])
        slopes.append(packed_x(spread, q) * slope)
    back = along(DERIVATIVE.T, slopes, -1)
    for side, corner in enumerate(corners):
        b = 7 * side
        slope = shifted_sum(shifts, 0, corner) * packed_x(spread, b)
        back[b] = back[b] + shifted_sum(shifts, 64, slope) + packed_x(mass, b) * corner
    for b in range(8):
        add_packed(image, b, join_vertical_packed(back[b]))
    send_faces(image, values, outer, shifts, face_x, to_even, to_odd)


def next_values(before_image, received, diagonal, jacobi, before, spread, mass, values, image):
    cross = [jnp.zeros((8, LANES), jnp.float32)] * 3
    square = [jnp.zeros((8, LANES), jnp.float32)] * 3
    for b in range(8):
        lines = []
        for a in range(8):
            old = before[row(a, b), :]
            scaled = assembled(a, b, before_image, received, 0) - diagonal[row(a, b), :] * old
            value = scaled * jacobi[row(a, b), :]
            values[row(a, b), :] = value
            kind = ends(a, b)
            cross[kind] = cross[kind] + scaled * old
            square[kind] = square[kind] + scaled * value
            lines.append(value)
        streamwise(lines, b, spread, mass, image)
    return weighted(cross), weighted(square)


def second_kernel(
    before_image, even_x, odd_x, odd_y, even_y, diagonal, jacobi, before, spread, mass,
    shifts, outer,
    values, image, face_x, to_even, to_odd, moments,
):
    received = (even_x, odd_x, even_y, odd_y)
    cross, square = next_values(
        before_image, received, diagonal, jacobi, before, spread, mass, values, image
    )
    moments[pl.ds(0, 8), :] = cross
    moments[pl.ds(8, 8), :] = square
    operate(values, spread, image)
    send_faces(image, values, outer, shifts, face_x, to_even, to_odd)


def third_kernel(
    before_image, even_x, odd_x, odd_y, even_y, diagonal, jacobi, before, spread, mass,
    shifts, outer,
    values, image, face_x, to_even, to_odd, moments,
):
    received = (even_x, odd_x, even_y, odd_y)
    cross, square = next_values(
        before_image, received, diagonal, jacobi, before, spread, mass, values, image
    )
    energy = operate(values, spread, image)
    send_faces(image, values, outer, shifts, face_x, to_even, to_odd)
    for k, part in enumerate((cross, square, energy)):
        moments[pl.ds(8 * k, 8), :] = part


def sums_kernel(moments0, moments1, moments2, sums):
    parts = [
        moments0[...], moments1[pl.ds(0, 8), :], moments1[pl.ds(8, 8), :], *(moments2[pl.ds(8 * k, 8), :] for k in range(3))
    ]
    lane = lax.broadcasted_iota(jnp.int32, (1, LANES), 1)
    line = jnp.zeros((1, LANES), jnp.float32)
    for k, part in enumerate(parts):
        total = jnp.sum(jnp.sum(part, 0, keepdims=True), 1, keepdims=True)
        line = jnp.where(lane == k, total, line)
    sums[...] = jnp.broadcast_to(line[None], sums.shape)


def recurrence(moments):
    moments = moments[:5] + [moments[5] - moments[4]]
    zero = jnp.zeros_like(moments[0])
    one = zero + 1.0

    def form(left, right, shift):
        total = zero
        for i in range(3):
            for j in range(3):
                if left[i] is not None and right[j] is not None:
                    entry = moments[i + j]
                    if shift:
                        entry = entry + moments[i + j + 1]
                    total = total + left[i] * right[j] * entry
        return total

    def ratio(top, bottom):
        fine = jnp.logical_and(bottom > 0.0, top > 0.0)
        return jnp.where(fine, top / jnp.where(fine, bottom, 1.0), 0.0)

    def add(left, scale, right):
        out = []
        for x, y in zip(left, right):
            if y is None:
                out.append(x)
            else:
                out.append(scale * y if x is None else x + scale * y)
        return out

    direction = [one, None, None, None]
    precond = [one, None, None, None]
    result = [None, None, None, None]
    norm = moments[0]
    for step in range(3):
        curve = form(direction, direction, True)
        length = ratio(norm, curve)
        result = add(result, length, direction)
        moved = add(direction, 1.0, [None] + direction[:3])
        if step == 0:
            precond = [jnp.where(curve > 0.0, moments[1] / curve, 1.0), -length, None, None]
        else:
            precond = add(precond, -length, moved)
        if step < 2:
            norm_next = form(precond, precond, False)
            direction = add(precond, ratio(norm_next, norm), direction)
            norm = norm_next
    return result[:3], precond


def to_slots(chosen, grid):
    total = None
    for part in parts_of(grid):
        term = lax.dot_general(
            chosen, part, (((1,), (1,)), ((), ())), preferred_element_type=jnp.float32
        )
        total = term if total is None else total + term
    return total


def solution_kernel(
    values0, values1, values2, sums, slot_rows, solution, precond_rows, solution_grid
):
    line = jnp.sum(sums[...], 0)[0:1]
    lane = lax.broadcasted_iota(jnp.int32, (1, LANES), 1)
    moments = [
        jnp.sum(jnp.where(lane == k, line, 0.0), 1, keepdims=True) for k in range(6)
    ]
    result, precond = recurrence(moments)
    result = [jnp.broadcast_to(entry, (8, LANES)) for entry in result]
    for k in range(4):
        precond_rows[pl.ds(8 * k, 8), :] = jnp.broadcast_to(precond[k], (8, LANES))
    for a in range(8):
        for b in range(8):
            rows = row(a, b)
            solution_grid[rows, :] = (
                result[0] * values0[rows, :]
                + result[1] * values1[rows, :]
                + result[2] * values2[rows, :]
            )
    chosen = selection(slot_rows).T.astype(jnp.bfloat16)
    solution[0, 0] = to_slots(chosen, solution_grid[...])


def last_kernel(
    before_image, even_x, odd_x, odd_y, even_y, diagonal, values0, values1, values2, precond_rows,
    slot_rows, residual, residual_grid,
):
    received = (even_x, odd_x, even_y, odd_y)
    precond = [precond_rows[pl.ds(8 * k, 8), :] for k in range(4)]
    for a in range(8):
        for b in range(8):
            rows = row(a, b)
            far = (
                precond[0] * values0[rows, :]
                + precond[1] * values1[rows, :]
                + (precond[2] - precond[3]) * values2[rows, :]
            )
            image = assembled(a, b, before_image, received, 0)
            residual_grid[rows, :] = diagonal[rows, :] * far + precond[3] * image
    chosen = selection(slot_rows).T.astype(jnp.bfloat16)
    residual[0, 0] = to_slots(chosen, residual_grid[...])


def call(kernel, name, shapes, scratch, *operands, outside=0, aliases=None):
    places = [pltpu.HBM] * outside + [pltpu.VMEM] * (len(operands) - outside)
    operands = [
        pltpu.with_memory_space_constraint(operand, place) if place == pltpu.HBM else operand
        for operand, place in zip(operands, places)
    ]
    return pl.pallas_call(
        kernel,
        out_shape=[jax.ShapeDtypeStruct(shape, jnp.float32) for shape in shapes],
        in_specs=[pl.BlockSpec(memory_space=place) for place in places],
        out_specs=[pl.BlockSpec(memory_space=pltpu.VMEM)] * len(shapes),
        scratch_shapes=scratch,
        input_output_aliases=aliases or {},
        compiler_params=pltpu.CompilerParams(vmem_limit_bytes=VMEM_BYTES),
        name=name,
    )(*operands)


def swapped(block, axis):
    extent = lax.axis_size(axis)
    even = [(i, i ^ 1) for i in range(extent)]
    odd = [(i, (((i + 1) ^ 1) - 1) % extent) for i in range(extent)]
    return lax.ppermute(block[0], axis, even), lax.ppermute(block[1], axis, odd)


def body(forcing, viscosity, mass_rate, slot_element):
    devices = lax.axis_size("gx") * lax.axis_size("yz")
    slots = slot_element[0]
    grid, face, tile = (POINTS, LANES), (64, LANES), (8, LANES)
    right, diagonal, spread, mass, out_x, *sent_y, corners, shifts, slot_rows = call(
        setup_kernel, "setup",
        [grid] * 4 + [(192, LANES), (200, LANES), (200, LANES), (32, LANES), (128, LANES)]
        + [tile],
        [
            pltpu.VMEM((1, LANES), jnp.int32),
            pltpu.VMEM((3, LANES, POINTS), jnp.float32),
            pltpu.SemaphoreType.DMA((4,)),
        ],
        slots, forcing, viscosity, mass_rate, outside=4,
    )
    received_x, received_y = swapped((out_x, out_x), "gx"), swapped(sent_y, "yz")[::-1]
    [shared] = call(corners_kernel, "corners", [(32, LANES)], [], corners, *received_y)
    received = (*received_x, *received_y, *swapped((shared, shared), "gx"))
    *early, outer, moments0 = call(
        early_kernel, "early", [grid] * 4 + [(208, LANES), tile], [],
        right, diagonal, *received_x, *received_y, spread, mass,
    )
    diagonal, jacobi, values0, image, out_x, *sent_y, moments0 = call(
        first_kernel, "first", [grid] * 4 + [face] * 3 + [tile], [],
        right, diagonal, *received, spread, mass, shifts, outer, *early, moments0,
        aliases={12: 0, 13: 1, 14: 2, 15: 3},
    )
    received = (*swapped((out_x, out_x), "gx"), *swapped(sent_y, "yz")[::-1])
    values1, image, out_x, *sent_y, moments1 = call(
        second_kernel, "second", [grid] * 2 + [face] * 3 + [(16, LANES)], [],
        image, *received, diagonal, jacobi, values0, spread, mass, shifts, outer,
    )
    received = (*swapped((out_x, out_x), "gx"), *swapped(sent_y, "yz")[::-1])
    values2, image, out_x, *sent_y, moments2 = call(
        third_kernel, "third", [grid] * 2 + [face] * 3 + [(24, LANES)], [],
        image, *received, diagonal, jacobi, values1, spread, mass, shifts, outer,
    )
    [sums] = call(sums_kernel, "sums", [(devices, 2, LANES)], [], moments0, moments1, moments2)
    sums = lax.all_to_all(sums, ("gx", "yz"), 0, 0)
    received = (*swapped((out_x, out_x), "gx"), *swapped(sent_y, "yz")[::-1])
    result, precond = call(
        solution_kernel, "solution", [forcing.shape, (32, LANES)],
        [pltpu.VMEM(grid, jnp.float32)],
        values0, values1, values2, sums, slot_rows,
    )
    [residual] = call(
        last_kernel, "last", [forcing.shape], [pltpu.VMEM(grid, jnp.float32)],
        image, *received, diagonal, values0, values1, values2, precond, slot_rows,
    )
    return result, residual


def solution(mesh):
    placed = (
        P("gx", "yz", None, None),
        P("gx", "yz", None, None),
        P("gx", "yz", None, None),
        P("gx", "yz", None),
    )
    return jax.shard_map(
        body,
        mesh=mesh,
        in_specs=placed,
        out_specs=(P("gx", "yz", None, None), P("gx", "yz", None, None)),
        check_vma=False,
    )
```

```python
import jax
import jax.numpy as jnp
import numpy as np
from jax import lax
from jax.experimental import pallas as pl
from jax.experimental.pallas import tpu as pltpu
from jax.sharding import PartitionSpec as P

EZ = 64
LANES = 128
HALF = 64
POINTS = 512
SPLIT = 2
VERTICAL = 4.0
VMEM_BYTES = 24 * 1024 * 1024


def legendre_rows(nodes, degree):
    rows = [nodes * 0.0 + 1.0, nodes]
    for order in range(2, degree + 1):
        rows.append(((2 * order - 1) * nodes * rows[-1] - (order - 1) * rows[-2]) / order)
    return np.stack(rows, 1)


def spectral_tables():
    degree = 7
    nodes = np.cos(np.pi * np.arange(degree + 1) / degree)
    for sweep in range(60):
        legendre = legendre_rows(nodes, degree)
        nodes = nodes - (nodes * legendre[:, degree] - legendre[:, degree - 1]) / (
            (degree + 1) * legendre[:, degree]
        )
    nodes = nodes[::-1].copy()
    top_values = legendre_rows(nodes, degree)[:, degree]
    weights = 2.0 / (degree * (degree + 1) * top_values**2)
    identity = np.eye(degree + 1)
    spacing = nodes[:, None] - nodes[None, :] + identity
    derivative = top_values[:, None] / top_values[None, :] / spacing * (1.0 - identity)
    corner_fix = np.zeros(degree + 1)
    corner_fix[0] = -degree * (degree + 1) / 4.0
    corner_fix[degree] = degree * (degree + 1) / 4.0
    derivative = derivative + identity * corner_fix[None, :]
    return (derivative, weights)


DERIVATIVE, WEIGHTS = spectral_tables()


def row(a, b):
    return pl.ds(64 * a + 8 * b, 8)


def across(a, c):
    return pl.ds(64 * a + c, 8, stride=8)


def along(matrix, lines, sign):
    evens = [lines[j] + lines[7 - j] for j in range(4)]
    odds = [lines[j] - lines[7 - j] for j in range(4)]
    out = [None] * 8
    for i in range(4):
        even = odd = None
        for j in range(4):
            even_term = evens[j] * float((matrix[i, j] + matrix[i, 7 - j]) / 2)
            odd_term = odds[j] * float((matrix[i, j] - matrix[i, 7 - j]) / 2)
            even = even_term if even is None else even + even_term
            odd = odd_term if odd is None else odd + odd_term
        out[i] = even + odd
        out[7 - i] = even - odd if sign > 0 else odd - even
    return out


def lane_index():
    return lax.broadcasted_iota(jnp.int32, (8, LANES), 1)


def sublane_index():
    return lax.broadcasted_iota(jnp.int32, (8, LANES), 0)


def join_vertical(low, high):
    layer = lane_index() % EZ
    new_low = low + jnp.where(layer > 0, pltpu.roll(high, 1, 1), 0.0)
    new_high = high + jnp.where(layer < EZ - 1, pltpu.roll(low, LANES - 1, 1), 0.0)
    return new_low, new_high


def packed_x(grid, b):
    return jnp.where(lane_index() < HALF, grid[row(0, b), :], grid[row(7, b), :])


def lowest_to_highest(low_side, to_even, to_odd, rows, low, high):
    to_even[rows, :] = jnp.where(low_side, low, high)
    to_odd[rows, :] = jnp.where(low_side, high, low)


def is_odd(axis):
    return lax.axis_index(axis) % 2 == 1


def ghost_x(from_even, from_odd, rows):
    odd = lax.axis_index("gx") % 2
    first = (lane_index() < HALF).astype(jnp.int32)
    return jnp.where(first != odd, from_even[rows, :], from_odd[rows, :])


def joined_x(a, low, high, ghost):
    first = lane_index() < HALF
    if a == 0:
        return low + pltpu.roll(jnp.where(first, high, ghost), HALF, 1)
    return high + pltpu.roll(jnp.where(first, ghost, low), HALF, 1)


def from_y(even_y, odd_y, b, rows):
    odd = is_odd("yz")
    pick = odd if b == 0 else jnp.logical_not(odd)
    return jnp.where(pick, even_y[rows, :], odd_y[rows, :])


def assembled(a, b, grid, received, field):
    even_x, odd_x, even_y, odd_y, *shared = received
    value = grid[row(a, b), :]
    if a in (0, 7):
        if shared and b in (0, 7):
            ghost = ghost_x(*shared, pl.ds(16 * field + 8 * (b // 7), 8))
        else:
            ghost = ghost_x(even_x, odd_x, pl.ds(64 * field + 8 * b, 8))
        value = joined_x(a, grid[row(0, b), :], grid[row(7, b), :], ghost)
    if b in (0, 7):
        rows = pl.ds(64 * field + 8 * a, 8)
        value = value + from_y(even_y, odd_y, b, rows)
    return value


def corners_kernel(corners, odd_y, even_y, shared):
    first = lane_index() < HALF
    for field in range(2):
        for side in range(2):
            rows = pl.ds(16 * field + 8 * side, 8)
            low = from_y(even_y, odd_y, 7 * side, pl.ds(64 * field, 8))
            high = from_y(even_y, odd_y, 7 * side, pl.ds(64 * field + 56, 8))
            shared[rows, :] = corners[rows, :] + jnp.where(first, low, high)


def selection(slots):
    elements = lax.broadcasted_iota(jnp.int32, (LANES, LANES), 0)
    return jnp.where(elements.astype(jnp.float32) == slots[pl.ds(0, 1), :], 1.0, 0.0)


def parts_of(values):
    parts = []
    for _ in range(SPLIT):
        parts.append(values.astype(jnp.bfloat16))
        values = values - parts[-1].astype(jnp.float32)
    return parts


def to_grid(chosen, values):
    parts = jnp.concatenate(parts_of(values), 0)
    picked = jnp.dot(
        jnp.concatenate([chosen.astype(jnp.bfloat16)] * SPLIT, 1),
        parts,
        preferred_element_type=jnp.float32,
    )
    return picked.T


def setup_kernel(
    slots, forcing, viscosity, mass_rate,
    right, diagonal, spread, mass, face_x, to_even, to_odd, corners, shifts, slot_rows,
    order, held, arrived,
):
    ordered = pltpu.make_async_copy(slots, order, arrived.at[3])
    copies = [
        pltpu.make_async_copy(source.at[0, 0], held.at[k], arrived.at[k])
        for k, source in enumerate((viscosity, mass_rate, forcing))
    ]
    for copy in [ordered] + copies:
        copy.start()
    point = sublane_index()
    last_weight = jnp.zeros((8, LANES), jnp.float32)
    for c in range(8):
        last_weight = jnp.where(point == c, float(WEIGHTS[c]), last_weight)
    ordered.wait()
    slot_rows[...] = jnp.broadcast_to(order[...].astype(jnp.float32), slot_rows.shape)
    chosen = selection(slot_rows)
    for copy in copies:
        copy.wait()
    spread[...] = to_grid(chosen, held[0])
    mass[...] = to_grid(chosen, held[1])
    for a in range(8):
        for b in range(8):
            weight = last_weight * float(WEIGHTS[a] * WEIGHTS[b])
            spread[row(a, b), :] *= weight
            mass[row(a, b), :] *= weight
    right[...] = to_grid(chosen, held[2])
    squares = (DERIVATIVE * DERIVATIVE).T
    for b in range(8):
        lines = along(squares, [spread[row(a, b), :] for a in range(8)], 1)
        for a in range(8):
            diagonal[row(a, b), :] = lines[a] + mass[row(a, b), :]
    for a in range(8):
        lines = along(squares, [spread[row(a, b), :] for b in range(8)], 1)
        for b in range(8):
            diagonal[row(a, b), :] += lines[b]
    for a in range(8):
        lines = along(VERTICAL * squares, [spread[across(a, c), :] for c in range(8)], 1)
        lines = [lines[c] + diagonal[across(a, c), :] for c in range(8)]
        lines[0], lines[7] = join_vertical(lines[0], lines[7])
        for c in range(8):
            diagonal[across(a, c), :] = lines[c]
        low, high = join_vertical(right[across(a, 0), :], right[across(a, 7), :])
        right[across(a, 0), :] = low
        right[across(a, 7), :] = high
    odd = is_odd("yz")
    for field, source in enumerate((right, diagonal, spread)):
        for b in range(8):
            face_x[pl.ds(64 * field + 8 * b, 8), :] = packed_x(source, b)
        faces = []
        for side in range(2):
            part = [source[row(a, 7 * side), :] for a in range(8)]
            if field < 2:
                corners[pl.ds(16 * field + 8 * side, 8), :] = packed_x(source, 7 * side)
                part = joined_inside(part, 0.0)
            faces.append(part)
        for a in range(8):
            rows = pl.ds(64 * field + 8 * a, 8)
            lowest_to_highest(odd, to_even, to_odd, rows, faces[0][a], faces[1][a])
    rows = pl.ds(192, 8)
    lowest_to_highest(odd, to_even, to_odd, rows, packed_x(mass, 0), packed_x(mass, 7))
    for k in range(8):
        along_shift = back_shift = jnp.zeros((8, LANES), jnp.float32)
        for c in range(8):
            other = (c + k) % 8
            along_shift = jnp.where(point == c, float(DERIVATIVE[c, other]), along_shift)
            back_shift = jnp.where(
                point == c, float(VERTICAL * DERIVATIVE[other, c]), back_shift
            )
        shifts[pl.ds(8 * k, 8), :] = along_shift
        shifts[pl.ds(64 + 8 * k, 8), :] = back_shift


def join_vertical_packed(value):
    layer, point = lane_index() % EZ, sublane_index()
    from_below = pltpu.roll(pltpu.roll(value, 1, 0), 1, 1)
    from_above = pltpu.roll(pltpu.roll(value, 7, 0), LANES - 1, 1)
    below = jnp.logical_and(point == 0, layer > 0)
    above = jnp.logical_and(point == 7, layer < EZ - 1)
    return value + jnp.where(below, from_below, jnp.where(above, from_above, 0.0))


def shifted_sum(shifts, start, value):
    total = shifts[pl.ds(start, 8), :] * value
    for k in range(1, 8):
        total = total + shifts[pl.ds(start + 8 * k, 8), :] * pltpu.roll(value, 8 - k, 0)
    return total


def end_row(lines, end):
    total = None
    for q in range(8):
        term = lines[q] * float(DERIVATIVE[q, end])
        total = term if total is None else total + term
    return total


def corner_shares(values, outer, shifts):
    first = lane_index() < HALF
    lines = [packed_x(values, b) for b in range(8)]
    slopes = along(DERIVATIVE, lines, -1)
    slopes = [slopes[q] * outer[pl.ds(8 * q, 8), :] for q in range(8)]
    for_y = [end_row(slopes, 0), end_row(slopes, 7)]
    for_x = []
    for side in range(2):
        base = 64 + 72 * side
        spread = [outer[pl.ds(base + 8 * a, 8), :] for a in range(8)]
        slopes = along(DERIVATIVE, [values[row(a, 7 * side), :] for a in range(8)], -1)
        slopes = [slopes[q] * spread[q] for q in range(8)]
        share = jnp.where(first, end_row(slopes, 0), end_row(slopes, 7))
        corner = lines[7 * side]
        slope = shifted_sum(shifts, 0, corner) * jnp.where(first, spread[0], spread[7])
        share = share + shifted_sum(shifts, 64, slope) + outer[pl.ds(base + 64, 8), :] * corner
        for_x.append(share)
    return [join_vertical_packed(share) for share in for_x], [
        join_vertical_packed(share) for share in for_y
    ]


def joined_inside(lines, share):
    first = lane_index() < HALF
    low, high = lines[0], lines[7]
    new_low = low + jnp.where(first, share, pltpu.roll(high, HALF, 1))
    new_high = high + jnp.where(first, pltpu.roll(low, HALF, 1), share)
    return [new_low] + lines[1:7] + [new_high]


def send_faces(image, values, outer, shifts, face_x, to_even, to_odd):
    for_x, for_y = corner_shares(values, outer, shifts)
    odd = is_odd("yz")
    for b in range(8):
        face = packed_x(image, b)
        if b in (0, 7):
            face = face + for_x[b // 7]
        face_x[pl.ds(8 * b, 8), :] = face
    faces = []
    for side in range(2):
        part = [image[row(a, 7 * side), :] for a in range(8)]
        part = joined_inside(part, for_y[side])
        faces.append(part)
    for a in range(8):
        lowest_to_highest(odd, to_even, to_odd, pl.ds(8 * a, 8), faces[0][a], faces[1][a])


def streamwise(lines, b, spread, mass):
    slopes = along(DERIVATIVE, lines, -1)
    back = along(DERIVATIVE.T, [slopes[a] * spread[row(a, b), :] for a in range(8)], -1)
    return [back[a] + mass[row(a, b), :] * lines[a] for a in range(8)]


def join_layers(image):
    for a in range(8):
        low, high = join_vertical(image[across(a, 0), :], image[across(a, 7), :])
        image[across(a, 0), :] = low
        image[across(a, 7), :] = high


def vertical_part(lines, spread):
    slopes = along(DERIVATIVE, lines, -1)
    return along(VERTICAL * DERIVATIVE.T, [slopes[c] * spread[c] for c in range(8)], -1)


def operate(values, spread, image):
    for a in range(8):
        slopes = along(DERIVATIVE, [values[row(a, b), :] for b in range(8)], -1)
        back = along(DERIVATIVE.T, [slopes[b] * spread[row(a, b), :] for b in range(8)], -1)
        for b in range(8):
            image[row(a, b), :] += back[b]
    for a in range(8):
        back = vertical_part(
            [values[across(a, c), :] for c in range(8)],
            [spread[across(a, c), :] for c in range(8)],
        )
        for c in range(8):
            image[across(a, c), :] += back[c]


def weighted(sums):
    layer, point = lane_index() % EZ, sublane_index()
    below = jnp.logical_and(point == 0, layer > 0)
    above = jnp.logical_and(point == 7, layer < EZ - 1)
    shared = jnp.where(jnp.logical_or(below, above), 0.5, 1.0)
    return (sums[0] + 0.5 * sums[1] + 0.25 * sums[2]) * shared


def ends(a, b):
    return int(a in (0, 7)) + int(b in (0, 7))


def early_kernel(
    right, diagonal, even_x, odd_x, odd_y, even_y, spread, mass,
    whole_diagonal, jacobi, values, image, outer, moments, from_low, from_high, from_side, packed,
):
    received = (even_x, odd_x, even_y, odd_y)
    first = lane_index() < HALF
    sums = [jnp.zeros((8, LANES), jnp.float32)] * 3
    for b in range(8):
        lines = []
        for a in range(8):
            source = assembled(a, b, right, received, 0)
            scale = assembled(a, b, diagonal, received, 1)
            inverse = 1.0 / scale
            value = source * inverse
            if ends(a, b) == 2:
                value = jnp.where(first, 0.0, value) if a == 0 else jnp.where(first, value, 0.0)
            whole_diagonal[row(a, b), :] = scale
            jacobi[row(a, b), :] = inverse
            values[row(a, b), :] = value
            sums[ends(a, b)] = sums[ends(a, b)] + source * value
            lines.append(value)
        back = streamwise(lines, b, spread, mass)
        for a in range(8):
            image[row(a, b), :] = back[a]
    moments[...] = weighted(sums)
    for b in range(8):
        outer[pl.ds(8 * b, 8), :] = pltpu.roll(
            ghost_x(even_x, odd_x, pl.ds(128 + 8 * b, 8)), HALF, 1
        )
    for side in range(2):
        for k in range(9):
            outer[pl.ds(64 + 72 * side + 8 * k, 8), :] = from_y(
                even_y, odd_y, 7 * side, pl.ds(128 + 8 * k, 8)
            )
    operate(values, spread, image)
    join_layers(image)
    for a in range(8):
        for end, out in ((0, from_low), (7, from_high)):
            slopes = [spread[row(a, q), :] * float(DERIVATIVE[q, end]) for q in range(8)]
            back = along(DERIVATIVE.T, slopes, -1)
            for b in range(8):
                out[row(a, b), :] = back[b]
    for b in range(8):
        packed[pl.ds(8 * b, 8), :] = packed_x(spread, b)
        back = along(
            DERIVATIVE.T, [spread[row(q, b), :] * outer_slope(q) for q in range(8)], -1
        )
        for a in range(8):
            from_side[row(a, b), :] = back[a]


def outer_slope(q):
    first = lane_index() < HALF
    return jnp.where(first, float(DERIVATIVE[q, 0]), float(DERIVATIVE[q, 7]))


def add_packed(grid, b, value):
    first = lane_index() < HALF
    grid[row(0, b), :] += jnp.where(first, value, 0.0)
    grid[row(7, b), :] += jnp.where(first, 0.0, value)


def first_kernel(
    right, diagonal, even_x, odd_x, odd_y, even_y, even_shared, odd_shared, spread, mass, shifts,
    outer, early_diagonal, early_jacobi, early_values, early_image, early_moments,
    whole_diagonal, jacobi, values, image, face_x, to_even, to_odd, moments,
):
    received = (even_x, odd_x, even_y, odd_y, even_shared, odd_shared)
    first = lane_index() < HALF
    corners = []
    total = jnp.zeros((8, LANES), jnp.float32)
    for b in (0, 7):
        packed = []
        for a in (0, 7):
            source = assembled(a, b, right, received, 0)
            scale = assembled(a, b, diagonal, received, 1)
            inverse = 1.0 / scale
            value = source * inverse
            whole_diagonal[row(a, b), :] = scale
            jacobi[row(a, b), :] = inverse
            values[row(a, b), :] = value
            packed.append((value, source * value))
        corners.append(jnp.where(first, packed[0][0], packed[1][0]))
        total = total + jnp.where(first, packed[0][1], packed[1][1])
    zero = jnp.zeros((8, LANES), jnp.float32)
    moments[...] = early_moments[...] + weighted([zero, zero, total])
    for side, corner in enumerate(corners):
        b = 7 * side
        slopes = []
        for q in range(8):
            slopes.append(spread[row(q, b), :] * (outer_slope(q) * corner))
        back = along(DERIVATIVE.T, slopes, -1)
        for a in range(8):
            image[row(a, b), :] += join_vertical_packed(back[a])
    slopes = []
    for q in range(8):
        slope = corners[0] * float(DERIVATIVE[q, 0]) + corners[1] * float(DERIVATIVE[q, 7])
        slopes.append(packed_x(spread, q) * slope)
    back = along(DERIVATIVE.T, slopes, -1)
    for side, corner in enumerate(corners):
        b = 7 * side
        slope = shifted_sum(shifts, 0, corner) * packed_x(spread, b)
        back[b] = back[b] + shifted_sum(shifts, 64, slope) + packed_x(mass, b) * corner
    for b in range(8):
        add_packed(image, b, join_vertical_packed(back[b]))
    send_faces(image, values, outer, shifts, face_x, to_even, to_odd)


def inner_kernel(
    before_image, diagonal, jacobi, before, spread, mass, values, image, moments
):
    first = lane_index() < HALF
    zero = jnp.zeros((8, LANES), jnp.float32)
    cross, square = [zero] * 3, [zero] * 3
    for b in range(8):
        lines = []
        for a in range(8):
            if b in (0, 7):
                values[row(a, b), :] = zero
                image[row(a, b), :] = zero
                continue
            joined = before_image[row(a, b), :]
            if a in (0, 7):
                joined = joined_x(a, before_image[row(0, b), :], before_image[row(7, b), :], 0.0)
            old = before[row(a, b), :]
            scaled = joined - diagonal[row(a, b), :] * old
            if a in (0, 7):
                scaled = jnp.where(first, 0.0, scaled) if a == 0 else jnp.where(first, scaled, 0.0)
            value = scaled * jacobi[row(a, b), :]
            values[row(a, b), :] = value
            kind = ends(a, b)
            cross[kind] = cross[kind] + scaled * old
            square[kind] = square[kind] + scaled * value
            lines.append(value)
        if lines:
            back = streamwise(lines, b, spread, mass)
            for a in range(8):
                image[row(a, b), :] = back[a]
    moments[pl.ds(0, 8), :] = weighted(cross)
    moments[pl.ds(8, 8), :] = weighted(square)
    operate(values, spread, image)


def outer_kernel(
    before_image, even_x, odd_x, odd_y, even_y, diagonal, jacobi, before, spread, mass, shifts,
    outer, from_low, from_high, from_side, packed, inner_moments, inner_values, inner_image,
    values, image, face_x, to_even, to_odd, moments, face, face_back,
):
    received = (even_x, odd_x, even_y, odd_y)
    zero = jnp.zeros((8, LANES), jnp.float32)
    cross, square = [zero] * 3, [zero] * 3
    sides = []
    for b in (0, 7):
        lines = []
        for a in range(8):
            old = before[row(a, b), :]
            scaled = assembled(a, b, before_image, received, 0) - diagonal[row(a, b), :] * old
            value = scaled * jacobi[row(a, b), :]
            values[row(a, b), :] = value
            kind = ends(a, b)
            cross[kind] = cross[kind] + scaled * old
            square[kind] = square[kind] + scaled * value
            lines.append(value)
        sides.append(lines)
    lines = [zero] * 8
    for b in range(1, 7):
        old = packed_x(before, b)
        ghost = pltpu.roll(ghost_x(even_x, odd_x, pl.ds(8 * b, 8)), HALF, 1)
        scaled = packed_x(before_image, b) + ghost - packed_x(diagonal, b) * old
        lines[b] = scaled * packed_x(jacobi, b)
        add_packed(values, b, lines[b])
        cross[1] = cross[1] + scaled * old
        square[1] = square[1] + scaled * lines[b]
    for b in range(8):
        face[pl.ds(8 * b, 8), :] = lines[b]
    back = vertical_part(
        [face[pl.ds(c, 8, stride=8), :] for c in range(8)],
        [packed[pl.ds(c, 8, stride=8), :] for c in range(8)],
    )
    for c in range(8):
        face_back[pl.ds(c, 8, stride=8), :] = back[c]
    slopes = along(DERIVATIVE, lines, -1)
    back = along(DERIVATIVE.T, [slopes[q] * packed[pl.ds(8 * q, 8), :] for q in range(8)], -1)
    for b in range(8):
        share = back[b] + face_back[pl.ds(8 * b, 8), :]
        if b not in (0, 7):
            share = share + packed_x(mass, b) * lines[b]
        add_packed(image, b, share)
    ends_back = [streamwise(sides[k], 7 * k, spread, mass) for k in range(2)]
    for a in range(8):
        for b in range(8):
            rows = row(a, b)
            share = from_low[rows, :] * sides[0][a] + from_high[rows, :] * sides[1][a]
            if b in (0, 7):
                share = share + ends_back[b // 7][a]
            else:
                share = share + from_side[rows, :] * lines[b]
            image[rows, :] += share
    for b in (0, 7):
        at = [pl.ds(8 * b + c, 8, stride=64) for c in range(8)]
        back = vertical_part(
            [values[at[c], :] for c in range(8)], [spread[at[c], :] for c in range(8)]
        )
        for c in range(8):
            image[at[c], :] += back[c]
    moments[pl.ds(0, 8), :] = inner_moments[pl.ds(0, 8), :] + weighted(cross)
    moments[pl.ds(8, 8), :] = inner_moments[pl.ds(8, 8), :] + weighted(square)
    if moments.shape[0] > 16:
        energy = [zero] * 4
        for a in range(8):
            for b in range(8):
                energy[b % 4] = energy[b % 4] + values[row(a, b), :] * image[row(a, b), :]
        moments[pl.ds(16, 8), :] = (energy[0] + energy[1]) + (energy[2] + energy[3])
    join_layers(image)
    send_faces(image, values, outer, shifts, face_x, to_even, to_odd)


def sums_kernel(moments0, moments1, moments2, sums):
    parts = [
        moments0[...], moments1[pl.ds(0, 8), :], moments1[pl.ds(8, 8), :], *(moments2[pl.ds(8 * k, 8), :] for k in range(3))
    ]
    lane = lax.broadcasted_iota(jnp.int32, (1, LANES), 1)
    line = jnp.zeros((1, LANES), jnp.float32)
    for k, part in enumerate(parts):
        total = jnp.sum(jnp.sum(part, 0, keepdims=True), 1, keepdims=True)
        line = jnp.where(lane == k, total, line)
    sums[...] = jnp.broadcast_to(line[None], sums.shape)


def recurrence(moments):
    moments = moments[:5] + [moments[5] - moments[4]]
    zero = jnp.zeros_like(moments[0])
    one = zero + 1.0

    def form(left, right, shift):
        total = zero
        for i in range(3):
            for j in range(3):
                if left[i] is not None and right[j] is not None:
                    entry = moments[i + j]
                    if shift:
                        entry = entry + moments[i + j + 1]
                    total = total + left[i] * right[j] * entry
        return total

    def ratio(top, bottom):
        fine = jnp.logical_and(bottom > 0.0, top > 0.0)
        return jnp.where(fine, top / jnp.where(fine, bottom, 1.0), 0.0)

    def add(left, scale, right):
        out = []
        for x, y in zip(left, right):
            if y is None:
                out.append(x)
            else:
                out.append(scale * y if x is None else x + scale * y)
        return out

    direction = [one, None, None, None]
    precond = [one, None, None, None]
    result = [None, None, None, None]
    norm = moments[0]
    for step in range(3):
        curve = form(direction, direction, True)
        length = ratio(norm, curve)
        result = add(result, length, direction)
        moved = add(direction, 1.0, [None] + direction[:3])
        if step == 0:
            precond = [jnp.where(curve > 0.0, moments[1] / curve, 1.0), -length, None, None]
        else:
            precond = add(precond, -length, moved)
        if step < 2:
            norm_next = form(precond, precond, False)
            direction = add(precond, ratio(norm_next, norm), direction)
            norm = norm_next
    return result[:3], precond


def to_slots(chosen, grid):
    total = None
    for part in parts_of(grid):
        term = lax.dot_general(
            chosen, part, (((1,), (1,)), ((), ())), preferred_element_type=jnp.float32
        )
        total = term if total is None else total + term
    return total


def solution_kernel(
    values0, values1, values2, sums, slot_rows, solution, precond_rows, solution_grid
):
    line = jnp.sum(sums[...], 0)[0:1]
    lane = lax.broadcasted_iota(jnp.int32, (1, LANES), 1)
    moments = [
        jnp.sum(jnp.where(lane == k, line, 0.0), 1, keepdims=True) for k in range(6)
    ]
    result, precond = recurrence(moments)
    result = [jnp.broadcast_to(entry, (8, LANES)) for entry in result]
    for k in range(4):
        precond_rows[pl.ds(8 * k, 8), :] = jnp.broadcast_to(precond[k], (8, LANES))
    for a in range(8):
        for b in range(8):
            rows = row(a, b)
            solution_grid[rows, :] = (
                result[0] * values0[rows, :]
                + result[1] * values1[rows, :]
                + result[2] * values2[rows, :]
            )
    chosen = selection(slot_rows).T.astype(jnp.bfloat16)
    solution[0, 0] = to_slots(chosen, solution_grid[...])


def last_kernel(
    before_image, even_x, odd_x, odd_y, even_y, diagonal, values0, values1, values2, precond_rows,
    slot_rows, residual, residual_grid,
):
    received = (even_x, odd_x, even_y, odd_y)
    precond = [precond_rows[pl.ds(8 * k, 8), :] for k in range(4)]
    for a in range(8):
        for b in range(8):
            rows = row(a, b)
            far = (
                precond[0] * values0[rows, :]
                + precond[1] * values1[rows, :]
                + (precond[2] - precond[3]) * values2[rows, :]
            )
            image = assembled(a, b, before_image, received, 0)
            residual_grid[rows, :] = diagonal[rows, :] * far + precond[3] * image
    chosen = selection(slot_rows).T.astype(jnp.bfloat16)
    residual[0, 0] = to_slots(chosen, residual_grid[...])


def call(kernel, name, shapes, scratch, *operands, outside=0, aliases=None):
    places = [pltpu.HBM] * outside + [pltpu.VMEM] * (len(operands) - outside)
    operands = [
        pltpu.with_memory_space_constraint(operand, place) if place == pltpu.HBM else operand
        for operand, place in zip(operands, places)
    ]
    return pl.pallas_call(
        kernel,
        out_shape=[jax.ShapeDtypeStruct(shape, jnp.float32) for shape in shapes],
        in_specs=[pl.BlockSpec(memory_space=place) for place in places],
        out_specs=[pl.BlockSpec(memory_space=pltpu.VMEM)] * len(shapes),
        scratch_shapes=scratch,
        input_output_aliases=aliases or {},
        compiler_params=pltpu.CompilerParams(vmem_limit_bytes=VMEM_BYTES),
        name=name,
    )(*operands)


def swapped(block, axis):
    extent = lax.axis_size(axis)
    even = [(i, i ^ 1) for i in range(extent)]
    odd = [(i, (((i + 1) ^ 1) - 1) % extent) for i in range(extent)]
    return lax.ppermute(block[0], axis, even), lax.ppermute(block[1], axis, odd)


def body(forcing, viscosity, mass_rate, slot_element):
    devices = lax.axis_size("gx") * lax.axis_size("yz")
    slots = slot_element[0]
    grid, face, tile = (POINTS, LANES), (64, LANES), (8, LANES)
    right, diagonal, spread, mass, out_x, *sent_y, corners, shifts, slot_rows = call(
        setup_kernel, "setup",
        [grid] * 4 + [(192, LANES), (200, LANES), (200, LANES), (32, LANES), (128, LANES)]
        + [tile],
        [
            pltpu.VMEM((1, LANES), jnp.int32),
            pltpu.VMEM((3, LANES, POINTS), jnp.float32),
            pltpu.SemaphoreType.DMA((4,)),
        ],
        slots, forcing, viscosity, mass_rate, outside=4,
    )
    received_x, received_y = swapped((out_x, out_x), "gx"), swapped(sent_y, "yz")[::-1]
    [shared] = call(corners_kernel, "corners", [(32, LANES)], [], corners, *received_y)
    received = (*received_x, *received_y, *swapped((shared, shared), "gx"))
    *early, outer, moments0, from_low, from_high, from_side, packed = call(
        early_kernel, "early", [grid] * 4 + [(208, LANES), tile] + [grid] * 3 + [face], [],
        right, diagonal, *received_x, *received_y, spread, mass,
    )
    diagonal, jacobi, values0, image, out_x, *sent_y, moments0 = call(
        first_kernel, "first", [grid] * 4 + [face] * 3 + [tile], [],
        right, diagonal, *received, spread, mass, shifts, outer, *early, moments0,
        aliases={12: 0, 13: 1, 14: 2, 15: 3},
    )
    fixed = (spread, mass, shifts, outer, from_low, from_high, from_side, packed)

    def advance(name, rows, image, before, out_x, sent_y):
        received = (*swapped((out_x, out_x), "gx"), *swapped(sent_y, "yz")[::-1])
        values, inner_image, moments = call(
            inner_kernel, "inner", [grid] * 2 + [(16, LANES)], [],
            image, diagonal, jacobi, before, spread, mass,
        )
        return call(
            outer_kernel, name, [grid] * 2 + [face] * 3 + [(rows, LANES)],
            [pltpu.VMEM(face, jnp.float32)] * 2,
            image, *received, diagonal, jacobi, before, *fixed, moments, values, inner_image,
            aliases={17: 0, 18: 1},
        )

    values1, image, out_x, *sent_y, moments1 = advance(
        "second", 16, image, values0, out_x, sent_y
    )
    values2, image, out_x, *sent_y, moments2 = advance(
        "third", 24, image, values1, out_x, sent_y
    )
    [sums] = call(sums_kernel, "sums", [(devices, 2, LANES)], [], moments0, moments1, moments2)
    sums = lax.all_to_all(sums, ("gx", "yz"), 0, 0)
    received = (*swapped((out_x, out_x), "gx"), *swapped(sent_y, "yz")[::-1])
    result, precond = call(
        solution_kernel, "solution", [forcing.shape, (32, LANES)],
        [pltpu.VMEM(grid, jnp.float32)],
        values0, values1, values2, sums, slot_rows,
    )
    [residual] = call(
        last_kernel, "last", [forcing.shape], [pltpu.VMEM(grid, jnp.float32)],
        image, *received, diagonal, values0, values1, values2, precond, slot_rows,
    )
    return result, residual


def solution(mesh):
    placed = (
        P("gx", "yz", None, None),
        P("gx", "yz", None, None),
        P("gx", "yz", None, None),
        P("gx", "yz", None),
    )
    return jax.shard_map(
        body,
        mesh=mesh,
        in_specs=placed,
        out_specs=(P("gx", "yz", None, None), P("gx", "yz", None, None)),
        check_vma=False,
    )
```

```python
import jax
import jax.numpy as jnp
import numpy as np
from jax import lax
from jax.experimental import pallas as pl
from jax.experimental.pallas import tpu as pltpu
from jax.sharding import PartitionSpec as P

EZ = 64
LANES = 128
HALF = 64
POINTS = 512
SPLIT = 2
VERTICAL = 4.0
VMEM_BYTES = 24 * 1024 * 1024


def legendre_rows(nodes, degree):
    rows = [nodes * 0.0 + 1.0, nodes]
    for order in range(2, degree + 1):
        rows.append(((2 * order - 1) * nodes * rows[-1] - (order - 1) * rows[-2]) / order)
    return np.stack(rows, 1)


def spectral_tables():
    degree = 7
    nodes = np.cos(np.pi * np.arange(degree + 1) / degree)
    for sweep in range(60):
        legendre = legendre_rows(nodes, degree)
        nodes = nodes - (nodes * legendre[:, degree] - legendre[:, degree - 1]) / (
            (degree + 1) * legendre[:, degree]
        )
    nodes = nodes[::-1].copy()
    top_values = legendre_rows(nodes, degree)[:, degree]
    weights = 2.0 / (degree * (degree + 1) * top_values**2)
    identity = np.eye(degree + 1)
    spacing = nodes[:, None] - nodes[None, :] + identity
    derivative = top_values[:, None] / top_values[None, :] / spacing * (1.0 - identity)
    corner_fix = np.zeros(degree + 1)
    corner_fix[0] = -degree * (degree + 1) / 4.0
    corner_fix[degree] = degree * (degree + 1) / 4.0
    derivative = derivative + identity * corner_fix[None, :]
    return (derivative, weights)


DERIVATIVE, WEIGHTS = spectral_tables()


def row(a, b):
    return pl.ds(64 * a + 8 * b, 8)


def across(a, c):
    return pl.ds(64 * a + c, 8, stride=8)


def along(matrix, lines, sign):
    evens = [lines[j] + lines[7 - j] for j in range(4)]
    odds = [lines[j] - lines[7 - j] for j in range(4)]
    out = [None] * 8
    for i in range(4):
        even = odd = None
        for j in range(4):
            even_term = evens[j] * float((matrix[i, j] + matrix[i, 7 - j]) / 2)
            odd_term = odds[j] * float((matrix[i, j] - matrix[i, 7 - j]) / 2)
            even = even_term if even is None else even + even_term
            odd = odd_term if odd is None else odd + odd_term
        out[i] = even + odd
        out[7 - i] = even - odd if sign > 0 else odd - even
    return out


def lane_index():
    return lax.broadcasted_iota(jnp.int32, (8, LANES), 1)


def sublane_index():
    return lax.broadcasted_iota(jnp.int32, (8, LANES), 0)


def join_vertical(low, high):
    layer = lane_index() % EZ
    new_low = low + jnp.where(layer > 0, pltpu.roll(high, 1, 1), 0.0)
    new_high = high + jnp.where(layer < EZ - 1, pltpu.roll(low, LANES - 1, 1), 0.0)
    return new_low, new_high


def packed_x(grid, b):
    return jnp.where(lane_index() < HALF, grid[row(0, b), :], grid[row(7, b), :])


def lowest_to_highest(low_side, to_even, to_odd, rows, low, high):
    to_even[rows, :] = jnp.where(low_side, low, high)
    to_odd[rows, :] = jnp.where(low_side, high, low)


def is_odd(axis):
    return lax.axis_index(axis) % 2 == 1


def ghost_x(from_even, from_odd, rows):
    odd = lax.axis_index("gx") % 2
    first = (lane_index() < HALF).astype(jnp.int32)
    return jnp.where(first != odd, from_even[rows, :], from_odd[rows, :])


def joined_x(a, low, high, ghost):
    first = lane_index() < HALF
    if a == 0:
        return low + pltpu.roll(jnp.where(first, high, ghost), HALF, 1)
    return high + pltpu.roll(jnp.where(first, ghost, low), HALF, 1)


def from_y(even_y, odd_y, b, rows):
    odd = is_odd("yz")
    pick = odd if b == 0 else jnp.logical_not(odd)
    return jnp.where(pick, even_y[rows, :], odd_y[rows, :])


def assembled(a, b, grid, received, field):
    even_x, odd_x, even_y, odd_y, *shared = received
    value = grid[row(a, b), :]
    if a in (0, 7):
        if shared and b in (0, 7):
            ghost = ghost_x(*shared, pl.ds(16 * field + 8 * (b // 7), 8))
        else:
            ghost = ghost_x(even_x, odd_x, pl.ds(64 * field + 8 * b, 8))
        value = joined_x(a, grid[row(0, b), :], grid[row(7, b), :], ghost)
    if b in (0, 7):
        rows = pl.ds(64 * field + 8 * a, 8)
        value = value + from_y(even_y, odd_y, b, rows)
    return value


def corners_kernel(corners, odd_y, even_y, shared):
    first = lane_index() < HALF
    for field in range(2):
        for side in range(2):
            rows = pl.ds(16 * field + 8 * side, 8)
            low = from_y(even_y, odd_y, 7 * side, pl.ds(64 * field, 8))
            high = from_y(even_y, odd_y, 7 * side, pl.ds(64 * field + 56, 8))
            shared[rows, :] = corners[rows, :] + jnp.where(first, low, high)


def selection(slots):
    elements = lax.broadcasted_iota(jnp.int32, (LANES, LANES), 0)
    return jnp.where(elements.astype(jnp.float32) == slots[pl.ds(0, 1), :], 1.0, 0.0)


def parts_of(values):
    parts = []
    for _ in range(SPLIT):
        parts.append(values.astype(jnp.bfloat16))
        values = values - parts[-1].astype(jnp.float32)
    return parts


def to_grid(chosen, values):
    parts = jnp.concatenate(parts_of(values), 0)
    picked = jnp.dot(
        jnp.concatenate([chosen.astype(jnp.bfloat16)] * SPLIT, 1),
        parts,
        preferred_element_type=jnp.float32,
    )
    return picked.T


def setup_kernel(
    slots, forcing, viscosity, mass_rate,
    right, diagonal, spread, mass, face_x, to_even, to_odd, corners, shifts, slot_rows,
    order, held, arrived,
):
    ordered = pltpu.make_async_copy(slots, order, arrived.at[3])
    copies = [
        pltpu.make_async_copy(source.at[0, 0], held.at[k], arrived.at[k])
        for k, source in enumerate((viscosity, mass_rate, forcing))
    ]
    for copy in [ordered] + copies:
        copy.start()
    point = sublane_index()
    last_weight = jnp.zeros((8, LANES), jnp.float32)
    for c in range(8):
        last_weight = jnp.where(point == c, float(WEIGHTS[c]), last_weight)
    ordered.wait()
    slot_rows[...] = jnp.broadcast_to(order[...].astype(jnp.float32), slot_rows.shape)
    chosen = selection(slot_rows)
    for copy in copies:
        copy.wait()
    spread[...] = to_grid(chosen, held[0])
    mass[...] = to_grid(chosen, held[1])
    for a in range(8):
        for b in range(8):
            weight = last_weight * float(WEIGHTS[a] * WEIGHTS[b])
            spread[row(a, b), :] *= weight
            mass[row(a, b), :] *= weight
    right[...] = to_grid(chosen, held[2])
    squares = (DERIVATIVE * DERIVATIVE).T
    for b in range(8):
        lines = along(squares, [spread[row(a, b), :] for a in range(8)], 1)
        for a in range(8):
            diagonal[row(a, b), :] = lines[a] + mass[row(a, b), :]
    for a in range(8):
        lines = along(squares, [spread[row(a, b), :] for b in range(8)], 1)
        for b in range(8):
            diagonal[row(a, b), :] += lines[b]
    for a in range(8):
        lines = along(VERTICAL * squares, [spread[across(a, c), :] for c in range(8)], 1)
        lines = [lines[c] + diagonal[across(a, c), :] for c in range(8)]
        lines[0], lines[7] = join_vertical(lines[0], lines[7])
        for c in range(8):
            diagonal[across(a, c), :] = lines[c]
        low, high = join_vertical(right[across(a, 0), :], right[across(a, 7), :])
        right[across(a, 0), :] = low
        right[across(a, 7), :] = high
    odd = is_odd("yz")
    for field, source in enumerate((right, diagonal, spread)):
        for b in range(8):
            face_x[pl.ds(64 * field + 8 * b, 8), :] = packed_x(source, b)
        faces = []
        for side in range(2):
            part = [source[row(a, 7 * side), :] for a in range(8)]
            if field < 2:
                corners[pl.ds(16 * field + 8 * side, 8), :] = packed_x(source, 7 * side)
                part = joined_inside(part, 0.0)
            faces.append(part)
        for a in range(8):
            rows = pl.ds(64 * field + 8 * a, 8)
            lowest_to_highest(odd, to_even, to_odd, rows, faces[0][a], faces[1][a])
    rows = pl.ds(192, 8)
    lowest_to_highest(odd, to_even, to_odd, rows, packed_x(mass, 0), packed_x(mass, 7))
    for k in range(8):
        along_shift = back_shift = jnp.zeros((8, LANES), jnp.float32)
        for c in range(8):
            other = (c + k) % 8
            along_shift = jnp.where(point == c, float(DERIVATIVE[c, other]), along_shift)
            back_shift = jnp.where(
                point == c, float(VERTICAL * DERIVATIVE[other, c]), back_shift
            )
        shifts[pl.ds(8 * k, 8), :] = along_shift
        shifts[pl.ds(64 + 8 * k, 8), :] = back_shift


def join_vertical_packed(value):
    layer, point = lane_index() % EZ, sublane_index()
    from_below = pltpu.roll(pltpu.roll(value, 1, 0), 1, 1)
    from_above = pltpu.roll(pltpu.roll(value, 7, 0), LANES - 1, 1)
    below = jnp.logical_and(point == 0, layer > 0)
    above = jnp.logical_and(point == 7, layer < EZ - 1)
    return value + jnp.where(below, from_below, jnp.where(above, from_above, 0.0))


def shifted_sum(shifts, start, value):
    total = shifts[pl.ds(start, 8), :] * value
    for k in range(1, 8):
        total = total + shifts[pl.ds(start + 8 * k, 8), :] * pltpu.roll(value, 8 - k, 0)
    return total


def end_row(lines, end):
    total = None
    for q in range(8):
        term = lines[q] * float(DERIVATIVE[q, end])
        total = term if total is None else total + term
    return total


def corner_shares(values, outer, shifts):
    first = lane_index() < HALF
    lines = [packed_x(values, b) for b in range(8)]
    slopes = along(DERIVATIVE, lines, -1)
    slopes = [slopes[q] * outer[pl.ds(8 * q, 8), :] for q in range(8)]
    for_y = [end_row(slopes, 0), end_row(slopes, 7)]
    for_x = []
    for side in range(2):
        base = 64 + 72 * side
        spread = [outer[pl.ds(base + 8 * a, 8), :] for a in range(8)]
        slopes = along(DERIVATIVE, [values[row(a, 7 * side), :] for a in range(8)], -1)
        slopes = [slopes[q] * spread[q] for q in range(8)]
        share = jnp.where(first, end_row(slopes, 0), end_row(slopes, 7))
        corner = lines[7 * side]
        slope = shifted_sum(shifts, 0, corner) * jnp.where(first, spread[0], spread[7])
        share = share + shifted_sum(shifts, 64, slope) + outer[pl.ds(base + 64, 8), :] * corner
        for_x.append(share)
    return [join_vertical_packed(share) for share in for_x], [
        join_vertical_packed(share) for share in for_y
    ]


def joined_inside(lines, share):
    first = lane_index() < HALF
    low, high = lines[0], lines[7]
    new_low = low + jnp.where(first, share, pltpu.roll(high, HALF, 1))
    new_high = high + jnp.where(first, pltpu.roll(low, HALF, 1), share)
    return [new_low] + lines[1:7] + [new_high]


def send_faces(image, values, outer, shifts, face_x, to_even, to_odd):
    for_x, for_y = corner_shares(values, outer, shifts)
    odd = is_odd("yz")
    for b in range(8):
        face = packed_x(image, b)
        if b in (0, 7):
            face = face + for_x[b // 7]
        face_x[pl.ds(8 * b, 8), :] = face
    faces = []
    for side in range(2):
        part = [image[row(a, 7 * side), :] for a in range(8)]
        part = joined_inside(part, for_y[side])
        faces.append(part)
    for a in range(8):
        lowest_to_highest(odd, to_even, to_odd, pl.ds(8 * a, 8), faces[0][a], faces[1][a])


def streamwise(lines, b, spread, mass):
    slopes = along(DERIVATIVE, lines, -1)
    back = along(DERIVATIVE.T, [slopes[a] * spread[row(a, b), :] for a in range(8)], -1)
    return [back[a] + mass[row(a, b), :] * lines[a] for a in range(8)]


def join_layers(image):
    for a in range(8):
        low, high = join_vertical(image[across(a, 0), :], image[across(a, 7), :])
        image[across(a, 0), :] = low
        image[across(a, 7), :] = high


def vertical_part(lines, spread):
    slopes = along(DERIVATIVE, lines, -1)
    return along(VERTICAL * DERIVATIVE.T, [slopes[c] * spread[c] for c in range(8)], -1)


def operate(values, spread, image):
    for a in range(8):
        slopes = along(DERIVATIVE, [values[row(a, b), :] for b in range(8)], -1)
        back = along(DERIVATIVE.T, [slopes[b] * spread[row(a, b), :] for b in range(8)], -1)
        for b in range(8):
            image[row(a, b), :] += back[b]
    for a in range(8):
        back = vertical_part(
            [values[across(a, c), :] for c in range(8)],
            [spread[across(a, c), :] for c in range(8)],
        )
        for c in range(8):
            image[across(a, c), :] += back[c]


def weighted(sums):
    layer, point = lane_index() % EZ, sublane_index()
    below = jnp.logical_and(point == 0, layer > 0)
    above = jnp.logical_and(point == 7, layer < EZ - 1)
    shared = jnp.where(jnp.logical_or(below, above), 0.5, 1.0)
    return (sums[0] + 0.5 * sums[1] + 0.25 * sums[2]) * shared


def ends(a, b):
    return int(a in (0, 7)) + int(b in (0, 7))


def early_kernel(
    right, diagonal, even_x, odd_x, odd_y, even_y, spread, mass,
    whole_diagonal, jacobi, values, image, outer, moments, from_low, from_high, from_side, packed,
):
    received = (even_x, odd_x, even_y, odd_y)
    first = lane_index() < HALF
    sums = [jnp.zeros((8, LANES), jnp.float32)] * 3
    for b in range(8):
        lines = []
        for a in range(8):
            source = assembled(a, b, right, received, 0)
            scale = assembled(a, b, diagonal, received, 1)
            inverse = 1.0 / scale
            value = source * inverse
            if ends(a, b) == 2:
                value = jnp.where(first, 0.0, value) if a == 0 else jnp.where(first, value, 0.0)
            whole_diagonal[row(a, b), :] = scale
            jacobi[row(a, b), :] = inverse
            values[row(a, b), :] = value
            sums[ends(a, b)] = sums[ends(a, b)] + source * value
            lines.append(value)
        back = streamwise(lines, b, spread, mass)
        for a in range(8):
            image[row(a, b), :] = back[a]
    moments[...] = weighted(sums)
    for b in range(8):
        outer[pl.ds(8 * b, 8), :] = pltpu.roll(
            ghost_x(even_x, odd_x, pl.ds(128 + 8 * b, 8)), HALF, 1
        )
    for side in range(2):
        for k in range(9):
            outer[pl.ds(64 + 72 * side + 8 * k, 8), :] = from_y(
                even_y, odd_y, 7 * side, pl.ds(128 + 8 * k, 8)
            )
    operate(values, spread, image)
    join_layers(image)
    for a in range(8):
        for end, out in ((0, from_low), (7, from_high)):
            slopes = [spread[row(a, q), :] * float(DERIVATIVE[q, end]) for q in range(8)]
            back = along(DERIVATIVE.T, slopes, -1)
            for b in range(8):
                out[row(a, b), :] = back[b]
    for b in range(8):
        packed[pl.ds(8 * b, 8), :] = packed_x(spread, b)
        packed[pl.ds(64 + 8 * b, 8), :] = spread[row(b, 0), :]
        packed[pl.ds(128 + 8 * b, 8), :] = spread[row(b, 7), :]
        back = along(
            DERIVATIVE.T, [spread[row(q, b), :] * outer_slope(q) for q in range(8)], -1
        )
        for a in range(8):
            from_side[row(a, b), :] = back[a]


def outer_slope(q):
    first = lane_index() < HALF
    return jnp.where(first, float(DERIVATIVE[q, 0]), float(DERIVATIVE[q, 7]))


def add_packed(grid, b, value):
    first = lane_index() < HALF
    grid[row(0, b), :] += jnp.where(first, value, 0.0)
    grid[row(7, b), :] += jnp.where(first, 0.0, value)


def first_kernel(
    right, diagonal, even_x, odd_x, odd_y, even_y, even_shared, odd_shared, spread, mass, shifts,
    outer, early_diagonal, early_jacobi, early_values, early_image, early_moments,
    whole_diagonal, jacobi, values, image, face_x, to_even, to_odd, moments,
):
    received = (even_x, odd_x, even_y, odd_y, even_shared, odd_shared)
    first = lane_index() < HALF
    corners = []
    total = jnp.zeros((8, LANES), jnp.float32)
    for b in (0, 7):
        packed = []
        for a in (0, 7):
            source = assembled(a, b, right, received, 0)
            scale = assembled(a, b, diagonal, received, 1)
            inverse = 1.0 / scale
            value = source * inverse
            whole_diagonal[row(a, b), :] = scale
            jacobi[row(a, b), :] = inverse
            values[row(a, b), :] = value
            packed.append((value, source * value))
        corners.append(jnp.where(first, packed[0][0], packed[1][0]))
        total = total + jnp.where(first, packed[0][1], packed[1][1])
    zero = jnp.zeros((8, LANES), jnp.float32)
    moments[...] = early_moments[...] + weighted([zero, zero, total])
    for side, corner in enumerate(corners):
        b = 7 * side
        slopes = []
        for q in range(8):
            slopes.append(spread[row(q, b), :] * (outer_slope(q) * corner))
        back = along(DERIVATIVE.T, slopes, -1)
        for a in range(8):
            image[row(a, b), :] += join_vertical_packed(back[a])
    slopes = []
    for q in range(8):
        slope = corners[0] * float(DERIVATIVE[q, 0]) + corners[1] * float(DERIVATIVE[q, 7])
        slopes.append(packed_x(spread, q) * slope)
    back = along(DERIVATIVE.T, slopes, -1)
    for side, corner in enumerate(corners):
        b = 7 * side
        slope = shifted_sum(shifts, 0, corner) * packed_x(spread, b)
        back[b] = back[b] + shifted_sum(shifts, 64, slope) + packed_x(mass, b) * corner
    for b in range(8):
        add_packed(image, b, join_vertical_packed(back[b]))
    send_faces(image, values, outer, shifts, face_x, to_even, to_odd)


def inner_kernel(
    before_image, diagonal, jacobi, before, spread, mass, values, image, moments
):
    first = lane_index() < HALF
    zero = jnp.zeros((8, LANES), jnp.float32)
    cross, square = [zero] * 3, [zero] * 3
    for b in range(8):
        lines = []
        for a in range(8):
            if b in (0, 7):
                values[row(a, b), :] = zero
                image[row(a, b), :] = zero
                continue
            joined = before_image[row(a, b), :]
            if a in (0, 7):
                joined = joined_x(a, before_image[row(0, b), :], before_image[row(7, b), :], 0.0)
            old = before[row(a, b), :]
            scaled = joined - diagonal[row(a, b), :] * old
            if a in (0, 7):
                scaled = jnp.where(first, 0.0, scaled) if a == 0 else jnp.where(first, scaled, 0.0)
            value = scaled * jacobi[row(a, b), :]
            values[row(a, b), :] = value
            kind = ends(a, b)
            cross[kind] = cross[kind] + scaled * old
            square[kind] = square[kind] + scaled * value
            lines.append(value)
        if lines:
            back = streamwise(lines, b, spread, mass)
            for a in range(8):
                image[row(a, b), :] = back[a]
    moments[pl.ds(0, 8), :] = weighted(cross)
    moments[pl.ds(8, 8), :] = weighted(square)
    operate(values, spread, image)


def outer_kernel(
    before_image, even_x, odd_x, odd_y, even_y, diagonal, jacobi, before, spread, mass, shifts,
    outer, from_low, from_high, from_side, packed, inner_moments, inner_values, inner_image,
    values, image, face_x, to_even, to_odd, moments, face, face_back,
):
    received = (even_x, odd_x, even_y, odd_y)
    first = lane_index() < HALF
    zero = jnp.zeros((8, LANES), jnp.float32)
    cross, square = [zero] * 3, [zero] * 3
    sides = []
    for b in (0, 7):
        lines = []
        for a in range(8):
            old = before[row(a, b), :]
            scaled = assembled(a, b, before_image, received, 0) - diagonal[row(a, b), :] * old
            value = scaled * jacobi[row(a, b), :]
            values[row(a, b), :] = value
            kind = ends(a, b)
            cross[kind] = cross[kind] + scaled * old
            square[kind] = square[kind] + scaled * value
            lines.append(value)
        sides.append(lines)
    lines = [zero] * 8
    for b in range(1, 7):
        old = packed_x(before, b)
        ghost = pltpu.roll(ghost_x(even_x, odd_x, pl.ds(8 * b, 8)), HALF, 1)
        scaled = packed_x(before_image, b) + ghost - packed_x(diagonal, b) * old
        lines[b] = scaled * packed_x(jacobi, b)
        add_packed(values, b, lines[b])
        cross[1] = cross[1] + scaled * old
        square[1] = square[1] + scaled * lines[b]
    for group, part in enumerate((lines, *sides)):
        base = 64 * group
        for k in range(8):
            face[pl.ds(base + 8 * k, 8), :] = part[k]
        back = vertical_part(
            [face[pl.ds(base + c, 8, stride=8), :] for c in range(8)],
            [packed[pl.ds(base + c, 8, stride=8), :] for c in range(8)],
        )
        for c in range(8):
            face_back[pl.ds(base + c, 8, stride=8), :] = back[c]
    slopes = along(DERIVATIVE, lines, -1)
    back = along(DERIVATIVE.T, [slopes[q] * packed[pl.ds(8 * q, 8), :] for q in range(8)], -1)
    shares = [back[b] + face_back[pl.ds(8 * b, 8), :] for b in range(8)]
    for b in range(1, 7):
        shares[b] = shares[b] + packed_x(mass, b) * lines[b]
    ends_back = [streamwise(sides[k], 7 * k, spread, mass) for k in range(2)]
    energy = [zero] * 4
    for a in range(8):
        for b in range(8):
            rows = row(a, b)
            share = from_low[rows, :] * sides[0][a] + from_high[rows, :] * sides[1][a]
            if b in (0, 7):
                side = b // 7
                share = share + ends_back[side][a]
                share = share + face_back[pl.ds(64 + 64 * side + 8 * a, 8), :]
            else:
                share = share + from_side[rows, :] * lines[b]
            if a == 0:
                share = share + jnp.where(first, shares[b], 0.0)
            if a == 7:
                share = share + jnp.where(first, 0.0, shares[b])
            share = image[rows, :] + share
            image[rows, :] = share
            if moments.shape[0] > 16:
                energy[b % 4] = energy[b % 4] + values[rows, :] * share
    moments[pl.ds(0, 8), :] = inner_moments[pl.ds(0, 8), :] + weighted(cross)
    moments[pl.ds(8, 8), :] = inner_moments[pl.ds(8, 8), :] + weighted(square)
    if moments.shape[0] > 16:
        moments[pl.ds(16, 8), :] = (energy[0] + energy[1]) + (energy[2] + energy[3])
    join_layers(image)
    send_faces(image, values, outer, shifts, face_x, to_even, to_odd)


def sums_kernel(moments0, moments1, moments2, sums):
    parts = [
        moments0[...], moments1[pl.ds(0, 8), :], moments1[pl.ds(8, 8), :], *(moments2[pl.ds(8 * k, 8), :] for k in range(3))
    ]
    lane = lax.broadcasted_iota(jnp.int32, (1, LANES), 1)
    line = jnp.zeros((1, LANES), jnp.float32)
    for k, part in enumerate(parts):
        total = jnp.sum(jnp.sum(part, 0, keepdims=True), 1, keepdims=True)
        line = jnp.where(lane == k, total, line)
    sums[...] = jnp.broadcast_to(line[None], sums.shape)


def recurrence(moments):
    moments = moments[:5] + [moments[5] - moments[4]]
    zero = jnp.zeros_like(moments[0])
    one = zero + 1.0

    def form(left, right, shift):
        total = zero
        for i in range(3):
            for j in range(3):
                if left[i] is not None and right[j] is not None:
                    entry = moments[i + j]
                    if shift:
                        entry = entry + moments[i + j + 1]
                    total = total + left[i] * right[j] * entry
        return total

    def ratio(top, bottom):
        fine = jnp.logical_and(bottom > 0.0, top > 0.0)
        return jnp.where(fine, top / jnp.where(fine, bottom, 1.0), 0.0)

    def add(left, scale, right):
        out = []
        for x, y in zip(left, right):
            if y is None:
                out.append(x)
            else:
                out.append(scale * y if x is None else x + scale * y)
        return out

    direction = [one, None, None, None]
    precond = [one, None, None, None]
    result = [None, None, None, None]
    norm = moments[0]
    for step in range(3):
        curve = form(direction, direction, True)
        length = ratio(norm, curve)
        result = add(result, length, direction)
        moved = add(direction, 1.0, [None] + direction[:3])
        if step == 0:
            precond = [jnp.where(curve > 0.0, moments[1] / curve, 1.0), -length, None, None]
        else:
            precond = add(precond, -length, moved)
        if step < 2:
            norm_next = form(precond, precond, False)
            direction = add(precond, ratio(norm_next, norm), direction)
            norm = norm_next
    return result[:3], precond


def to_slots(chosen, grid):
    total = None
    for part in parts_of(grid):
        term = lax.dot_general(
            chosen, part, (((1,), (1,)), ((), ())), preferred_element_type=jnp.float32
        )
        total = term if total is None else total + term
    return total


def solution_kernel(
    values0, values1, values2, sums, slot_rows, solution, precond_rows, solution_grid
):
    line = jnp.sum(sums[...], 0)[0:1]
    lane = lax.broadcasted_iota(jnp.int32, (1, LANES), 1)
    moments = [
        jnp.sum(jnp.where(lane == k, line, 0.0), 1, keepdims=True) for k in range(6)
    ]
    result, precond = recurrence(moments)
    result = [jnp.broadcast_to(entry, (8, LANES)) for entry in result]
    for k in range(4):
        precond_rows[pl.ds(8 * k, 8), :] = jnp.broadcast_to(precond[k], (8, LANES))
    for a in range(8):
        for b in range(8):
            rows = row(a, b)
            solution_grid[rows, :] = (
                result[0] * values0[rows, :]
                + result[1] * values1[rows, :]
                + result[2] * values2[rows, :]
            )
    chosen = selection(slot_rows).T.astype(jnp.bfloat16)
    solution[0, 0] = to_slots(chosen, solution_grid[...])


def last_kernel(
    before_image, even_x, odd_x, odd_y, even_y, diagonal, values0, values1, values2, precond_rows,
    slot_rows, residual, residual_grid,
):
    received = (even_x, odd_x, even_y, odd_y)
    precond = [precond_rows[pl.ds(8 * k, 8), :] for k in range(4)]
    for a in range(8):
        for b in range(8):
            rows = row(a, b)
            far = (
                precond[0] * values0[rows, :]
                + precond[1] * values1[rows, :]
                + (precond[2] - precond[3]) * values2[rows, :]
            )
            image = assembled(a, b, before_image, received, 0)
            residual_grid[rows, :] = diagonal[rows, :] * far + precond[3] * image
    chosen = selection(slot_rows).T.astype(jnp.bfloat16)
    residual[0, 0] = to_slots(chosen, residual_grid[...])


def call(kernel, name, shapes, scratch, *operands, outside=0, aliases=None):
    places = [pltpu.HBM] * outside + [pltpu.VMEM] * (len(operands) - outside)
    operands = [
        pltpu.with_memory_space_constraint(operand, place) if place == pltpu.HBM else operand
        for operand, place in zip(operands, places)
    ]
    return pl.pallas_call(
        kernel,
        out_shape=[jax.ShapeDtypeStruct(shape, jnp.float32) for shape in shapes],
        in_specs=[pl.BlockSpec(memory_space=place) for place in places],
        out_specs=[pl.BlockSpec(memory_space=pltpu.VMEM)] * len(shapes),
        scratch_shapes=scratch,
        input_output_aliases=aliases or {},
        compiler_params=pltpu.CompilerParams(vmem_limit_bytes=VMEM_BYTES),
        name=name,
    )(*operands)


def swapped(block, axis):
    extent = lax.axis_size(axis)
    even = [(i, i ^ 1) for i in range(extent)]
    odd = [(i, (((i + 1) ^ 1) - 1) % extent) for i in range(extent)]
    return lax.ppermute(block[0], axis, even), lax.ppermute(block[1], axis, odd)


def body(forcing, viscosity, mass_rate, slot_element):
    devices = lax.axis_size("gx") * lax.axis_size("yz")
    slots = slot_element[0]
    grid, face, tile = (POINTS, LANES), (64, LANES), (8, LANES)
    right, diagonal, spread, mass, out_x, *sent_y, corners, shifts, slot_rows = call(
        setup_kernel, "setup",
        [grid] * 4 + [(192, LANES), (200, LANES), (200, LANES), (32, LANES), (128, LANES)]
        + [tile],
        [
            pltpu.VMEM((1, LANES), jnp.int32),
            pltpu.VMEM((3, LANES, POINTS), jnp.float32),
            pltpu.SemaphoreType.DMA((4,)),
        ],
        slots, forcing, viscosity, mass_rate, outside=4,
    )
    received_x, received_y = swapped((out_x, out_x), "gx"), swapped(sent_y, "yz")[::-1]
    [shared] = call(corners_kernel, "corners", [(32, LANES)], [], corners, *received_y)
    received = (*received_x, *received_y, *swapped((shared, shared), "gx"))
    *early, outer, moments0, from_low, from_high, from_side, packed = call(
        early_kernel, "early", [grid] * 4 + [(208, LANES), tile] + [grid] * 3 + [(192, LANES)], [],
        right, diagonal, *received_x, *received_y, spread, mass,
    )
    diagonal, jacobi, values0, image, out_x, *sent_y, moments0 = call(
        first_kernel, "first", [grid] * 4 + [face] * 3 + [tile], [],
        right, diagonal, *received, spread, mass, shifts, outer, *early, moments0,
        aliases={12: 0, 13: 1, 14: 2, 15: 3},
    )
    fixed = (spread, mass, shifts, outer, from_low, from_high, from_side, packed)

    def advance(name, rows, image, before, out_x, sent_y):
        received = (*swapped((out_x, out_x), "gx"), *swapped(sent_y, "yz")[::-1])
        values, inner_image, moments = call(
            inner_kernel, "inner", [grid] * 2 + [(16, LANES)], [],
            image, diagonal, jacobi, before, spread, mass,
        )
        return call(
            outer_kernel, name, [grid] * 2 + [face] * 3 + [(rows, LANES)],
            [pltpu.VMEM((192, LANES), jnp.float32)] * 2,
            image, *received, diagonal, jacobi, before, *fixed, moments, values, inner_image,
            aliases={17: 0, 18: 1},
        )

    values1, image, out_x, *sent_y, moments1 = advance(
        "second", 16, image, values0, out_x, sent_y
    )
    values2, image, out_x, *sent_y, moments2 = advance(
        "third", 24, image, values1, out_x, sent_y
    )
    [sums] = call(sums_kernel, "sums", [(devices, 2, LANES)], [], moments0, moments1, moments2)
    sums = lax.all_to_all(sums, ("gx", "yz"), 0, 0)
    received = (*swapped((out_x, out_x), "gx"), *swapped(sent_y, "yz")[::-1])
    result, precond = call(
        solution_kernel, "solution", [forcing.shape, (32, LANES)],
        [pltpu.VMEM(grid, jnp.float32)],
        values0, values1, values2, sums, slot_rows,
    )
    [residual] = call(
        last_kernel, "last", [forcing.shape], [pltpu.VMEM(grid, jnp.float32)],
        image, *received, diagonal, values0, values1, values2, precond, slot_rows,
    )
    return result, residual


def solution(mesh):
    placed = (
        P("gx", "yz", None, None),
        P("gx", "yz", None, None),
        P("gx", "yz", None, None),
        P("gx", "yz", None),
    )
    return jax.shard_map(
        body,
        mesh=mesh,
        in_specs=placed,
        out_specs=(P("gx", "yz", None, None), P("gx", "yz", None, None)),
        check_vma=False,
    )
```

```python
import jax
import jax.numpy as jnp
import numpy as np
from jax import lax
from jax.experimental import pallas as pl
from jax.experimental.pallas import tpu as pltpu
from jax.sharding import PartitionSpec as P

EZ = 64
LANES = 128
HALF = 64
POINTS = 512
SPLIT = 2
VERTICAL = 4.0
VMEM_BYTES = 24 * 1024 * 1024


def legendre_rows(nodes, degree):
    rows = [nodes * 0.0 + 1.0, nodes]
    for order in range(2, degree + 1):
        rows.append(((2 * order - 1) * nodes * rows[-1] - (order - 1) * rows[-2]) / order)
    return np.stack(rows, 1)


def spectral_tables():
    degree = 7
    nodes = np.cos(np.pi * np.arange(degree + 1) / degree)
    for sweep in range(60):
        legendre = legendre_rows(nodes, degree)
        nodes = nodes - (nodes * legendre[:, degree] - legendre[:, degree - 1]) / (
            (degree + 1) * legendre[:, degree]
        )
    nodes = nodes[::-1].copy()
    top_values = legendre_rows(nodes, degree)[:, degree]
    weights = 2.0 / (degree * (degree + 1) * top_values**2)
    identity = np.eye(degree + 1)
    spacing = nodes[:, None] - nodes[None, :] + identity
    derivative = top_values[:, None] / top_values[None, :] / spacing * (1.0 - identity)
    corner_fix = np.zeros(degree + 1)
    corner_fix[0] = -degree * (degree + 1) / 4.0
    corner_fix[degree] = degree * (degree + 1) / 4.0
    derivative = derivative + identity * corner_fix[None, :]
    return (derivative, weights)


DERIVATIVE, WEIGHTS = spectral_tables()


def row(a, b):
    return pl.ds(64 * a + 8 * b, 8)


def across(a, c):
    return pl.ds(64 * a + c, 8, stride=8)


def along(matrix, lines, sign):
    evens = [lines[j] + lines[7 - j] for j in range(4)]
    odds = [lines[j] - lines[7 - j] for j in range(4)]
    out = [None] * 8
    for i in range(4):
        even = odd = None
        for j in range(4):
            even_term = evens[j] * float((matrix[i, j] + matrix[i, 7 - j]) / 2)
            odd_term = odds[j] * float((matrix[i, j] - matrix[i, 7 - j]) / 2)
            even = even_term if even is None else even + even_term
            odd = odd_term if odd is None else odd + odd_term
        out[i] = even + odd
        out[7 - i] = even - odd if sign > 0 else odd - even
    return out


def lane_index():
    return lax.broadcasted_iota(jnp.int32, (8, LANES), 1)


def sublane_index():
    return lax.broadcasted_iota(jnp.int32, (8, LANES), 0)


def join_vertical(low, high):
    layer = lane_index() % EZ
    new_low = low + jnp.where(layer > 0, pltpu.roll(high, 1, 1), 0.0)
    new_high = high + jnp.where(layer < EZ - 1, pltpu.roll(low, LANES - 1, 1), 0.0)
    return new_low, new_high


def packed_x(grid, b):
    return jnp.where(lane_index() < HALF, grid[row(0, b), :], grid[row(7, b), :])


def lowest_to_highest(low_side, to_even, to_odd, rows, low, high):
    to_even[rows, :] = jnp.where(low_side, low, high)
    to_odd[rows, :] = jnp.where(low_side, high, low)


def is_odd(axis):
    return lax.axis_index(axis) % 2 == 1


def ghost_x(from_even, from_odd, rows):
    odd = lax.axis_index("gx") % 2
    first = (lane_index() < HALF).astype(jnp.int32)
    return jnp.where(first != odd, from_even[rows, :], from_odd[rows, :])


def joined_x(a, low, high, ghost):
    first = lane_index() < HALF
    if a == 0:
        return low + pltpu.roll(jnp.where(first, high, ghost), HALF, 1)
    return high + pltpu.roll(jnp.where(first, ghost, low), HALF, 1)


def from_y(even_y, odd_y, b, rows):
    odd = is_odd("yz")
    pick = odd if b == 0 else jnp.logical_not(odd)
    return jnp.where(pick, even_y[rows, :], odd_y[rows, :])


def assembled(a, b, grid, received, field):
    even_x, odd_x, even_y, odd_y, *shared = received
    value = grid[row(a, b), :]
    if a in (0, 7):
        if shared and b in (0, 7):
            ghost = ghost_x(*shared, pl.ds(16 * field + 8 * (b // 7), 8))
        else:
            ghost = ghost_x(even_x, odd_x, pl.ds(64 * field + 8 * b, 8))
        value = joined_x(a, grid[row(0, b), :], grid[row(7, b), :], ghost)
    if b in (0, 7):
        rows = pl.ds(64 * field + 8 * a, 8)
        value = value + from_y(even_y, odd_y, b, rows)
    return value


def corners_kernel(corners, odd_y, even_y, shared):
    first = lane_index() < HALF
    for field in range(2):
        for side in range(2):
            rows = pl.ds(16 * field + 8 * side, 8)
            low = from_y(even_y, odd_y, 7 * side, pl.ds(64 * field, 8))
            high = from_y(even_y, odd_y, 7 * side, pl.ds(64 * field + 56, 8))
            shared[rows, :] = corners[rows, :] + jnp.where(first, low, high)


def selection(slots):
    elements = lax.broadcasted_iota(jnp.int32, (LANES, LANES), 0)
    return jnp.where(elements.astype(jnp.float32) == slots[pl.ds(0, 1), :], 1.0, 0.0)


def parts_of(values):
    parts = []
    for _ in range(SPLIT):
        parts.append(values.astype(jnp.bfloat16))
        values = values - parts[-1].astype(jnp.float32)
    return parts


def to_grid(chosen, values):
    parts = jnp.concatenate(parts_of(values), 0)
    picked = jnp.dot(
        jnp.concatenate([chosen.astype(jnp.bfloat16)] * SPLIT, 1),
        parts,
        preferred_element_type=jnp.float32,
    )
    return picked.T


def setup_kernel(
    slots, forcing, viscosity, mass_rate,
    right, diagonal, spread, mass, face_x, to_even, to_odd, corners, shifts, slot_rows,
    order, held, arrived,
):
    ordered = pltpu.make_async_copy(slots, order, arrived.at[3])
    copies = [
        pltpu.make_async_copy(source.at[0, 0], held.at[k], arrived.at[k])
        for k, source in enumerate((viscosity, mass_rate, forcing))
    ]
    for copy in [ordered] + copies:
        copy.start()
    point = sublane_index()
    last_weight = jnp.zeros((8, LANES), jnp.float32)
    for c in range(8):
        last_weight = jnp.where(point == c, float(WEIGHTS[c]), last_weight)
    ordered.wait()
    slot_rows[...] = jnp.broadcast_to(order[...].astype(jnp.float32), slot_rows.shape)
    chosen = selection(slot_rows)
    for copy in copies:
        copy.wait()
    spread[...] = to_grid(chosen, held[0])
    mass[...] = to_grid(chosen, held[1])
    for a in range(8):
        for b in range(8):
            weight = last_weight * float(WEIGHTS[a] * WEIGHTS[b])
            spread[row(a, b), :] *= weight
            mass[row(a, b), :] *= weight
    right[...] = to_grid(chosen, held[2])
    squares = (DERIVATIVE * DERIVATIVE).T
    for b in range(8):
        lines = along(squares, [spread[row(a, b), :] for a in range(8)], 1)
        for a in range(8):
            diagonal[row(a, b), :] = lines[a] + mass[row(a, b), :]
    for a in range(8):
        lines = along(squares, [spread[row(a, b), :] for b in range(8)], 1)
        for b in range(8):
            diagonal[row(a, b), :] += lines[b]
    for a in range(8):
        lines = along(VERTICAL * squares, [spread[across(a, c), :] for c in range(8)], 1)
        lines = [lines[c] + diagonal[across(a, c), :] for c in range(8)]
        lines[0], lines[7] = join_vertical(lines[0], lines[7])
        for c in range(8):
            diagonal[across(a, c), :] = lines[c]
        low, high = join_vertical(right[across(a, 0), :], right[across(a, 7), :])
        right[across(a, 0), :] = low
        right[across(a, 7), :] = high
    odd = is_odd("yz")
    for field, source in enumerate((right, diagonal, spread)):
        for b in range(8):
            face_x[pl.ds(64 * field + 8 * b, 8), :] = packed_x(source, b)
        faces = []
        for side in range(2):
            part = [source[row(a, 7 * side), :] for a in range(8)]
            if field < 2:
                corners[pl.ds(16 * field + 8 * side, 8), :] = packed_x(source, 7 * side)
                part = joined_inside(part, 0.0)
            faces.append(part)
        for a in range(8):
            rows = pl.ds(64 * field + 8 * a, 8)
            lowest_to_highest(odd, to_even, to_odd, rows, faces[0][a], faces[1][a])
    rows = pl.ds(192, 8)
    lowest_to_highest(odd, to_even, to_odd, rows, packed_x(mass, 0), packed_x(mass, 7))
    for k in range(8):
        along_shift = back_shift = jnp.zeros((8, LANES), jnp.float32)
        for c in range(8):
            other = (c + k) % 8
            along_shift = jnp.where(point == c, float(DERIVATIVE[c, other]), along_shift)
            back_shift = jnp.where(
                point == c, float(VERTICAL * DERIVATIVE[other, c]), back_shift
            )
        shifts[pl.ds(8 * k, 8), :] = along_shift
        shifts[pl.ds(64 + 8 * k, 8), :] = back_shift


def join_vertical_packed(value):
    layer, point = lane_index() % EZ, sublane_index()
    from_below = pltpu.roll(pltpu.roll(value, 1, 0), 1, 1)
    from_above = pltpu.roll(pltpu.roll(value, 7, 0), LANES - 1, 1)
    below = jnp.logical_and(point == 0, layer > 0)
    above = jnp.logical_and(point == 7, layer < EZ - 1)
    return value + jnp.where(below, from_below, jnp.where(above, from_above, 0.0))


def shifted_sum(shifts, start, value):
    total = shifts[pl.ds(start, 8), :] * value
    for k in range(1, 8):
        total = total + shifts[pl.ds(start + 8 * k, 8), :] * pltpu.roll(value, 8 - k, 0)
    return total


def end_row(lines, end):
    total = None
    for q in range(8):
        term = lines[q] * float(DERIVATIVE[q, end])
        total = term if total is None else total + term
    return total


def corner_shares(values, outer, shifts):
    first = lane_index() < HALF
    lines = [packed_x(values, b) for b in range(8)]
    slopes = along(DERIVATIVE, lines, -1)
    slopes = [slopes[q] * outer[pl.ds(8 * q, 8), :] for q in range(8)]
    for_y = [end_row(slopes, 0), end_row(slopes, 7)]
    for_x = []
    for side in range(2):
        base = 64 + 72 * side
        spread = [outer[pl.ds(base + 8 * a, 8), :] for a in range(8)]
        slopes = along(DERIVATIVE, [values[row(a, 7 * side), :] for a in range(8)], -1)
        slopes = [slopes[q] * spread[q] for q in range(8)]
        share = jnp.where(first, end_row(slopes, 0), end_row(slopes, 7))
        corner = lines[7 * side]
        slope = shifted_sum(shifts, 0, corner) * jnp.where(first, spread[0], spread[7])
        share = share + shifted_sum(shifts, 64, slope) + outer[pl.ds(base + 64, 8), :] * corner
        for_x.append(share)
    return [join_vertical_packed(share) for share in for_x], [
        join_vertical_packed(share) for share in for_y
    ]


def joined_inside(lines, share):
    first = lane_index() < HALF
    low, high = lines[0], lines[7]
    new_low = low + jnp.where(first, share, pltpu.roll(high, HALF, 1))
    new_high = high + jnp.where(first, pltpu.roll(low, HALF, 1), share)
    return [new_low] + lines[1:7] + [new_high]


def send_faces(image, values, outer, shifts, face_x, to_even, to_odd):
    for_x, for_y = corner_shares(values, outer, shifts)
    odd = is_odd("yz")
    for b in range(8):
        face = packed_x(image, b)
        if b in (0, 7):
            face = face + for_x[b // 7]
        face_x[pl.ds(8 * b, 8), :] = face
    faces = []
    for side in range(2):
        part = [image[row(a, 7 * side), :] for a in range(8)]
        part = joined_inside(part, for_y[side])
        faces.append(part)
    for a in range(8):
        lowest_to_highest(odd, to_even, to_odd, pl.ds(8 * a, 8), faces[0][a], faces[1][a])


def streamwise(lines, b, spread, mass):
    slopes = along(DERIVATIVE, lines, -1)
    back = along(DERIVATIVE.T, [slopes[a] * spread[row(a, b), :] for a in range(8)], -1)
    return [back[a] + mass[row(a, b), :] * lines[a] for a in range(8)]


def join_layers(image):
    for a in range(8):
        low, high = join_vertical(image[across(a, 0), :], image[across(a, 7), :])
        image[across(a, 0), :] = low
        image[across(a, 7), :] = high


def vertical_part(lines, spread):
    slopes = along(DERIVATIVE, lines, -1)
    return along(VERTICAL * DERIVATIVE.T, [slopes[c] * spread[c] for c in range(8)], -1)


def operate(values, spread, image):
    for a in range(8):
        slopes = along(DERIVATIVE, [values[row(a, b), :] for b in range(8)], -1)
        back = along(DERIVATIVE.T, [slopes[b] * spread[row(a, b), :] for b in range(8)], -1)
        for b in range(8):
            image[row(a, b), :] += back[b]
    for a in range(8):
        back = vertical_part(
            [values[across(a, c), :] for c in range(8)],
            [spread[across(a, c), :] for c in range(8)],
        )
        for c in range(8):
            image[across(a, c), :] += back[c]


def weighted(sums):
    layer, point = lane_index() % EZ, sublane_index()
    below = jnp.logical_and(point == 0, layer > 0)
    above = jnp.logical_and(point == 7, layer < EZ - 1)
    shared = jnp.where(jnp.logical_or(below, above), 0.5, 1.0)
    return (sums[0] + 0.5 * sums[1] + 0.25 * sums[2]) * shared


def ends(a, b):
    return int(a in (0, 7)) + int(b in (0, 7))


def early_kernel(
    right, diagonal, even_x, odd_x, odd_y, even_y, spread, mass,
    whole_diagonal, jacobi, values, image, outer, moments, from_low, from_high, from_side, packed,
):
    received = (even_x, odd_x, even_y, odd_y)
    first = lane_index() < HALF
    sums = [jnp.zeros((8, LANES), jnp.float32)] * 3
    for b in range(8):
        lines = []
        for a in range(8):
            source = assembled(a, b, right, received, 0)
            scale = assembled(a, b, diagonal, received, 1)
            inverse = 1.0 / scale
            value = source * inverse
            if ends(a, b) == 2:
                value = jnp.where(first, 0.0, value) if a == 0 else jnp.where(first, value, 0.0)
            whole_diagonal[row(a, b), :] = scale
            jacobi[row(a, b), :] = inverse
            values[row(a, b), :] = value
            sums[ends(a, b)] = sums[ends(a, b)] + source * value
            lines.append(value)
        back = streamwise(lines, b, spread, mass)
        for a in range(8):
            image[row(a, b), :] = back[a]
    moments[...] = weighted(sums)
    for b in range(8):
        outer[pl.ds(8 * b, 8), :] = pltpu.roll(
            ghost_x(even_x, odd_x, pl.ds(128 + 8 * b, 8)), HALF, 1
        )
    for side in range(2):
        for k in range(9):
            outer[pl.ds(64 + 72 * side + 8 * k, 8), :] = from_y(
                even_y, odd_y, 7 * side, pl.ds(128 + 8 * k, 8)
            )
    operate(values, spread, image)
    join_layers(image)
    for a in range(8):
        for end, out in ((0, from_low), (7, from_high)):
            slopes = [spread[row(a, q), :] * float(DERIVATIVE[q, end]) for q in range(8)]
            back = along(DERIVATIVE.T, slopes, -1)
            for b in range(8):
                out[row(a, b), :] = back[b]
    for b in range(8):
        packed[pl.ds(8 * b, 8), :] = packed_x(spread, b)
        packed[pl.ds(64 + 8 * b, 8), :] = spread[row(b, 0), :]
        packed[pl.ds(128 + 8 * b, 8), :] = spread[row(b, 7), :]
        back = along(
            DERIVATIVE.T, [spread[row(q, b), :] * outer_slope(q) for q in range(8)], -1
        )
        for a in range(8):
            from_side[row(a, b), :] = back[a]


def outer_slope(q):
    first = lane_index() < HALF
    return jnp.where(first, float(DERIVATIVE[q, 0]), float(DERIVATIVE[q, 7]))


def add_packed(grid, b, value):
    first = lane_index() < HALF
    grid[row(0, b), :] += jnp.where(first, value, 0.0)
    grid[row(7, b), :] += jnp.where(first, 0.0, value)


def first_kernel(
    right, diagonal, even_x, odd_x, odd_y, even_y, even_shared, odd_shared, spread, mass, shifts,
    outer, early_diagonal, early_jacobi, early_values, early_image, early_moments,
    whole_diagonal, jacobi, values, image, face_x, to_even, to_odd, moments,
):
    received = (even_x, odd_x, even_y, odd_y, even_shared, odd_shared)
    first = lane_index() < HALF
    corners = []
    total = jnp.zeros((8, LANES), jnp.float32)
    for b in (0, 7):
        packed = []
        for a in (0, 7):
            source = assembled(a, b, right, received, 0)
            scale = assembled(a, b, diagonal, received, 1)
            inverse = 1.0 / scale
            value = source * inverse
            whole_diagonal[row(a, b), :] = scale
            jacobi[row(a, b), :] = inverse
            values[row(a, b), :] = value
            packed.append((value, source * value))
        corners.append(jnp.where(first, packed[0][0], packed[1][0]))
        total = total + jnp.where(first, packed[0][1], packed[1][1])
    zero = jnp.zeros((8, LANES), jnp.float32)
    moments[...] = early_moments[...] + weighted([zero, zero, total])
    for side, corner in enumerate(corners):
        b = 7 * side
        slopes = []
        for q in range(8):
            slopes.append(spread[row(q, b), :] * (outer_slope(q) * corner))
        back = along(DERIVATIVE.T, slopes, -1)
        for a in range(8):
            image[row(a, b), :] += join_vertical_packed(back[a])
    slopes = []
    for q in range(8):
        slope = corners[0] * float(DERIVATIVE[q, 0]) + corners[1] * float(DERIVATIVE[q, 7])
        slopes.append(packed_x(spread, q) * slope)
    back = along(DERIVATIVE.T, slopes, -1)
    for side, corner in enumerate(corners):
        b = 7 * side
        slope = shifted_sum(shifts, 0, corner) * packed_x(spread, b)
        back[b] = back[b] + shifted_sum(shifts, 64, slope) + packed_x(mass, b) * corner
    for b in range(8):
        add_packed(image, b, join_vertical_packed(back[b]))
    send_faces(image, values, outer, shifts, face_x, to_even, to_odd)


def inner_kernel(
    before_image, diagonal, jacobi, before, spread, mass, values, image, moments
):
    first = lane_index() < HALF
    zero = jnp.zeros((8, LANES), jnp.float32)
    cross, square = [zero] * 3, [zero] * 3
    for b in range(8):
        lines = []
        for a in range(8):
            if b in (0, 7):
                values[row(a, b), :] = zero
                image[row(a, b), :] = zero
                continue
            joined = before_image[row(a, b), :]
            if a in (0, 7):
                joined = joined_x(a, before_image[row(0, b), :], before_image[row(7, b), :], 0.0)
            old = before[row(a, b), :]
            scaled = joined - diagonal[row(a, b), :] * old
            if a in (0, 7):
                scaled = jnp.where(first, 0.0, scaled) if a == 0 else jnp.where(first, scaled, 0.0)
            value = scaled * jacobi[row(a, b), :]
            values[row(a, b), :] = value
            kind = ends(a, b)
            cross[kind] = cross[kind] + scaled * old
            square[kind] = square[kind] + scaled * value
            lines.append(value)
        if lines:
            back = streamwise(lines, b, spread, mass)
            for a in range(8):
                image[row(a, b), :] = back[a]
    moments[pl.ds(0, 8), :] = weighted(cross)
    moments[pl.ds(8, 8), :] = weighted(square)
    operate(values, spread, image)


def outer_kernel(
    before_image, even_x, odd_x, odd_y, even_y, diagonal, jacobi, before, spread, mass, shifts,
    outer, from_low, from_high, from_side, packed, inner_moments, earlier, inner_values,
    inner_image, values, image, face_x, to_even, to_odd, moments, face, face_back, *summed,
):
    received = (even_x, odd_x, even_y, odd_y)
    first = lane_index() < HALF
    zero = jnp.zeros((8, LANES), jnp.float32)
    cross, square = [zero] * 3, [zero] * 3
    sides = []
    for b in (0, 7):
        lines = []
        for a in range(8):
            old = before[row(a, b), :]
            scaled = assembled(a, b, before_image, received, 0) - diagonal[row(a, b), :] * old
            value = scaled * jacobi[row(a, b), :]
            values[row(a, b), :] = value
            kind = ends(a, b)
            cross[kind] = cross[kind] + scaled * old
            square[kind] = square[kind] + scaled * value
            lines.append(value)
        sides.append(lines)
    lines = [zero] * 8
    for b in range(1, 7):
        old = packed_x(before, b)
        ghost = pltpu.roll(ghost_x(even_x, odd_x, pl.ds(8 * b, 8)), HALF, 1)
        scaled = packed_x(before_image, b) + ghost - packed_x(diagonal, b) * old
        lines[b] = scaled * packed_x(jacobi, b)
        add_packed(values, b, lines[b])
        cross[1] = cross[1] + scaled * old
        square[1] = square[1] + scaled * lines[b]
    for group, part in enumerate((lines, *sides)):
        base = 64 * group
        for k in range(8):
            face[pl.ds(base + 8 * k, 8), :] = part[k]
        back = vertical_part(
            [face[pl.ds(base + c, 8, stride=8), :] for c in range(8)],
            [packed[pl.ds(base + c, 8, stride=8), :] for c in range(8)],
        )
        for c in range(8):
            face_back[pl.ds(base + c, 8, stride=8), :] = back[c]
    slopes = along(DERIVATIVE, lines, -1)
    back = along(DERIVATIVE.T, [slopes[q] * packed[pl.ds(8 * q, 8), :] for q in range(8)], -1)
    shares = [back[b] + face_back[pl.ds(8 * b, 8), :] for b in range(8)]
    for b in range(1, 7):
        shares[b] = shares[b] + packed_x(mass, b) * lines[b]
    ends_back = [streamwise(sides[k], 7 * k, spread, mass) for k in range(2)]
    energy = [zero] * 4
    for a in range(8):
        for b in range(8):
            rows = row(a, b)
            share = from_low[rows, :] * sides[0][a] + from_high[rows, :] * sides[1][a]
            if b in (0, 7):
                side = b // 7
                share = share + ends_back[side][a]
                share = share + face_back[pl.ds(64 + 64 * side + 8 * a, 8), :]
            else:
                share = share + from_side[rows, :] * lines[b]
            if a == 0:
                share = share + jnp.where(first, shares[b], 0.0)
            if a == 7:
                share = share + jnp.where(first, 0.0, shares[b])
            share = image[rows, :] + share
            image[rows, :] = share
            if summed:
                energy[b % 4] = energy[b % 4] + values[rows, :] * share
    cross = inner_moments[pl.ds(0, 8), :] + weighted(cross)
    square = inner_moments[pl.ds(8, 8), :] + weighted(square)
    if summed:
        held, copied = summed
        energy = (energy[0] + energy[1]) + (energy[2] + energy[3])
        parts = [earlier[pl.ds(8 * k, 8), :] for k in range(3)] + [cross, square, energy]
        held[...] = jnp.broadcast_to(sums_line(parts)[None], held.shape)
        copy = pltpu.make_async_copy(held, moments, copied)
        copy.start()
    else:
        moments[pl.ds(0, 8), :] = earlier[...]
        moments[pl.ds(8, 8), :] = cross
        moments[pl.ds(16, 8), :] = square
    join_layers(image)
    send_faces(image, values, outer, shifts, face_x, to_even, to_odd)
    if summed:
        copy.wait()


def sums_line(parts):
    lane = lax.broadcasted_iota(jnp.int32, (1, LANES), 1)
    line = jnp.zeros((1, LANES), jnp.float32)
    for k, part in enumerate(parts):
        total = jnp.sum(jnp.sum(part, 0, keepdims=True), 1, keepdims=True)
        line = jnp.where(lane == k, total, line)
    return line


def recurrence(moments):
    moments = moments[:5] + [moments[5] - moments[4]]
    zero = jnp.zeros_like(moments[0])
    one = zero + 1.0

    def form(left, right, shift):
        total = zero
        for i in range(3):
            for j in range(3):
                if left[i] is not None and right[j] is not None:
                    entry = moments[i + j]
                    if shift:
                        entry = entry + moments[i + j + 1]
                    total = total + left[i] * right[j] * entry
        return total

    def ratio(top, bottom):
        fine = jnp.logical_and(bottom > 0.0, top > 0.0)
        return jnp.where(fine, top / jnp.where(fine, bottom, 1.0), 0.0)

    def add(left, scale, right):
        out = []
        for x, y in zip(left, right):
            if y is None:
                out.append(x)
            else:
                out.append(scale * y if x is None else x + scale * y)
        return out

    direction = [one, None, None, None]
    precond = [one, None, None, None]
    result = [None, None, None, None]
    norm = moments[0]
    for step in range(3):
        curve = form(direction, direction, True)
        length = ratio(norm, curve)
        result = add(result, length, direction)
        moved = add(direction, 1.0, [None] + direction[:3])
        if step == 0:
            precond = [jnp.where(curve > 0.0, moments[1] / curve, 1.0), -length, None, None]
        else:
            precond = add(precond, -length, moved)
        if step < 2:
            norm_next = form(precond, precond, False)
            direction = add(precond, ratio(norm_next, norm), direction)
            norm = norm_next
    return result[:3], precond


def to_slots(chosen, grid):
    total = None
    for part in parts_of(grid):
        term = lax.dot_general(
            chosen, part, (((1,), (1,)), ((), ())), preferred_element_type=jnp.float32
        )
        total = term if total is None else total + term
    return total


def solution_kernel(
    values0, values1, values2, sums, slot_rows, solution, precond_rows, solution_grid
):
    line = jnp.sum(sums[...], 0)[0:1]
    lane = lax.broadcasted_iota(jnp.int32, (1, LANES), 1)
    moments = [
        jnp.sum(jnp.where(lane == k, line, 0.0), 1, keepdims=True) for k in range(6)
    ]
    result, precond = recurrence(moments)
    result = [jnp.broadcast_to(entry, (8, LANES)) for entry in result]
    for k in range(4):
        precond_rows[pl.ds(8 * k, 8), :] = jnp.broadcast_to(precond[k], (8, LANES))
    for a in range(8):
        for b in range(8):
            rows = row(a, b)
            solution_grid[rows, :] = (
                result[0] * values0[rows, :]
                + result[1] * values1[rows, :]
                + result[2] * values2[rows, :]
            )
    chosen = selection(slot_rows).T.astype(jnp.bfloat16)
    solution[0, 0] = to_slots(chosen, solution_grid[...])


def last_kernel(
    before_image, even_x, odd_x, odd_y, even_y, diagonal, values0, values1, values2, precond_rows,
    slot_rows, residual, residual_grid,
):
    received = (even_x, odd_x, even_y, odd_y)
    precond = [precond_rows[pl.ds(8 * k, 8), :] for k in range(4)]
    for a in range(8):
        for b in range(8):
            rows = row(a, b)
            far = (
                precond[0] * values0[rows, :]
                + precond[1] * values1[rows, :]
                + (precond[2] - precond[3]) * values2[rows, :]
            )
            image = assembled(a, b, before_image, received, 0)
            residual_grid[rows, :] = diagonal[rows, :] * far + precond[3] * image
    chosen = selection(slot_rows).T.astype(jnp.bfloat16)
    residual[0, 0] = to_slots(chosen, residual_grid[...])


def call(kernel, name, shapes, scratch, *operands, outside=0, aliases=None, copied=0):
    places = [pltpu.HBM] * outside + [pltpu.VMEM] * (len(operands) - outside)
    operands = [
        pltpu.with_memory_space_constraint(operand, place) if place == pltpu.HBM else operand
        for operand, place in zip(operands, places)
    ]
    return pl.pallas_call(
        kernel,
        out_shape=[jax.ShapeDtypeStruct(shape, jnp.float32) for shape in shapes],
        in_specs=[pl.BlockSpec(memory_space=place) for place in places],
        out_specs=[pl.BlockSpec(memory_space=pltpu.VMEM)] * (len(shapes) - copied)
        + [pl.BlockSpec(memory_space=pltpu.HBM)] * copied,
        scratch_shapes=scratch,
        input_output_aliases=aliases or {},
        compiler_params=pltpu.CompilerParams(vmem_limit_bytes=VMEM_BYTES),
        name=name,
    )(*operands)


def swapped(block, axis):
    extent = lax.axis_size(axis)
    even = [(i, i ^ 1) for i in range(extent)]
    odd = [(i, (((i + 1) ^ 1) - 1) % extent) for i in range(extent)]
    return lax.ppermute(block[0], axis, even), lax.ppermute(block[1], axis, odd)


def body(forcing, viscosity, mass_rate, slot_element):
    devices = lax.axis_size("gx") * lax.axis_size("yz")
    slots = slot_element[0]
    grid, face, tile = (POINTS, LANES), (64, LANES), (8, LANES)
    right, diagonal, spread, mass, out_x, *sent_y, corners, shifts, slot_rows = call(
        setup_kernel, "setup",
        [grid] * 4 + [(192, LANES), (200, LANES), (200, LANES), (32, LANES), (128, LANES)]
        + [tile],
        [
            pltpu.VMEM((1, LANES), jnp.int32),
            pltpu.VMEM((3, LANES, POINTS), jnp.float32),
            pltpu.SemaphoreType.DMA((4,)),
        ],
        slots, forcing, viscosity, mass_rate, outside=4,
    )
    received_x, received_y = swapped((out_x, out_x), "gx"), swapped(sent_y, "yz")[::-1]
    [shared] = call(corners_kernel, "corners", [(32, LANES)], [], corners, *received_y)
    received = (*received_x, *received_y, *swapped((shared, shared), "gx"))
    *early, outer, moments0, from_low, from_high, from_side, packed = call(
        early_kernel, "early", [grid] * 4 + [(208, LANES), tile] + [grid] * 3 + [(192, LANES)], [],
        right, diagonal, *received_x, *received_y, spread, mass,
    )
    diagonal, jacobi, values0, image, out_x, *sent_y, moments0 = call(
        first_kernel, "first", [grid] * 4 + [face] * 3 + [tile], [],
        right, diagonal, *received, spread, mass, shifts, outer, *early, moments0,
        aliases={12: 0, 13: 1, 14: 2, 15: 3},
    )
    fixed = (spread, mass, shifts, outer, from_low, from_high, from_side, packed)

    def advance(name, earlier, image, before, out_x, sent_y, last=False):
        received = (*swapped((out_x, out_x), "gx"), *swapped(sent_y, "yz")[::-1])
        values, inner_image, moments = call(
            inner_kernel, "inner", [grid] * 2 + [(16, LANES)], [],
            image, diagonal, jacobi, before, spread, mass,
        )
        out = (devices, 2, LANES) if last else (24, LANES)
        scratch = [pltpu.VMEM((192, LANES), jnp.float32)] * 2
        if last:
            scratch = scratch + [pltpu.VMEM(out, jnp.float32), pltpu.SemaphoreType.DMA]
        return call(
            outer_kernel, name, [grid] * 2 + [face] * 3 + [out], scratch,
            image, *received, diagonal, jacobi, before, *fixed, moments, earlier, values,
            inner_image,
            aliases={18: 0, 19: 1}, copied=int(last),
        )

    values1, image, out_x, *sent_y, moments1 = advance(
        "second", moments0, image, values0, out_x, sent_y
    )
    values2, image, out_x, *sent_y, sums = advance(
        "third", moments1, image, values1, out_x, sent_y, last=True
    )
    sums = lax.all_to_all(sums, ("gx", "yz"), 0, 0)
    received = (*swapped((out_x, out_x), "gx"), *swapped(sent_y, "yz")[::-1])
    result, precond = call(
        solution_kernel, "solution", [forcing.shape, (32, LANES)],
        [pltpu.VMEM(grid, jnp.float32)],
        values0, values1, values2, sums, slot_rows,
    )
    [residual] = call(
        last_kernel, "last", [forcing.shape], [pltpu.VMEM(grid, jnp.float32)],
        image, *received, diagonal, values0, values1, values2, precond, slot_rows,
    )
    return result, residual


def solution(mesh):
    placed = (
        P("gx", "yz", None, None),
        P("gx", "yz", None, None),
        P("gx", "yz", None, None),
        P("gx", "yz", None),
    )
    return jax.shard_map(
        body,
        mesh=mesh,
        in_specs=placed,
        out_specs=(P("gx", "yz", None, None), P("gx", "yz", None, None)),
        check_vma=False,
    )
```

```python
import jax
import jax.numpy as jnp
import numpy as np
from jax import lax
from jax.experimental import pallas as pl
from jax.experimental.pallas import tpu as pltpu
from jax.sharding import PartitionSpec as P

EZ = 64
LANES = 128
HALF = 64
POINTS = 512
SPLIT = 2
VERTICAL = 4.0
VMEM_BYTES = 24 * 1024 * 1024


def legendre_rows(nodes, degree):
    rows = [nodes * 0.0 + 1.0, nodes]
    for order in range(2, degree + 1):
        rows.append(((2 * order - 1) * nodes * rows[-1] - (order - 1) * rows[-2]) / order)
    return np.stack(rows, 1)


def spectral_tables():
    degree = 7
    nodes = np.cos(np.pi * np.arange(degree + 1) / degree)
    for sweep in range(60):
        legendre = legendre_rows(nodes, degree)
        nodes = nodes - (nodes * legendre[:, degree] - legendre[:, degree - 1]) / (
            (degree + 1) * legendre[:, degree]
        )
    nodes = nodes[::-1].copy()
    top_values = legendre_rows(nodes, degree)[:, degree]
    weights = 2.0 / (degree * (degree + 1) * top_values**2)
    identity = np.eye(degree + 1)
    spacing = nodes[:, None] - nodes[None, :] + identity
    derivative = top_values[:, None] / top_values[None, :] / spacing * (1.0 - identity)
    corner_fix = np.zeros(degree + 1)
    corner_fix[0] = -degree * (degree + 1) / 4.0
    corner_fix[degree] = degree * (degree + 1) / 4.0
    derivative = derivative + identity * corner_fix[None, :]
    return (derivative, weights)


DERIVATIVE, WEIGHTS = spectral_tables()


def row(a, b):
    return pl.ds(64 * a + 8 * b, 8)


def across(a, c):
    return pl.ds(64 * a + c, 8, stride=8)


def along(matrix, lines, sign):
    evens = [lines[j] + lines[7 - j] for j in range(4)]
    odds = [lines[j] - lines[7 - j] for j in range(4)]
    out = [None] * 8
    for i in range(4):
        even = odd = None
        for j in range(4):
            even_term = evens[j] * float((matrix[i, j] + matrix[i, 7 - j]) / 2)
            odd_term = odds[j] * float((matrix[i, j] - matrix[i, 7 - j]) / 2)
            even = even_term if even is None else even + even_term
            odd = odd_term if odd is None else odd + odd_term
        out[i] = even + odd
        out[7 - i] = even - odd if sign > 0 else odd - even
    return out


def lane_index():
    return lax.broadcasted_iota(jnp.int32, (8, LANES), 1)


def sublane_index():
    return lax.broadcasted_iota(jnp.int32, (8, LANES), 0)


def join_vertical(low, high):
    layer = lane_index() % EZ
    new_low = low + jnp.where(layer > 0, pltpu.roll(high, 1, 1), 0.0)
    new_high = high + jnp.where(layer < EZ - 1, pltpu.roll(low, LANES - 1, 1), 0.0)
    return new_low, new_high


def packed_x(grid, b):
    return jnp.where(lane_index() < HALF, grid[row(0, b), :], grid[row(7, b), :])


def lowest_to_highest(low_side, to_even, to_odd, rows, low, high):
    to_even[rows, :] = jnp.where(low_side, low, high)
    to_odd[rows, :] = jnp.where(low_side, high, low)


def is_odd(axis):
    return lax.axis_index(axis) % 2 == 1


def ghost_x(from_even, from_odd, rows):
    odd = lax.axis_index("gx") % 2
    first = (lane_index() < HALF).astype(jnp.int32)
    return jnp.where(first != odd, from_even[rows, :], from_odd[rows, :])


def joined_x(a, low, high, ghost):
    first = lane_index() < HALF
    if a == 0:
        return low + pltpu.roll(jnp.where(first, high, ghost), HALF, 1)
    return high + pltpu.roll(jnp.where(first, ghost, low), HALF, 1)


def from_y(even_y, odd_y, b, rows):
    odd = is_odd("yz")
    pick = odd if b == 0 else jnp.logical_not(odd)
    return jnp.where(pick, even_y[rows, :], odd_y[rows, :])


def assembled(a, b, grid, received, field):
    even_x, odd_x, even_y, odd_y, *shared = received
    value = grid[row(a, b), :]
    if a in (0, 7):
        if shared and b in (0, 7):
            ghost = ghost_x(*shared, pl.ds(16 * field + 8 * (b // 7), 8))
        else:
            ghost = ghost_x(even_x, odd_x, pl.ds(64 * field + 8 * b, 8))
        value = joined_x(a, grid[row(0, b), :], grid[row(7, b), :], ghost)
    if b in (0, 7):
        rows = pl.ds(64 * field + 8 * a, 8)
        value = value + from_y(even_y, odd_y, b, rows)
    return value


def corners_kernel(corners, odd_y, even_y, shared):
    first = lane_index() < HALF
    for field in range(2):
        for side in range(2):
            rows = pl.ds(16 * field + 8 * side, 8)
            low = from_y(even_y, odd_y, 7 * side, pl.ds(64 * field, 8))
            high = from_y(even_y, odd_y, 7 * side, pl.ds(64 * field + 56, 8))
            shared[rows, :] = corners[rows, :] + jnp.where(first, low, high)


def selection(slots):
    elements = lax.broadcasted_iota(jnp.int32, (LANES, LANES), 0)
    return jnp.where(elements.astype(jnp.float32) == slots[pl.ds(0, 1), :], 1.0, 0.0)


def parts_of(values):
    parts = []
    for _ in range(SPLIT):
        parts.append(values.astype(jnp.bfloat16))
        values = values - parts[-1].astype(jnp.float32)
    return parts


def to_grid(chosen, values):
    parts = jnp.concatenate(parts_of(values), 0)
    picked = jnp.dot(
        jnp.concatenate([chosen.astype(jnp.bfloat16)] * SPLIT, 1),
        parts,
        preferred_element_type=jnp.float32,
    )
    return picked.T


def setup_kernel(
    slots, forcing, viscosity, mass_rate,
    right, diagonal, spread, mass, face_x, to_even, to_odd, corners, shifts, slot_rows,
    order, held, arrived,
):
    ordered = pltpu.make_async_copy(slots, order, arrived.at[3])
    copies = [
        pltpu.make_async_copy(source.at[0, 0], held.at[k], arrived.at[k])
        for k, source in enumerate((viscosity, mass_rate, forcing))
    ]
    for copy in [ordered] + copies:
        copy.start()
    point = sublane_index()
    last_weight = jnp.zeros((8, LANES), jnp.float32)
    for c in range(8):
        last_weight = jnp.where(point == c, float(WEIGHTS[c]), last_weight)
    ordered.wait()
    slot_rows[...] = jnp.broadcast_to(order[...].astype(jnp.float32), slot_rows.shape)
    chosen = selection(slot_rows)
    for copy in copies:
        copy.wait()
    spread[...] = to_grid(chosen, held[0])
    mass[...] = to_grid(chosen, held[1])
    for a in range(8):
        for b in range(8):
            weight = last_weight * float(WEIGHTS[a] * WEIGHTS[b])
            spread[row(a, b), :] *= weight
            mass[row(a, b), :] *= weight
    right[...] = to_grid(chosen, held[2])
    squares = (DERIVATIVE * DERIVATIVE).T
    for b in range(8):
        lines = along(squares, [spread[row(a, b), :] for a in range(8)], 1)
        for a in range(8):
            diagonal[row(a, b), :] = lines[a] + mass[row(a, b), :]
    for a in range(8):
        lines = along(squares, [spread[row(a, b), :] for b in range(8)], 1)
        for b in range(8):
            diagonal[row(a, b), :] += lines[b]
    for a in range(8):
        lines = along(VERTICAL * squares, [spread[across(a, c), :] for c in range(8)], 1)
        lines = [lines[c] + diagonal[across(a, c), :] for c in range(8)]
        lines[0], lines[7] = join_vertical(lines[0], lines[7])
        for c in range(8):
            diagonal[across(a, c), :] = lines[c]
        low, high = join_vertical(right[across(a, 0), :], right[across(a, 7), :])
        right[across(a, 0), :] = low
        right[across(a, 7), :] = high
    odd = is_odd("yz")
    for field, source in enumerate((right, diagonal, spread)):
        for b in range(8):
            face_x[pl.ds(64 * field + 8 * b, 8), :] = packed_x(source, b)
        faces = []
        for side in range(2):
            part = [source[row(a, 7 * side), :] for a in range(8)]
            if field < 2:
                corners[pl.ds(16 * field + 8 * side, 8), :] = packed_x(source, 7 * side)
                part = joined_inside(part, 0.0)
            faces.append(part)
        for a in range(8):
            rows = pl.ds(64 * field + 8 * a, 8)
            lowest_to_highest(odd, to_even, to_odd, rows, faces[0][a], faces[1][a])
    rows = pl.ds(192, 8)
    lowest_to_highest(odd, to_even, to_odd, rows, packed_x(mass, 0), packed_x(mass, 7))
    for k in range(8):
        along_shift = back_shift = jnp.zeros((8, LANES), jnp.float32)
        for c in range(8):
            other = (c + k) % 8
            along_shift = jnp.where(point == c, float(DERIVATIVE[c, other]), along_shift)
            back_shift = jnp.where(
                point == c, float(VERTICAL * DERIVATIVE[other, c]), back_shift
            )
        shifts[pl.ds(8 * k, 8), :] = along_shift
        shifts[pl.ds(64 + 8 * k, 8), :] = back_shift


def join_vertical_packed(value):
    layer, point = lane_index() % EZ, sublane_index()
    from_below = pltpu.roll(pltpu.roll(value, 1, 0), 1, 1)
    from_above = pltpu.roll(pltpu.roll(value, 7, 0), LANES - 1, 1)
    below = jnp.logical_and(point == 0, layer > 0)
    above = jnp.logical_and(point == 7, layer < EZ - 1)
    return value + jnp.where(below, from_below, jnp.where(above, from_above, 0.0))


def shifted_sum(shifts, start, value):
    total = shifts[pl.ds(start, 8), :] * value
    for k in range(1, 8):
        total = total + shifts[pl.ds(start + 8 * k, 8), :] * pltpu.roll(value, 8 - k, 0)
    return total


def end_row(lines, end):
    total = None
    for q in range(8):
        term = lines[q] * float(DERIVATIVE[q, end])
        total = term if total is None else total + term
    return total


def corner_shares(values, outer, shifts):
    first = lane_index() < HALF
    lines = [packed_x(values, b) for b in range(8)]
    slopes = along(DERIVATIVE, lines, -1)
    slopes = [slopes[q] * outer[pl.ds(8 * q, 8), :] for q in range(8)]
    for_y = [end_row(slopes, 0), end_row(slopes, 7)]
    for_x = []
    for side in range(2):
        base = 64 + 72 * side
        spread = [outer[pl.ds(base + 8 * a, 8), :] for a in range(8)]
        slopes = along(DERIVATIVE, [values[row(a, 7 * side), :] for a in range(8)], -1)
        slopes = [slopes[q] * spread[q] for q in range(8)]
        share = jnp.where(first, end_row(slopes, 0), end_row(slopes, 7))
        corner = lines[7 * side]
        slope = shifted_sum(shifts, 0, corner) * jnp.where(first, spread[0], spread[7])
        share = share + shifted_sum(shifts, 64, slope) + outer[pl.ds(base + 64, 8), :] * corner
        for_x.append(share)
    return [join_vertical_packed(share) for share in for_x], [
        join_vertical_packed(share) for share in for_y
    ]


def joined_inside(lines, share):
    first = lane_index() < HALF
    low, high = lines[0], lines[7]
    new_low = low + jnp.where(first, share, pltpu.roll(high, HALF, 1))
    new_high = high + jnp.where(first, pltpu.roll(low, HALF, 1), share)
    return [new_low] + lines[1:7] + [new_high]


def send_faces(image, values, outer, shifts, face_x, to_even, to_odd):
    for_x, for_y = corner_shares(values, outer, shifts)
    odd = is_odd("yz")
    for b in range(8):
        face = packed_x(image, b)
        if b in (0, 7):
            face = face + for_x[b // 7]
        face_x[pl.ds(8 * b, 8), :] = face
    faces = []
    for side in range(2):
        part = [image[row(a, 7 * side), :] for a in range(8)]
        part = joined_inside(part, for_y[side])
        faces.append(part)
    for a in range(8):
        lowest_to_highest(odd, to_even, to_odd, pl.ds(8 * a, 8), faces[0][a], faces[1][a])


def streamwise(lines, b, spread, mass):
    slopes = along(DERIVATIVE, lines, -1)
    back = along(DERIVATIVE.T, [slopes[a] * spread[row(a, b), :] for a in range(8)], -1)
    return [back[a] + mass[row(a, b), :] * lines[a] for a in range(8)]


def join_layers(image):
    for a in range(8):
        low, high = join_vertical(image[across(a, 0), :], image[across(a, 7), :])
        image[across(a, 0), :] = low
        image[across(a, 7), :] = high


def vertical_part(lines, spread):
    slopes = along(DERIVATIVE, lines, -1)
    return along(VERTICAL * DERIVATIVE.T, [slopes[c] * spread[c] for c in range(8)], -1)


def operate(values, spread, image):
    for a in range(8):
        slopes = along(DERIVATIVE, [values[row(a, b), :] for b in range(8)], -1)
        back = along(DERIVATIVE.T, [slopes[b] * spread[row(a, b), :] for b in range(8)], -1)
        for b in range(8):
            image[row(a, b), :] += back[b]
    for a in range(8):
        back = vertical_part(
            [values[across(a, c), :] for c in range(8)],
            [spread[across(a, c), :] for c in range(8)],
        )
        for c in range(8):
            image[across(a, c), :] += back[c]


def weighted(sums):
    layer, point = lane_index() % EZ, sublane_index()
    below = jnp.logical_and(point == 0, layer > 0)
    above = jnp.logical_and(point == 7, layer < EZ - 1)
    shared = jnp.where(jnp.logical_or(below, above), 0.5, 1.0)
    return (sums[0] + 0.5 * sums[1] + 0.25 * sums[2]) * shared


def ends(a, b):
    return int(a in (0, 7)) + int(b in (0, 7))


def early_kernel(
    right, diagonal, even_x, odd_x, odd_y, even_y, spread, mass, slot_rows,
    whole_diagonal, jacobi, values, image, outer, moments, from_low, from_high, from_side, packed,
    chosen,
):
    received = (even_x, odd_x, even_y, odd_y)
    first = lane_index() < HALF
    sums = [jnp.zeros((8, LANES), jnp.float32)] * 3
    for b in range(8):
        lines = []
        for a in range(8):
            source = assembled(a, b, right, received, 0)
            scale = assembled(a, b, diagonal, received, 1)
            inverse = 1.0 / scale
            value = source * inverse
            if ends(a, b) == 2:
                value = jnp.where(first, 0.0, value) if a == 0 else jnp.where(first, value, 0.0)
            whole_diagonal[row(a, b), :] = scale
            jacobi[row(a, b), :] = inverse
            values[row(a, b), :] = value
            sums[ends(a, b)] = sums[ends(a, b)] + source * value
            lines.append(value)
        back = streamwise(lines, b, spread, mass)
        for a in range(8):
            image[row(a, b), :] = back[a]
    moments[...] = weighted(sums)
    for b in range(8):
        outer[pl.ds(8 * b, 8), :] = pltpu.roll(
            ghost_x(even_x, odd_x, pl.ds(128 + 8 * b, 8)), HALF, 1
        )
    for side in range(2):
        for k in range(9):
            outer[pl.ds(64 + 72 * side + 8 * k, 8), :] = from_y(
                even_y, odd_y, 7 * side, pl.ds(128 + 8 * k, 8)
            )
    operate(values, spread, image)
    join_layers(image)
    chosen[...] = selection(slot_rows).T
    for a in range(8):
        for end, out in ((0, from_low), (7, from_high)):
            slopes = [spread[row(a, q), :] * float(DERIVATIVE[q, end]) for q in range(8)]
            back = along(DERIVATIVE.T, slopes, -1)
            for b in range(8):
                out[row(a, b), :] = back[b]
    for b in range(8):
        packed[pl.ds(8 * b, 8), :] = packed_x(spread, b)
        packed[pl.ds(64 + 8 * b, 8), :] = spread[row(b, 0), :]
        packed[pl.ds(128 + 8 * b, 8), :] = spread[row(b, 7), :]
        back = along(
            DERIVATIVE.T, [spread[row(q, b), :] * outer_slope(q) for q in range(8)], -1
        )
        for a in range(8):
            from_side[row(a, b), :] = back[a]


def outer_slope(q):
    first = lane_index() < HALF
    return jnp.where(first, float(DERIVATIVE[q, 0]), float(DERIVATIVE[q, 7]))


def add_packed(grid, b, value):
    first = lane_index() < HALF
    grid[row(0, b), :] += jnp.where(first, value, 0.0)
    grid[row(7, b), :] += jnp.where(first, 0.0, value)


def first_kernel(
    right, diagonal, even_x, odd_x, odd_y, even_y, even_shared, odd_shared, spread, mass, shifts,
    outer, early_diagonal, early_jacobi, early_values, early_image, early_moments,
    whole_diagonal, jacobi, values, image, face_x, to_even, to_odd, moments,
):
    received = (even_x, odd_x, even_y, odd_y, even_shared, odd_shared)
    first = lane_index() < HALF
    corners = []
    total = jnp.zeros((8, LANES), jnp.float32)
    for b in (0, 7):
        packed = []
        for a in (0, 7):
            source = assembled(a, b, right, received, 0)
            scale = assembled(a, b, diagonal, received, 1)
            inverse = 1.0 / scale
            value = source * inverse
            whole_diagonal[row(a, b), :] = scale
            jacobi[row(a, b), :] = inverse
            values[row(a, b), :] = value
            packed.append((value, source * value))
        corners.append(jnp.where(first, packed[0][0], packed[1][0]))
        total = total + jnp.where(first, packed[0][1], packed[1][1])
    zero = jnp.zeros((8, LANES), jnp.float32)
    moments[...] = early_moments[...] + weighted([zero, zero, total])
    for side, corner in enumerate(corners):
        b = 7 * side
        slopes = []
        for q in range(8):
            slopes.append(spread[row(q, b), :] * (outer_slope(q) * corner))
        back = along(DERIVATIVE.T, slopes, -1)
        for a in range(8):
            image[row(a, b), :] += join_vertical_packed(back[a])
    slopes = []
    for q in range(8):
        slope = corners[0] * float(DERIVATIVE[q, 0]) + corners[1] * float(DERIVATIVE[q, 7])
        slopes.append(packed_x(spread, q) * slope)
    back = along(DERIVATIVE.T, slopes, -1)
    for side, corner in enumerate(corners):
        b = 7 * side
        slope = shifted_sum(shifts, 0, corner) * packed_x(spread, b)
        back[b] = back[b] + shifted_sum(shifts, 64, slope) + packed_x(mass, b) * corner
    for b in range(8):
        add_packed(image, b, join_vertical_packed(back[b]))
    send_faces(image, values, outer, shifts, face_x, to_even, to_odd)


def inner_kernel(
    before_image, diagonal, jacobi, before, spread, mass, values, image, moments
):
    first = lane_index() < HALF
    zero = jnp.zeros((8, LANES), jnp.float32)
    cross, square = [zero] * 3, [zero] * 3
    for b in range(8):
        lines = []
        for a in range(8):
            if b in (0, 7):
                values[row(a, b), :] = zero
                image[row(a, b), :] = zero
                continue
            joined = before_image[row(a, b), :]
            if a in (0, 7):
                joined = joined_x(a, before_image[row(0, b), :], before_image[row(7, b), :], 0.0)
            old = before[row(a, b), :]
            scaled = joined - diagonal[row(a, b), :] * old
            if a in (0, 7):
                scaled = jnp.where(first, 0.0, scaled) if a == 0 else jnp.where(first, scaled, 0.0)
            value = scaled * jacobi[row(a, b), :]
            values[row(a, b), :] = value
            kind = ends(a, b)
            cross[kind] = cross[kind] + scaled * old
            square[kind] = square[kind] + scaled * value
            lines.append(value)
        if lines:
            back = streamwise(lines, b, spread, mass)
            for a in range(8):
                image[row(a, b), :] = back[a]
    moments[pl.ds(0, 8), :] = weighted(cross)
    moments[pl.ds(8, 8), :] = weighted(square)
    operate(values, spread, image)


def outer_kernel(
    before_image, even_x, odd_x, odd_y, even_y, diagonal, jacobi, before, spread, mass, shifts,
    outer, from_low, from_high, from_side, packed, inner_moments, earlier, inner_values,
    inner_image, values, image, face_x, to_even, to_odd, moments, face, face_back, *summed,
):
    received = (even_x, odd_x, even_y, odd_y)
    first = lane_index() < HALF
    zero = jnp.zeros((8, LANES), jnp.float32)
    cross, square = [zero] * 3, [zero] * 3
    sides = []
    for b in (0, 7):
        lines = []
        for a in range(8):
            old = before[row(a, b), :]
            scaled = assembled(a, b, before_image, received, 0) - diagonal[row(a, b), :] * old
            value = scaled * jacobi[row(a, b), :]
            values[row(a, b), :] = value
            kind = ends(a, b)
            cross[kind] = cross[kind] + scaled * old
            square[kind] = square[kind] + scaled * value
            lines.append(value)
        sides.append(lines)
    lines = [zero] * 8
    for b in range(1, 7):
        old = packed_x(before, b)
        ghost = pltpu.roll(ghost_x(even_x, odd_x, pl.ds(8 * b, 8)), HALF, 1)
        scaled = packed_x(before_image, b) + ghost - packed_x(diagonal, b) * old
        lines[b] = scaled * packed_x(jacobi, b)
        add_packed(values, b, lines[b])
        cross[1] = cross[1] + scaled * old
        square[1] = square[1] + scaled * lines[b]
    for group, part in enumerate((lines, *sides)):
        base = 64 * group
        for k in range(8):
            face[pl.ds(base + 8 * k, 8), :] = part[k]
        back = vertical_part(
            [face[pl.ds(base + c, 8, stride=8), :] for c in range(8)],
            [packed[pl.ds(base + c, 8, stride=8), :] for c in range(8)],
        )
        for c in range(8):
            face_back[pl.ds(base + c, 8, stride=8), :] = back[c]
    slopes = along(DERIVATIVE, lines, -1)
    back = along(DERIVATIVE.T, [slopes[q] * packed[pl.ds(8 * q, 8), :] for q in range(8)], -1)
    shares = [back[b] + face_back[pl.ds(8 * b, 8), :] for b in range(8)]
    for b in range(1, 7):
        shares[b] = shares[b] + packed_x(mass, b) * lines[b]
    ends_back = [streamwise(sides[k], 7 * k, spread, mass) for k in range(2)]
    energy = [zero] * 4
    for a in range(8):
        for b in range(8):
            rows = row(a, b)
            share = from_low[rows, :] * sides[0][a] + from_high[rows, :] * sides[1][a]
            if b in (0, 7):
                side = b // 7
                share = share + ends_back[side][a]
                share = share + face_back[pl.ds(64 + 64 * side + 8 * a, 8), :]
            else:
                share = share + from_side[rows, :] * lines[b]
            if a == 0:
                share = share + jnp.where(first, shares[b], 0.0)
            if a == 7:
                share = share + jnp.where(first, 0.0, shares[b])
            share = image[rows, :] + share
            image[rows, :] = share
            if summed:
                energy[b % 4] = energy[b % 4] + values[rows, :] * share
    cross = inner_moments[pl.ds(0, 8), :] + weighted(cross)
    square = inner_moments[pl.ds(8, 8), :] + weighted(square)
    if summed:
        held, copied = summed
        energy = (energy[0] + energy[1]) + (energy[2] + energy[3])
        parts = [earlier[pl.ds(8 * k, 8), :] for k in range(3)] + [cross, square, energy]
        held[...] = jnp.broadcast_to(sums_line(parts)[None], held.shape)
        copy = pltpu.make_async_copy(held, moments, copied)
        copy.start()
    else:
        moments[pl.ds(0, 8), :] = earlier[...]
        moments[pl.ds(8, 8), :] = cross
        moments[pl.ds(16, 8), :] = square
    join_layers(image)
    send_faces(image, values, outer, shifts, face_x, to_even, to_odd)
    if summed:
        copy.wait()


def sums_line(parts):
    lane = lax.broadcasted_iota(jnp.int32, (1, LANES), 1)
    line = jnp.zeros((1, LANES), jnp.float32)
    for k, part in enumerate(parts):
        total = jnp.sum(jnp.sum(part, 0, keepdims=True), 1, keepdims=True)
        line = jnp.where(lane == k, total, line)
    return line


def recurrence(moments):
    moments = moments[:5] + [moments[5] - moments[4]]
    zero = jnp.zeros_like(moments[0])
    one = zero + 1.0

    def form(left, right, shift):
        total = zero
        for i in range(3):
            for j in range(3):
                if left[i] is not None and right[j] is not None:
                    entry = moments[i + j]
                    if shift:
                        entry = entry + moments[i + j + 1]
                    total = total + left[i] * right[j] * entry
        return total

    def ratio(top, bottom):
        fine = jnp.logical_and(bottom > 0.0, top > 0.0)
        return jnp.where(fine, top / jnp.where(fine, bottom, 1.0), 0.0)

    def add(left, scale, right):
        out = []
        for x, y in zip(left, right):
            if y is None:
                out.append(x)
            else:
                out.append(scale * y if x is None else x + scale * y)
        return out

    direction = [one, None, None, None]
    precond = [one, None, None, None]
    result = [None, None, None, None]
    norm = moments[0]
    for step in range(3):
        curve = form(direction, direction, True)
        length = ratio(norm, curve)
        result = add(result, length, direction)
        moved = add(direction, 1.0, [None] + direction[:3])
        if step == 0:
            precond = [jnp.where(curve > 0.0, moments[1] / curve, 1.0), -length, None, None]
        else:
            precond = add(precond, -length, moved)
        if step < 2:
            norm_next = form(precond, precond, False)
            direction = add(precond, ratio(norm_next, norm), direction)
            norm = norm_next
    return result[:3], precond


def to_slots(chosen, grid):
    total = None
    for part in parts_of(grid):
        term = lax.dot_general(
            chosen, part, (((1,), (1,)), ((), ())), preferred_element_type=jnp.float32
        )
        total = term if total is None else total + term
    return total


def solution_kernel(
    values0, values1, values2, sums, chosen, solution, precond_rows, solution_grid
):
    line = jnp.sum(sums[...], 0)[0:1]
    lane = lax.broadcasted_iota(jnp.int32, (1, LANES), 1)
    moments = [
        jnp.sum(jnp.where(lane == k, line, 0.0), 1, keepdims=True) for k in range(6)
    ]
    result, precond = recurrence(moments)
    result = [jnp.broadcast_to(entry, (8, LANES)) for entry in result]
    for k in range(4):
        precond_rows[pl.ds(8 * k, 8), :] = jnp.broadcast_to(precond[k], (8, LANES))
    for a in range(8):
        for b in range(8):
            rows = row(a, b)
            solution_grid[rows, :] = (
                result[0] * values0[rows, :]
                + result[1] * values1[rows, :]
                + result[2] * values2[rows, :]
            )
    solution[0, 0] = to_slots(chosen[...].astype(jnp.bfloat16), solution_grid[...])


def last_kernel(
    before_image, even_x, odd_x, odd_y, even_y, diagonal, values0, values1, values2, precond_rows,
    chosen, residual, residual_grid,
):
    received = (even_x, odd_x, even_y, odd_y)
    precond = [precond_rows[pl.ds(8 * k, 8), :] for k in range(4)]
    for a in range(8):
        for b in range(8):
            rows = row(a, b)
            far = (
                precond[0] * values0[rows, :]
                + precond[1] * values1[rows, :]
                + (precond[2] - precond[3]) * values2[rows, :]
            )
            image = assembled(a, b, before_image, received, 0)
            residual_grid[rows, :] = diagonal[rows, :] * far + precond[3] * image
    residual[0, 0] = to_slots(chosen[...].astype(jnp.bfloat16), residual_grid[...])


def call(kernel, name, shapes, scratch, *operands, outside=0, aliases=None, copied=0):
    places = [pltpu.HBM] * outside + [pltpu.VMEM] * (len(operands) - outside)
    operands = [
        pltpu.with_memory_space_constraint(operand, place) if place == pltpu.HBM else operand
        for operand, place in zip(operands, places)
    ]
    return pl.pallas_call(
        kernel,
        out_shape=[jax.ShapeDtypeStruct(shape, jnp.float32) for shape in shapes],
        in_specs=[pl.BlockSpec(memory_space=place) for place in places],
        out_specs=[pl.BlockSpec(memory_space=pltpu.VMEM)] * (len(shapes) - copied)
        + [pl.BlockSpec(memory_space=pltpu.HBM)] * copied,
        scratch_shapes=scratch,
        input_output_aliases=aliases or {},
        compiler_params=pltpu.CompilerParams(vmem_limit_bytes=VMEM_BYTES),
        name=name,
    )(*operands)


def swapped(block, axis):
    extent = lax.axis_size(axis)
    even = [(i, i ^ 1) for i in range(extent)]
    odd = [(i, (((i + 1) ^ 1) - 1) % extent) for i in range(extent)]
    return lax.ppermute(block[0], axis, even), lax.ppermute(block[1], axis, odd)


def body(forcing, viscosity, mass_rate, slot_element):
    devices = lax.axis_size("gx") * lax.axis_size("yz")
    slots = slot_element[0]
    grid, face, tile = (POINTS, LANES), (64, LANES), (8, LANES)
    right, diagonal, spread, mass, out_x, *sent_y, corners, shifts, slot_rows = call(
        setup_kernel, "setup",
        [grid] * 4 + [(192, LANES), (200, LANES), (200, LANES), (32, LANES), (128, LANES)]
        + [tile],
        [
            pltpu.VMEM((1, LANES), jnp.int32),
            pltpu.VMEM((3, LANES, POINTS), jnp.float32),
            pltpu.SemaphoreType.DMA((4,)),
        ],
        slots, forcing, viscosity, mass_rate, outside=4,
    )
    received_x, received_y = swapped((out_x, out_x), "gx"), swapped(sent_y, "yz")[::-1]
    [shared] = call(corners_kernel, "corners", [(32, LANES)], [], corners, *received_y)
    received = (*received_x, *received_y, *swapped((shared, shared), "gx"))
    *early, outer, moments0, from_low, from_high, from_side, packed, chosen = call(
        early_kernel, "early", [grid] * 4 + [(208, LANES), tile] + [grid] * 3 + [(192, LANES)]
        + [(LANES, LANES)], [],
        right, diagonal, *received_x, *received_y, spread, mass, slot_rows,
    )
    diagonal, jacobi, values0, image, out_x, *sent_y, moments0 = call(
        first_kernel, "first", [grid] * 4 + [face] * 3 + [tile], [],
        right, diagonal, *received, spread, mass, shifts, outer, *early, moments0,
        aliases={12: 0, 13: 1, 14: 2, 15: 3},
    )
    fixed = (spread, mass, shifts, outer, from_low, from_high, from_side, packed)

    def advance(name, earlier, image, before, out_x, sent_y, last=False):
        received = (*swapped((out_x, out_x), "gx"), *swapped(sent_y, "yz")[::-1])
        values, inner_image, moments = call(
            inner_kernel, "inner", [grid] * 2 + [(16, LANES)], [],
            image, diagonal, jacobi, before, spread, mass,
        )
        out = (devices, 2, LANES) if last else (24, LANES)
        scratch = [pltpu.VMEM((192, LANES), jnp.float32)] * 2
        if last:
            scratch = scratch + [pltpu.VMEM(out, jnp.float32), pltpu.SemaphoreType.DMA]
        return call(
            outer_kernel, name, [grid] * 2 + [face] * 3 + [out], scratch,
            image, *received, diagonal, jacobi, before, *fixed, moments, earlier, values,
            inner_image,
            aliases={18: 0, 19: 1}, copied=int(last),
        )

    values1, image, out_x, *sent_y, moments1 = advance(
        "second", moments0, image, values0, out_x, sent_y
    )
    values2, image, out_x, *sent_y, sums = advance(
        "third", moments1, image, values1, out_x, sent_y, last=True
    )
    sums = lax.all_to_all(sums, ("gx", "yz"), 0, 0)
    received = (*swapped((out_x, out_x), "gx"), *swapped(sent_y, "yz")[::-1])
    result, precond = call(
        solution_kernel, "solution", [forcing.shape, (32, LANES)],
        [pltpu.VMEM(grid, jnp.float32)],
        values0, values1, values2, sums, chosen,
    )
    [residual] = call(
        last_kernel, "last", [forcing.shape], [pltpu.VMEM(grid, jnp.float32)],
        image, *received, diagonal, values0, values1, values2, precond, chosen,
    )
    return result, residual


def solution(mesh):
    placed = (
        P("gx", "yz", None, None),
        P("gx", "yz", None, None),
        P("gx", "yz", None, None),
        P("gx", "yz", None),
    )
    return jax.shard_map(
        body,
        mesh=mesh,
        in_specs=placed,
        out_specs=(P("gx", "yz", None, None), P("gx", "yz", None, None)),
        check_vma=False,
    )
```
